32 devices in a mesh: dp: 8 (over z, x), band: 4 (over y, core).
Axes of the slice: x: 2, y: 2, z: 4, core: 2. Of those that a mesh axis runs over, the one named last changes fastest.
Arguments:
- tokens: bfloat16 [96, 256, 768], P('dp', 'band'), may hold values from -6 to 6
- cotangent: bfloat16 [96, 256, 768], P('dp', 'band'), may hold values from -6 to 6
- image_rows: int32 [96], P('dp'), may hold values from 10 to 16, as said below
- qkv_weight: float32 [768, 2304], P('dp', 'band'), may hold values from -0.21875 to 0.21875
- out_weight: float32 [768, 768], P('dp', 'band'), may hold values from -1.75 to 1.75
- up_weight: float32 [768, 3072], P('dp', 'band'), may hold values from -0.21875 to 0.21875
- down_weight: float32 [3072, 768], P('dp', 'band'), may hold values from -0.109375 to 0.109375
- vectors: float32 [768, 14], P('dp'), may hold values from -1.5 to 1.5, as said below
- qkv_first: float32 [768, 2304], P('dp', 'band'), may hold values from -640 to 640
- out_first: float32 [768, 768], P('dp', 'band'), may hold values from -96 to 96
- up_first: float32 [768, 3072], P('dp', 'band'), may hold values from -224 to 224
- down_first: float32 [3072, 768], P('dp', 'band'), may hold values from -448 to 448
- vector_first: float32 [768, 14], P('dp'), may hold values from -896 to 896
- qkv_second: float32 [768, 2304], P('dp', 'band'), may hold values from 4014.08 to 64225.28
- out_second: float32 [768, 768], P('dp', 'band'), may hold values from 81.92 to 1310.72
- up_second: float32 [768, 3072], P('dp', 'band'), may hold values from 512 to 8192
- down_second: float32 [3072, 768], P('dp', 'band'), may hold values from 2048 to 32768
- vector_second: float32 [768, 14], P('dp'), may hold values from 8192 to 131072
Outputs:
- layer_out: bfloat16 [96, 256, 768], P('dp', 'band')
- token_grad: float32 [96, 256, 768], P('dp', 'band')
- qkv_new: float32 [768, 2304], P('dp', 'band')
- out_new: float32 [768, 768], P('dp', 'band')
- up_new: float32 [768, 3072], P('dp', 'band')
- down_new: float32 [3072, 768], P('dp', 'band')
- vector_new: float32 [768, 14], P('dp')
- qkv_first_new: float32 [768, 2304], P('dp', 'band')
- out_first_new: float32 [768, 768], P('dp', 'band')
- up_first_new: float32 [768, 3072], P('dp', 'band')
- down_first_new: float32 [3072, 768], P('dp', 'band')
- vector_first_new: float32 [768, 14], P('dp')
- qkv_second_new: float32 [768, 2304], P('dp', 'band')
- out_second_new: float32 [768, 768], P('dp', 'band')
- up_second_new: float32 [768, 3072], P('dp', 'band')
- down_second_new: float32 [3072, 768], P('dp', 'band')
- vector_second_new: float32 [768, 14], P('dp')
- down_bias_gradient: float32 [768], P('dp')
The draws below stay inside these ranges and needn't reach their ends.
Inputs may be any that keep to these rules, and one draw needn't show every extreme that they name: `image_rows`: each image has 10, 14 or 16 grid rows and as many grid columns; among the 12 images of each index of dp at least one has 16. `vectors`: columns 0, 5, 6 and 9 are gains and layer scales, the other columns biases.
All inputs are finite; a program needn't handle non-finite values.
Results may differ from the reference program's by a relative error of at most 0.018.
Values may be sent and summed in bfloat16 or wider, within the bound.
No kernel may reach another device: no remote copies, remote signals or barrier semaphores. Data moves between devices by JAX's collectives and lax.ppermute only.
A program may use at most 192 MiB of HBM per device.

```python
import math
from functools import partial
import jax
import jax.numpy as jnp
from jax import lax

D = 768
H = 12
HD = 64
FF = 3072
GRID = 16
VEC = 14
STEP = 7
IMG_DEV = 12
SLOTS = 256
IMAGES = 96


def draw_image_rows(key, part):
    key = jax.random.fold_in(key, 7)
    pick_key, full_key = jax.random.split(key)
    picked = jax.random.randint(pick_key, (IMAGES,), 0, 3)
    grid_rows = jnp.where(picked == 0, GRID * 5 // 8, jnp.where(picked == 1, GRID * 7 // 8, GRID))
    groups = IMAGES // IMG_DEV
    chosen = jax.random.randint(full_key, (groups,), 0, IMG_DEV)
    position = jnp.arange(IMAGES) % IMG_DEV
    group_of = jnp.arange(IMAGES) // IMG_DEV
    is_full = position == chosen[group_of]
    return jnp.where(is_full, GRID, grid_rows).astype(jnp.int32)


def draw_vectors(key, part):
    key = jax.random.fold_in(key, 11)
    spread_key, normal_key = jax.random.split(key)
    spread = jax.random.uniform(spread_key, (D, VEC), jnp.float32, -1.0, 1.0)
    normal = jax.random.normal(normal_key, (D, VEC), jnp.float32)
    column = jnp.arange(VEC)[None, :]
    is_gain = (column == 0) | (column == 5) | (column == 6) | (column == 9)
    return jnp.where(is_gain, 1.0 + 0.5 * spread, jnp.clip(0.3 * normal, -1.5, 1.5)).astype(jnp.float32)


def spiked(values, own_key, source, target, parts, factor):
    owner, partner = [(jnp.arange(values.shape[dim]) // (values.shape[dim] // parts)).reshape([-1 if axis == dim else 1 for axis in range(values.ndim)]) for dim in (source, target)]
    chosen = jax.random.permutation(own_key, parts)[partner]
    strong = (owner == chosen) | (owner == (partner + parts // 2) % parts)
    return jnp.where(strong, factor * values, values)


def steps_of(stream_key, dims, cuts, smallest, high):
    def one(axis_at, shards_of):
        draws = jax.random.uniform(jax.random.fold_in(jax.random.fold_in(stream_key, 6), axis_at), (shards_of,), jnp.float32, smallest / len(cuts), high / len(cuts))
        return jnp.repeat(jnp.exp(draws), dims[axis_at] // shards_of).reshape((-1,) + (1,) * (len(dims) - axis_at - 1))

    loudness = one(*cuts[0])
    for cut in cuts[1:]:
        loudness = loudness * one(*cut)
    return loudness


def normal_values(own_key, extent, scale, bound, shards=(), held_as=jnp.bfloat16):
    array = scale * jax.random.normal(own_key, extent, jnp.float32)
    if shards:
        array = array * steps_of(own_key, extent, shards, -0.22, 0.18)
    return jnp.clip(array, -bound, bound).astype(held_as)


def noise_with(rng, extent, width, reach, cuts, heavy, kind=jnp.bfloat16):
    values = width * jax.random.normal(rng, extent, jnp.float32)
    if cuts:
        values = values * steps_of(rng, extent, cuts, -0.22, 0.18)
    return jnp.clip(spiked(values, jax.random.fold_in(rng, 3), *heavy), -reach, reach).astype(kind)


def setup_inputs(seed: int = 0) -> dict:
    keys = jax.random.split(jax.random.key(seed), 19)
    return {
        "tokens": noise_with(keys[0], (IMAGES, SLOTS, D), 1.0, 6.0, ((0, 8), (1, 4)), (0, 2, 8, 2.0)),
        "cotangent": normal_values(keys[1], (IMAGES, SLOTS, D), 1.0, 6.0, ((0, 8), (1, 4))),
        "image_rows": draw_image_rows(jax.random.fold_in(keys[18], 71), 0),
        "qkv_weight": normal_values(keys[3], (D, 3 * D), D ** -0.5, 0.21875, ((0, 8), (1, 4)), jnp.float32),
        "out_weight": normal_values(keys[4], (D, D), (D // 64) ** -0.5, 1.75, ((0, 8), (1, 4)), jnp.float32),
        "up_weight": normal_values(keys[5], (D, FF), D ** -0.5, 0.21875, ((0, 8), (1, 4)), jnp.float32),
        "down_weight": normal_values(keys[6], (FF, D), FF ** -0.5, 0.109375, ((0, 8), (1, 4)), jnp.float32),
        "vectors": draw_vectors(jax.random.fold_in(keys[18], 71), 0),
        "qkv_first": normal_values(keys[8], (D, 3 * D), (0.7 * (IMAGES * SLOTS) ** 0.5), 640.0, ((0, 8), (1, 4)), jnp.float32),
        "out_first": normal_values(keys[9], (D, D), (0.1 * (IMAGES * SLOTS) ** 0.5), 96.0, ((0, 8), (1, 4)), jnp.float32),
        "up_first": normal_values(keys[10], (D, FF), (0.25 * (IMAGES * SLOTS) ** 0.5), 224.0, ((0, 8), (1, 4)), jnp.float32),
        "down_first": normal_values(keys[11], (FF, D), (0.5 * (IMAGES * SLOTS) ** 0.5), 448.0, ((0, 8), (1, 4)), jnp.float32),
        "vector_first": normal_values(keys[12], (D, VEC), ((IMAGES * SLOTS) ** 0.5), 896.0, ((0, 8),), jnp.float32),
        "qkv_second": jnp.clip(jnp.exp(math.log(64225.28) - 2.7725887 * jax.random.uniform(keys[13], (D, 3 * D), jnp.float32) ** steps_of(keys[13], (D, 3 * D), ((0, 8), (1, 4)), -0.2, 0.2)), 4014.08, 64225.28),
        "out_second": jnp.clip(jnp.exp(math.log(1310.72) - 2.7725887 * jax.random.uniform(keys[14], (D, D), jnp.float32) ** steps_of(keys[14], (D, D), ((0, 8), (1, 4)), -0.2, 0.2)), 81.92, 1310.72),
        "up_second": jnp.clip(jnp.exp(math.log(8192.0) - 2.7725887 * jax.random.uniform(keys[15], (D, FF), jnp.float32) ** steps_of(keys[15], (D, FF), ((0, 8), (1, 4)), -0.2, 0.2)), 512.0, 8192.0),
        "down_second": jnp.clip(jnp.exp(math.log(32768.0) - 2.7725887 * jax.random.uniform(keys[16], (FF, D), jnp.float32) ** steps_of(keys[16], (FF, D), ((0, 8), (1, 4)), -0.2, 0.2)), 2048.0, 32768.0),
        "vector_second": jnp.clip(jnp.exp(math.log(131072.0) - 2.7725887 * jax.random.uniform(keys[17], (D, VEC), jnp.float32) ** steps_of(keys[17], (D, VEC), ((0, 8),), -0.2, 0.2)), 8192.0, 131072.0),
    }


@jax.custom_vjp
def low(v):
    return lax.optimization_barrier(v.astype(jnp.bfloat16)).astype(jnp.float32)

@jax.custom_vjp
def low_back(v):
    return v

def low_keep(v):
    return (low(v), None)

def low_pass(kept, grad):
    return (grad,)

def back_keep(v):
    return (v, None)

def back_low(kept, grad):
    return (low(grad),)
low.defvjp(low_keep, low_pass)
low_back.defvjp(back_keep, back_low)
NORM_EPS = 1e-06
ADAM_EPS = 1e-08
BETA_ONE = 0.5
BETA_TWO = 0.6
MATRIX_DECAY = 0.05
VECTOR_RATE = 0.5
MASK_FILL = -1e+30
HIGHEST = lax.Precision.HIGHEST

def layer_norm(values, gain, shift):
    center = values - lax.optimization_barrier(jnp.mean(values, axis=-1, keepdims=True))
    spread = lax.optimization_barrier(jnp.mean(center * center, axis=-1, keepdims=True))
    return center * lax.rsqrt(spread + NORM_EPS) * gain + shift

def forward(valid_mask, inputs, qkv_weight, out_weight, up_weight, down_weight, vectors):
    gain_one = vectors[:, 0]
    shift_one = vectors[:, 1]
    query_bias = vectors[:, 2]
    value_bias = vectors[:, 3]
    out_bias = vectors[:, 4]
    scale_one = vectors[:, 5]
    gain_two = vectors[:, 6]
    shift_two = vectors[:, 7]
    down_bias = vectors[:, 8]
    scale_two = vectors[:, 9]
    up_bias = vectors[:, 10:14].T.reshape(-1)
    group_size = inputs.shape[0]
    normed = low(layer_norm(inputs, gain_one, shift_one))
    qkv_bias = jnp.concatenate([query_bias, jnp.zeros_like(query_bias), value_bias])
    project = jnp.einsum('gsd,de->gse', normed, qkv_weight, precision=HIGHEST) + qkv_bias
    project = low(low_back(project))
    parts_qkv = project.reshape(group_size, SLOTS, 3, H, HD)
    scores = jnp.einsum('gshe,gthe->ghst', parts_qkv[:, :, 0], parts_qkv[:, :, 1], precision=HIGHEST) * HD ** (-0.5)
    scores = low_back(scores)
    key_mask = valid_mask[:, None, None, :] > 0.5
    attn_prob = jax.nn.softmax(jnp.where(key_mask, scores, MASK_FILL), axis=-1)
    head_out = jnp.einsum('ghst,gthe->gshe', low(attn_prob), parts_qkv[:, :, 2], precision=HIGHEST)
    mixed_out = low(low_back(head_out.reshape(group_size, SLOTS, D)))
    branch = low_back(jnp.einsum('gsd,de->gse', mixed_out, out_weight, precision=HIGHEST) + out_bias)
    middle = inputs + scale_one * branch
    normed_two = low(layer_norm(middle, gain_two, shift_two))
    hidden = low_back(jnp.einsum('gsd,df->gsf', normed_two, up_weight, precision=HIGHEST) + up_bias)
    active = low(jax.nn.gelu(hidden, approximate=False))
    branch_two = low_back(jnp.einsum('gsf,fd->gsd', active, down_weight, precision=HIGHEST) + down_bias)
    return (middle + scale_two * branch_two) * valid_mask[:, :, None]

def adamw_update(master, gradient, moment_one, moment_two, step_rate, weight_decay):
    first_new = BETA_ONE * moment_one + (1.0 - BETA_ONE) * gradient
    second_new = BETA_TWO * moment_two + (1.0 - BETA_TWO) * gradient * gradient
    first_hat = first_new / (1.0 - BETA_ONE ** STEP)
    second_hat = second_new / (1.0 - BETA_TWO ** STEP)
    master_new = master - step_rate * (first_hat / (jnp.sqrt(second_hat) + ADAM_EPS) + weight_decay * master)
    return (master_new, first_new, second_new)

def rounded_copy(master):
    return master.astype(jnp.bfloat16).astype(jnp.float32)

def reference(tokens, cotangent, image_rows, qkv_weight, out_weight, up_weight, down_weight, vectors, qkv_first, out_first, up_first, down_first, vector_first, qkv_second, out_second, up_second, down_second, vector_second):
    slot_index = jnp.arange(SLOTS)
    row_limit = image_rows[:, None]
    valid_mask = (((slot_index // GRID)[None, :] < row_limit) & ((slot_index % GRID)[None, :] < row_limit)).astype(jnp.float32)
    working = (rounded_copy(qkv_weight), rounded_copy(out_weight), rounded_copy(up_weight), rounded_copy(down_weight), rounded_copy(vectors))
    groups = IMAGES // IMG_DEV
    token_groups = tokens.reshape(groups, IMG_DEV, SLOTS, D)
    cot_groups = cotangent.reshape(groups, IMG_DEV, SLOTS, D)
    mask_groups = valid_mask.reshape(groups, IMG_DEV, SLOTS)

    def group_step(totals, packed):
        token_block, cot_block, mask_block = packed
        result, pullback = jax.vjp(partial(forward, mask_block), token_block.astype(jnp.float32), working[0], working[1], working[2], working[3], working[4])
        gradients = pullback(cot_block.astype(jnp.float32))
        totals = jax.tree.map(jnp.add, totals, tuple(gradients[1:]))
        return (totals, (result.astype(jnp.bfloat16), gradients[0]))
    initial = jax.tree.map(jnp.zeros_like, working)
    totals, (outputs, token_grads) = lax.scan(group_step, initial, (token_groups, cot_groups, mask_groups))
    layer_out = outputs.reshape(IMAGES, SLOTS, D)
    token_grad = token_grads.reshape(IMAGES, SLOTS, D)
    down_bias_gradient = totals[4][:, 8]
    qkv_new = adamw_update(qkv_weight, totals[0], qkv_first, qkv_second, D ** (-0.5), MATRIX_DECAY)
    out_new = adamw_update(out_weight, totals[1], out_first, out_second, (D // 64) ** (-0.5), MATRIX_DECAY)
    up_new = adamw_update(up_weight, totals[2], up_first, up_second, D ** (-0.5), MATRIX_DECAY)
    down_new = adamw_update(down_weight, totals[3], down_first, down_second, FF ** (-0.5), MATRIX_DECAY)
    vector_new = adamw_update(vectors, totals[4], vector_first, vector_second, VECTOR_RATE, 0.0)
    return (layer_out, token_grad, qkv_new[0], out_new[0], up_new[0], down_new[0], vector_new[0], qkv_new[1], out_new[1], up_new[1], down_new[1], vector_new[1], qkv_new[2], out_new[2], up_new[2], down_new[2], vector_new[2], down_bias_gradient)
```

```python
import math
from functools import partial

import jax
import jax.numpy as jnp
from jax import lax
from jax.experimental import pallas as pl
from jax.experimental.pallas import tpu as pltpu
from jax.sharding import PartitionSpec as P

D = 768
H = 12
HD = 64
FF = 3072
GRID = 16
STEP = 7
SLOTS = 256
NORM_EPS = 1e-06
ADAM_EPS = 1e-08
BETA_ONE = 0.5
BETA_TWO = 0.6
MATRIX_DECAY = 0.05
VECTOR_RATE = 0.5
MASK_FILL = -1e30
R = 768
IMGS = 3
W1 = 640
W2 = 224
F32 = jnp.float32
BF16 = jnp.bfloat16
VMEM_LIMIT = 58 * 1024 * 1024


def adamw_update(master, gradient, moment_one, moment_two, step_rate, weight_decay):
    first_new = BETA_ONE * moment_one + (1.0 - BETA_ONE) * gradient
    second_new = BETA_TWO * moment_two + (1.0 - BETA_TWO) * gradient * gradient
    first_hat = first_new / (1.0 - BETA_ONE**STEP)
    second_hat = second_new / (1.0 - BETA_TWO**STEP)
    master_new = master - step_rate * (
        first_hat / (jnp.sqrt(second_hat) + ADAM_EPS) + weight_decay * master
    )
    return (master_new, first_new, second_new)


def dot(a, b):
    return lax.dot_general(a, b, (((1,), (0,)), ((), ())), preferred_element_type=F32)


def dot_nt(a, b):
    return lax.dot_general(a, b, (((1,), (1,)), ((), ())), preferred_element_type=F32)


def dot_tn(a, b):
    return lax.dot_general(a, b, (((0,), (0,)), ((), ())), preferred_element_type=F32)


def load_all(sources, target, sems):
    span = target.shape[0] // len(sources)
    copies = [
        pltpu.make_async_copy(ref, target.at[pl.ds(k * span, span)], sems.at[k])
        for k, ref in enumerate(sources)
    ]
    for copy in copies:
        copy.start()
    return copies


def norm_parts(values):
    center = values - jnp.mean(values, axis=-1, keepdims=True)
    spread = jnp.mean(center * center, axis=-1, keepdims=True)
    inverse = lax.rsqrt(spread + NORM_EPS)
    return center * inverse, inverse


def norm_back(gy, gain, xh, inverse):
    e = gy * gain
    return inverse * (
        e - jnp.mean(e, axis=-1, keepdims=True) - xh * jnp.mean(e * xh, axis=-1, keepdims=True)
    )


def head_cut(ref, img, j):
    lane = (j % 9) * HD
    base = lane // 128 * 128
    tile = ref[j // 9, :, img, :, base : base + 128].reshape(SLOTS, 128)
    return tile[:, lane - base : lane - base + HD]


def attend_kernel(count, maps, x_ref, bias_ref, *refs):
    sources, refs = refs[:count], refs[count:]
    qkv_ref, mixed_ref, total_ref, vec_ref, weights, n1_ref, sems = refs
    copies = load_all(sources, weights, sems)
    for copy in copies:
        copy.wait()

    def block(b, i):
        return maps[b] * 8 + maps[4 + i]

    tail = jnp.concatenate([weights[block(0, i), :, 512:640] for i in range(8)], axis=0)
    table = jnp.transpose(tail.astype(F32))
    vec_ref[...] = table[64:80]
    vec = table[64:80]
    for m in range(3):
        rows = x_ref[:, m].reshape(SLOTS, D).astype(F32)
        xh, _ = norm_parts(rows)
        n1_ref[m] = (xh * vec[0:1] + vec[1:2]).astype(BF16)
    bias = jnp.concatenate([vec[2:3], jnp.zeros((1, D), F32), vec[3:4], jnp.zeros((1, 64), F32)], axis=1)
    for b in range(4):
        w = jnp.concatenate([weights[block(b, i)] for i in range(8)], axis=0)
        for m in range(3):
            part = dot(n1_ref[m], w) + bias[:, 576 * b : 576 * b + 640]
            qkv_ref[b, :, m] = part.astype(BF16).reshape(4, 64, W1)

    def image(img, carry):
        column = bias_ref[img]
        for pair in range(H // 2):
            outs = []
            for h in (2 * pair, 2 * pair + 1):
                q = head_cut(qkv_ref, img, h) * BF16(HD**-0.5)
                k = head_cut(qkv_ref, img, H + h)
                v = head_cut(qkv_ref, img, 2 * H + h)
                scores = dot_nt(k, q) + column
                highest = jnp.max(scores, axis=0, keepdims=True)
                shifted = jnp.exp(scores - highest)
                totals = jnp.sum(shifted, axis=0, keepdims=True)
                low = (shifted * (1.0 / totals)).astype(BF16)
                total_ref[img, pl.ds(h, 1), :] = highest + jnp.log(totals)
                outs.append(dot_tn(v, low))
            both = jnp.transpose(jnp.concatenate(outs, axis=0))
            mixed_ref[:, img, :, 128 * pair : 128 * pair + 128] = both.astype(BF16).reshape(4, 64, 128)
        return carry

    lax.fori_loop(0, IMGS, image, 0)


def gelu_parts(v):
    cdf = 0.5 * (1.0 + lax.erf(v * (0.5**0.5)))
    pdf = jnp.exp(v * v * -0.5) * ((2.0 * math.pi) ** -0.5)
    return v * cdf, cdf + v * pdf


def feed_kernel(count, maps, x_ref, cot_ref, mixed_ref, valid_ref, vec_ref, *refs):
    sources, refs = refs[:count], refs[count:]
    (layer_ref, middle_grad_ref, mixed_grad_ref, vec_grad_ref, keep_ref, send_ref,
     weights, grads, up, down, out, branch_ref, mid_ref, xh_ref, inv_ref, n2_ref, gb_ref, n2t_ref, gbt_ref,
     act_ref, gh_ref, br2_ref, gn2_ref, sems, out_sems) = refs
    copies = load_all(sources, weights, sems)
    for copy in copies:
        copy.wait()

    def block(b, i):
        return maps[b] * 8 + maps[4 + i]

    vec = vec_ref[...]
    for b in range(4):
        for i in range(8):
            piece = weights[block(b, i), 192:224, 0:576]
            for g in range(3):
                out[96 * i + 32 * g : 96 * i + 32 * g + 32, 192 * b : 192 * b + 192] = piece[:, 192 * g : 192 * g + 192]
    for m in range(3):
        rows = pl.ds(m * SLOTS, SLOTS)
        x = x_ref[:, m].reshape(SLOTS, D).astype(F32)
        mixed = mixed_ref[:, m].reshape(SLOTS, D)
        branch = dot(mixed, out[...]) + vec[4:5]
        branch_ref[rows] = branch
        middle = x + vec[5:6] * branch
        mid_ref[rows] = middle
        xh, inverse = norm_parts(middle)
        xh_ref[rows] = xh
        inv_ref[rows] = inverse
        n2_ref[rows] = (xh * vec[6:7] + vec[7:8]).astype(BF16)
        back = cot_ref[:, m].reshape(SLOTS, D).astype(F32) * valid_ref[m]
        gb_ref[rows] = (back * vec[9:10]).astype(BF16)
    n2t_ref[...] = jnp.transpose(n2_ref[...])
    gbt_ref[...] = jnp.transpose(gb_ref[...])
    br2_ref[...] = jnp.zeros((R, D), F32)
    gn2_ref[...] = jnp.zeros((R, D), F32)

    def tile(t, carry):
        for i in range(8):
            up[96 * i : 96 * i + 96] = weights[block(t, i), 0:96]
        for b in range(4):
            for half in range(2):
                piece = weights[block(b, 2 * t + half), 96:192]
                for e in range(2):
                    down[192 * b + 96 * e : 192 * b + 96 * e + 96, 384 * half : 384 * half + 384] = piece[
                        :, 384 * e : 384 * e + 384
                    ]
        up_bias = vec_ref[pl.ds(10 + t, 1), :]
        bias_sum = jnp.zeros((1, D), F32)
        for m in range(3):
            rows = slice(m * SLOTS, m * SLOTS + SLOTS)
            hidden = dot(n2_ref[rows], up[...]) + up_bias
            active, slope = gelu_parts(hidden)
            act_ref[rows] = active.astype(BF16)
            gh = dot(gb_ref[rows], down[...]) * slope
            low = gh.astype(BF16)
            gh_ref[rows] = low
            bias_sum += jnp.sum(low.astype(F32), axis=0, keepdims=True)
            br2_ref[rows] += dot_nt(act_ref[rows], down[...])
            gn2_ref[rows] += dot_nt(gh_ref[rows], up[...])
        vec_grad_ref[pl.ds(10 + t, 1), :] = bias_sum
        up_grad = dot(n2t_ref[...], gh_ref[...]).astype(BF16)
        for i in range(8):
            grads[block(t, i), 0:96] = up_grad[96 * i : 96 * i + 96]
        down_grad = dot(gbt_ref[...], act_ref[...]).astype(BF16)
        for b in range(4):
            for half in range(2):
                for e in range(2):
                    grads[block(b, 2 * t + half), 96:192, 384 * e : 384 * e + 384] = down_grad[
                        192 * b + 96 * e : 192 * b + 96 * e + 96, 384 * half : 384 * half + 384
                    ]
        return carry

    lax.fori_loop(0, 4, tile, 0)
    sums = [jnp.zeros((1, D), F32) for _ in range(10)]
    for m in range(3):
        rows = pl.ds(m * SLOTS, SLOTS)
        valid = valid_ref[m]
        back = cot_ref[:, m].reshape(SLOTS, D).astype(F32) * valid
        branch_two = br2_ref[rows] + vec[8:9]
        layer = (mid_ref[rows] + vec[9:10] * branch_two) * valid
        layer_ref[:, m] = layer.astype(BF16).reshape(4, 64, D)
        sums[9] += jnp.sum(back * branch_two, axis=0, keepdims=True)
        sums[8] += jnp.sum(gb_ref[rows].astype(F32), axis=0, keepdims=True)
        gy = gn2_ref[rows]
        xh = xh_ref[rows]
        sums[6] += jnp.sum(gy * xh, axis=0, keepdims=True)
        sums[7] += jnp.sum(gy, axis=0, keepdims=True)
        grad = norm_back(gy, vec[6:7], xh, inv_ref[rows]) + back
        middle_grad_ref[:, m] = grad.reshape(4, 64, D)
        sums[5] += jnp.sum(grad * branch_ref[rows], axis=0, keepdims=True)
        low = (grad * vec[5:6]).astype(BF16)
        sums[4] += jnp.sum(low.astype(F32), axis=0, keepdims=True)
        gh_ref[rows] = low
        mixed_grad_ref[:, m] = dot_nt(low, out[...]).astype(BF16).reshape(4, 64, D)
        act_ref[rows] = mixed_ref[:, m].reshape(SLOTS, D)
    vec_grad_ref[14:16] = jnp.zeros((2, D), F32)
    for k in range(10):
        vec_grad_ref[k : k + 1] = sums[k]
    out_grad = dot_tn(act_ref[...], gh_ref[...]).astype(BF16)
    for b in range(4):
        for i in range(8):
            pieces = [out_grad[96 * i + 32 * g : 96 * i + 32 * g + 32, 192 * b : 192 * b + 192] for g in range(3)]
            grads[block(b, i), 192:224] = jnp.concatenate(pieces + [jnp.zeros((32, 192), BF16)], axis=1)
    half = grads.shape[0] // 2
    puts = [
        pltpu.make_async_copy(grads.at[pl.ds(k * half, half)], ref, out_sems.at[k])
        for k, ref in enumerate((keep_ref, send_ref))
    ]
    for put in puts:
        put.start()
    for put in puts:
        put.wait()


def back_kernel(count, maps, x_ref, bias_ref, qkv_ref, total_ref, mixed_grad_ref, middle_grad_ref, vec_ref, vec_in_ref, *refs):
    sources, refs = refs[:count], refs[count:]
    token_grad_ref, keep_ref, send_ref, weights, grads, gq_ref, xh_ref, inv_ref, n1t_ref, sems, out_sems = refs
    copies = load_all(sources, weights, sems)

    def block(b, i):
        return maps[b] * 8 + maps[4 + i]

    def image(img, carry):
        column = bias_ref[img]
        parts = [None] * 36
        for h in range(H):
            q = head_cut(qkv_ref, img, h) * BF16(HD**-0.5)
            k = head_cut(qkv_ref, img, H + h)
            v = head_cut(qkv_ref, img, 2 * H + h)
            base = h // 2 * 128
            tile = mixed_grad_ref[:, img, :, base : base + 128].reshape(SLOTS, 128)
            grad_out = tile[:, h % 2 * HD : h % 2 * HD + HD]
            scores = dot_nt(k, q) + column
            again = jnp.exp(scores - total_ref[img, pl.ds(h, 1), :])
            grad_weights = dot_nt(v, grad_out)
            center = jnp.sum(again * grad_weights, axis=0, keepdims=True)
            grad_scores = (again * (grad_weights - center)).astype(BF16)
            parts[2 * H + h] = dot(again.astype(BF16), grad_out)
            parts[H + h] = dot(grad_scores, q)
            parts[h] = jnp.transpose(dot_tn(k, grad_scores)) * (HD**-0.5)
            for j in (h, H + h, 2 * H + h):
                lane = (j % 9) * HD
                gq_ref[j // 9, :, img, :, lane : lane + HD] = parts[j].astype(BF16).reshape(4, 64, HD)
        return carry

    gq_ref[:, :, :, :, 512:640] = jnp.zeros((4, 4, IMGS, 64, 128), BF16)
    lax.fori_loop(0, IMGS, image, 0)
    vec = vec_ref[...]
    for m in range(3):
        rows = pl.ds(m * SLOTS, SLOTS)
        xh, inverse = norm_parts(x_ref[:, m].reshape(SLOTS, D).astype(F32))
        xh_ref[rows] = xh
        inv_ref[rows] = inverse
        n1t_ref[:, m * SLOTS : m * SLOTS + SLOTS] = jnp.transpose((xh * vec[0:1] + vec[1:2]).astype(BF16))
    for copy in copies:
        copy.wait()
    gain_sum, shift_sum = jnp.zeros((1, D), F32), jnp.zeros((1, D), F32)
    for m in range(3):
        rows = pl.ds(m * SLOTS, SLOTS)
        gy = jnp.zeros((SLOTS, D), F32)
        for b in range(4):
            w = jnp.concatenate([weights[block(b, i)] for i in range(8)], axis=0)
            gy += dot_nt(gq_ref[b, :, m].reshape(SLOTS, W1), w)
        xh = xh_ref[rows]
        gain_sum += jnp.sum(gy * xh, axis=0, keepdims=True)
        shift_sum += jnp.sum(gy, axis=0, keepdims=True)
        grad = norm_back(gy, vec[0:1], xh, inv_ref[rows]) + middle_grad_ref[:, m].reshape(SLOTS, D)
        token_grad_ref[:, m] = grad.astype(BF16).reshape(4, 64, D)
    col = []
    for b in range(4):
        total = jnp.zeros((1, W1), F32)
        for m in range(3):
            total += jnp.sum(gq_ref[b, :, m].reshape(SLOTS, W1).astype(F32), axis=0, keepdims=True)
        col.append(total[:, :576])
    flat = jnp.concatenate(col, axis=1)
    vec_in = vec_in_ref[...]
    table = jnp.concatenate(
        [jnp.zeros((64, D), F32), gain_sum, shift_sum, flat[:, :D], flat[:, 2 * D :], vec_in[4:16], jnp.zeros((48, D), F32)], axis=0
    )
    tail = jnp.transpose(table)
    for b in range(4):
        grad_rows = jnp.concatenate([gq_ref[b, :, m].reshape(SLOTS, W1) for m in range(3)], axis=0)
        grad = dot(n1t_ref[...], grad_rows)
        last = (grad[:, 512:640] + tail).astype(BF16)
        grad = grad.astype(BF16)
        for i in range(8):
            grads[block(b, i), :, 0:512] = grad[96 * i : 96 * i + 96, 0:512]
            grads[block(b, i), :, 512:640] = last[96 * i : 96 * i + 96]
    half = grads.shape[0] // 2
    puts = [
        pltpu.make_async_copy(grads.at[pl.ds(k * half, half)], ref, out_sems.at[k])
        for k, ref in enumerate((keep_ref, send_ref))
    ]
    for put in puts:
        put.start()
    for put in puts:
        put.wait()


def swap_band(values, k):
    return lax.ppermute(values, "band", [(b, b ^ k) for b in range(lax.axis_size("band"))])


def swap_dp(values, k):
    return lax.ppermute(values, "dp", [(d, d ^ k) for d in range(lax.axis_size("dp"))])


def spread_images(values, mine):
    groups = values.reshape(4, IMGS, 64, D)
    parts = [lax.dynamic_index_in_dim(groups, mine ^ k, 0, keepdims=False) for k in range(4)]
    return jnp.stack([parts[0]] + [swap_band(parts[k], k) for k in (1, 2, 3)])


def collect_images(values, mine):
    parts = jnp.stack([values[0]] + [swap_band(values[k], k) for k in (1, 2, 3)])
    return jnp.concatenate(
        [lax.dynamic_index_in_dim(parts, mine ^ g, 0, keepdims=True) for g in range(4)]
    ).reshape(12, 64, D)


def pack_first(qkv, vectors):
    return jnp.concatenate([qkv, vectors, jnp.zeros((qkv.shape[0], W1 - 590), BF16)], axis=1)


def pack_second(up, down, out):
    turned = down.T
    lower = jnp.concatenate([turned[:96], turned[96:]], axis=1)
    spare = jnp.zeros((32, 192), BF16)
    last = jnp.concatenate([out[:32], out[32:64], out[64:96], spare], axis=1)
    return jnp.concatenate([up, lower, last], axis=0)


def unpack_second(block):
    turned = jnp.concatenate([block[96:192, :384], block[96:192, 384:]], axis=0)
    out = jnp.concatenate([block[192:, 192 * g : 192 * g + 192] for g in range(3)], axis=0)
    return block[:96], turned.T, out


def gather_blocks(shard):
    near = jnp.stack([shard] + [swap_dp(shard, 2 * k) for k in (1, 2, 3)])
    across = swap_dp(near, 1)
    beside = swap_band(near, 2)
    corner = jnp.concatenate([swap_band(across[:2], 2), swap_dp(beside[2:], 1)])
    parts = [near, across, beside, corner]
    return parts + [swap_band(part, 1) for part in parts]


def gather_blocks_full(blocks):
    parts = [blocks, swap_band(blocks, 2)]
    return parts + [swap_band(part, 1) for part in parts]


def add(*terms):
    return sum(term.astype(F32) for term in terms).astype(BF16)


def reduce_blocks(keep, send):
    shape = keep.shape[1:]
    keep = keep.reshape(2, 2, 4, *shape)
    other = swap_band(send, 1).reshape(2, 2, 4, *shape)
    from_across = swap_dp(add(keep[1, 1, :2], other[1, 1, :2]), 1)
    from_beside = swap_band(add(keep[1, 1, 2:], other[1, 1, 2:]), 2)
    beside = jnp.concatenate(
        [add(keep[1, 0, :2], other[1, 0, :2], from_across), add(keep[1, 0, 2:], other[1, 0, 2:])]
    )
    across = jnp.concatenate(
        [add(keep[0, 1, :2], other[0, 1, :2]), add(keep[0, 1, 2:], other[0, 1, 2:], from_beside)]
    )
    got_across = swap_dp(across, 1)
    got_beside = swap_band(beside, 2)
    near = [add(keep[0, 0, k], other[0, 0, k], got_across[k], got_beside[k]) for k in range(4)]
    parts = [near[0]] + [swap_dp(near[k], 2 * k) for k in (1, 2, 3)]
    return sum(part.astype(F32) for part in parts)


def reduce_blocks_full(keep, send):
    shape = keep.shape[1:]
    keep = keep.reshape(2, 8, *shape)
    other = swap_band(send, 1).reshape(2, 8, *shape)
    got = swap_band(add(keep[1], other[1]), 2)
    return add(keep[0], other[0], got)


def kernel_call(body, sources, smem, operands, out_shapes, out_spaces, scratch, flops):
    specs = [pl.BlockSpec(memory_space=pltpu.SMEM)]
    specs += [pl.BlockSpec(memory_space=pltpu.VMEM) for _ in operands]
    specs += [pl.BlockSpec(memory_space=pl.ANY) for _ in sources]
    moved = sum(v.size * v.dtype.itemsize for v in (*operands, *sources, *out_shapes))
    return pl.pallas_call(
        partial(body, len(sources)),
        out_shape=out_shapes,
        in_specs=specs,
        out_specs=tuple(pl.BlockSpec(memory_space=space) for space in out_spaces),
        scratch_shapes=scratch,
        compiler_params=pltpu.CompilerParams(vmem_limit_bytes=VMEM_LIMIT),
        cost_estimate=pl.CostEstimate(flops=flops, bytes_accessed=moved, transcendentals=0),
    )(smem, *operands, *sources)


def on_device(
    tokens, cotangent, image_rows, qkv_weight, out_weight, up_weight, down_weight, vectors,
    qkv_first, out_first, up_first, down_first, vector_first,
    qkv_second, out_second, up_second, down_second, vector_second,
):
    dp_count = lax.axis_size("dp")
    dp_mine = lax.axis_index("dp")
    mine = lax.axis_index("band")
    direct = dp_count == 8
    low = [w.astype(BF16) for w in (qkv_weight, out_weight, up_weight, down_weight, vectors)]
    if direct:
        first = gather_blocks(pack_first(low[0], low[4]))
        second = gather_blocks(pack_second(low[2], low[3], low[1]))
        flip = jnp.arange(8, dtype=jnp.int32) ^ dp_mine
        place = flip % 2 * 4 + flip // 2
    else:
        qkv_all, out_all, up_all, down_all, vec_all = [
            lax.all_gather(w, "dp", axis=0, tiled=True) for w in low
        ]
        first = jnp.stack(
            [pack_first(qkv_all[96 * i : 96 * i + 96], vec_all[96 * i : 96 * i + 96]) for i in range(8)]
        )
        second = jnp.stack(
            [
                pack_second(
                    up_all[96 * i : 96 * i + 96],
                    down_all[384 * i : 384 * i + 384],
                    out_all[96 * i : 96 * i + 96],
                )
                for i in range(8)
            ]
        )
        first = gather_blocks_full(first)
        second = gather_blocks_full(second)
        place = jnp.arange(8, dtype=jnp.int32)
    flip = jnp.arange(4, dtype=jnp.int32) ^ mine
    maps = jnp.concatenate([flip % 2 * 2 + flip // 2, place]).astype(jnp.int32)

    slots = (flip[:, None] * 64 + jnp.arange(64)[None, :]).reshape(SLOTS)
    limits = lax.dynamic_slice_in_dim(image_rows, mine * IMGS, IMGS)[:, None]
    inside = (slots // GRID < limits) & (slots % GRID < limits)
    valid = inside.astype(F32)[:, :, None]
    key_bias = jnp.where(inside, 0.0, MASK_FILL).astype(F32)[:, :, None]
    x = spread_images(tokens, mine)
    cot = spread_images(cotangent, mine)

    rows_shape = (4, IMGS, 64, D)
    sds = jax.ShapeDtypeStruct
    any_, vmem = pl.ANY, pltpu.VMEM
    qkv, mixed, totals, vec = kernel_call(
        attend_kernel, first, maps, (x, key_bias),
        (sds((4, 4, IMGS, 64, W1), BF16), sds(rows_shape, BF16), sds((IMGS, H, SLOTS), F32), sds((16, D), F32)),
        (vmem,) * 4,
        [vmem((32, 96, W1), BF16), vmem((IMGS, SLOTS, D), BF16), pltpu.SemaphoreType.DMA((8,))],
        4_000_000_000,
    )
    wide = lambda dtype: vmem((R, D), dtype)
    layer, middle_grad, mixed_grad, vec_grad, keep2, send2 = kernel_call(
        feed_kernel, second, maps, (x, cot, mixed, valid, vec),
        (sds(rows_shape, BF16), sds(rows_shape, F32), sds(rows_shape, BF16), sds((16, D), F32),
         sds((16, W2, D), BF16), sds((16, W2, D), BF16)),
        (vmem, vmem, vmem, vmem, any_, any_),
        [vmem((32, W2, D), BF16), vmem((32, W2, D), BF16), wide(BF16), wide(BF16), wide(BF16),
         wide(F32), wide(F32), wide(F32), vmem((R, 1), F32), wide(BF16), wide(BF16), wide(BF16), wide(BF16),
         wide(BF16), wide(BF16), wide(F32), wide(F32),
         pltpu.SemaphoreType.DMA((8,)), pltpu.SemaphoreType.DMA((2,))],
        24_000_000_000,
    )
    token_grad, keep1, send1 = kernel_call(
        back_kernel, first, maps, (x, key_bias, qkv, totals, mixed_grad, middle_grad, vec, vec_grad),
        (sds(rows_shape, BF16), sds((16, 96, W1), BF16), sds((16, 96, W1), BF16)),
        (vmem, any_, any_),
        [vmem((32, 96, W1), BF16), vmem((32, 96, W1), BF16), vmem((4, 4, IMGS, 64, W1), BF16),
         wide(F32), vmem((R, 1), F32), wide(BF16),
         pltpu.SemaphoreType.DMA((8,)), pltpu.SemaphoreType.DMA((2,))],
        8_000_000_000,
    )
    if direct:
        grad2 = reduce_blocks(keep2, send2)
        grad1 = reduce_blocks(keep1, send1)
        up_grad, down_grad, out_grad = unpack_second(grad2)
        qkv_grad, vector_grad = grad1[:, :576], grad1[:, 576:590]
    else:
        grad2 = reduce_blocks_full(keep2, send2)
        grad1 = reduce_blocks_full(keep1, send1)
        parts = [unpack_second(grad2[i]) for i in range(8)]
        up_grad, down_grad, out_grad = [jnp.concatenate(p) for p in zip(*parts)]
        flat = grad1.reshape(D, W1)
        up_grad, down_grad, out_grad, qkv_grad, vector_grad = [
            lax.psum_scatter(g.astype(F32), "dp", scatter_dimension=0, tiled=True)
            for g in (up_grad, down_grad, out_grad, flat[:, :576], flat[:, 576:590])
        ]
    layer_out = collect_images(layer, mine)
    token_out = collect_images(token_grad, mine).astype(F32)
    down_bias_gradient = vector_grad[:, 8]
    qkv_new = adamw_update(qkv_weight, qkv_grad, qkv_first, qkv_second, D ** (-0.5), MATRIX_DECAY)
    out_new = adamw_update(out_weight, out_grad, out_first, out_second, (D // 64) ** (-0.5), MATRIX_DECAY)
    up_new = adamw_update(up_weight, up_grad, up_first, up_second, D ** (-0.5), MATRIX_DECAY)
    down_new = adamw_update(down_weight, down_grad, down_first, down_second, FF ** (-0.5), MATRIX_DECAY)
    vector_new = adamw_update(vectors, vector_grad, vector_first, vector_second, VECTOR_RATE, 0.0)
    news = (qkv_new, out_new, up_new, down_new, vector_new)
    return (
        (layer_out, token_out)
        + tuple(n[0] for n in news)
        + tuple(n[1] for n in news)
        + tuple(n[2] for n in news)
        + (down_bias_gradient,)
    )


def solution(mesh):
    rows, matrix, table = P("dp", "band", None), P("dp", "band"), P("dp", None)
    state = (matrix, matrix, matrix, matrix, table)
    return jax.shard_map(
        on_device,
        mesh=mesh,
        in_specs=(rows, rows, P("dp")) + state + state + state,
        out_specs=(rows, rows) + state + state + state + (P("dp"),),
        check_vma=False,
    )
```

```python
import math
from functools import partial

import jax
import jax.numpy as jnp
from jax import lax
from jax.experimental import pallas as pl
from jax.experimental.pallas import tpu as pltpu
from jax.sharding import PartitionSpec as P

D = 768
H = 12
HD = 64
FF = 3072
GRID = 16
STEP = 7
SLOTS = 256
NORM_EPS = 1e-06
ADAM_EPS = 1e-08
BETA_ONE = 0.5
BETA_TWO = 0.6
MATRIX_DECAY = 0.05
VECTOR_RATE = 0.5
MASK_FILL = -1e30
R = 768
IMGS = 3
W1 = 640
GROUPS = 3
TILE = FF // GROUPS
FLIP, LIMIT = 12, 16
F32 = jnp.float32
BF16 = jnp.bfloat16
MIB = 1024 * 1024


def adamw_update(master, gradient, moment_one, moment_two, step_rate, weight_decay):
    first_new = BETA_ONE * moment_one + (1.0 - BETA_ONE) * gradient
    second_new = BETA_TWO * moment_two + (1.0 - BETA_TWO) * gradient * gradient
    first_hat = first_new / (1.0 - BETA_ONE**STEP)
    second_hat = second_new / (1.0 - BETA_TWO**STEP)
    master_new = master - step_rate * (
        first_hat / (jnp.sqrt(second_hat) + ADAM_EPS) + weight_decay * master
    )
    return (master_new, first_new, second_new)


def dot(a, b):
    return lax.dot_general(a, b, (((1,), (0,)), ((), ())), preferred_element_type=F32)


def dot_nt(a, b):
    return lax.dot_general(a, b, (((1,), (1,)), ((), ())), preferred_element_type=F32)


def dot_tn(a, b):
    return lax.dot_general(a, b, (((0,), (0,)), ((), ())), preferred_element_type=F32)


def sds(shape, dtype):
    return jax.ShapeDtypeStruct(shape, dtype)


def as_list(value):
    return list(value) if isinstance(value, (list, tuple)) else [value]


class Staging:
    def __init__(self, ins, in_sems, outs, out_sems):
        self.waits = [[pltpu.make_async_copy(s, t, in_sems.at[n]) for s, t, n in group] for group in ins]
        self.puts = [[pltpu.make_async_copy(s, t, out_sems.at[n]) for s, t, n in group] for group in outs]
        self.waited, self.started = set(), set()
        for group in self.waits:
            for copy in group:
                copy.start()

    def need(self, *which):
        for k in which:
            if k not in self.waited:
                self.waited.add(k)
                for copy in self.waits[k]:
                    copy.wait()

    def put(self, *which):
        for k in which:
            if k not in self.started:
                self.started.add(k)
                for copy in self.puts[k]:
                    copy.start()

    def finish(self):
        self.need(*range(len(self.waits)))
        self.put(*range(len(self.puts)))
        for group in self.puts:
            for copy in group:
                copy.wait()


def staged_call(body, smem, operands, outs, scratch, flops, far=()):
    operands = [as_list(v) for v in operands]
    outs = [as_list(v) for v in outs]
    flat_in = [v for group in operands for v in group]
    flat_out = [v for group in outs for v in group]

    def buffer(group):
        return pltpu.VMEM((sum(v.shape[0] for v in group), *group[0].shape[1:]), group[0].dtype)

    def kernel(*refs):
        refs = list(refs)
        take = lambda n: [refs.pop(0) for _ in range(n)]
        info, sources, raw, targets = take(len(smem)), take(len(flat_in)), take(len(far)), take(len(flat_out))
        in_refs, out_refs, extra = take(len(operands)), take(len(outs)), take(len(scratch))
        in_sems, out_sems = refs

        def pairs(groups, far, near, outward):
            result, n = [], 0
            for group, ref in zip(groups, near):
                row, entry = 0, []
                for v in group:
                    part = ref if len(group) == 1 else ref.at[pl.ds(row, v.shape[0])]
                    entry.append((part, far[n], n) if outward else (far[n], part, n))
                    row, n = row + v.shape[0], n + 1
                result.append(entry)
            return result

        staging = Staging(
            pairs(operands, sources, in_refs, False), in_sems, pairs(outs, targets, out_refs, True), out_sems
        )
        body(staging, *info, *raw, in_refs, out_refs, *extra)
        staging.finish()

    moved = sum(v.size * v.dtype.itemsize for v in (*flat_in, *far, *flat_out))
    return pl.pallas_call(
        kernel,
        out_shape=tuple(flat_out),
        in_specs=[pl.BlockSpec(memory_space=pltpu.SMEM) for _ in smem]
        + [pl.BlockSpec(memory_space=pl.ANY) for _ in (*flat_in, *far)],
        out_specs=tuple(pl.BlockSpec(memory_space=pl.ANY) for _ in flat_out),
        scratch_shapes=[buffer(g) for g in operands]
        + [buffer(g) for g in outs]
        + list(scratch)
        + [pltpu.SemaphoreType.DMA((len(flat_in),)), pltpu.SemaphoreType.DMA((len(flat_out),))],
        compiler_params=pltpu.CompilerParams(vmem_limit_bytes=58 * MIB),
        cost_estimate=pl.CostEstimate(flops=flops, bytes_accessed=moved, transcendentals=0),
    )(*smem, *flat_in, *far)


def norm_parts(values):
    center = values - jnp.mean(values, axis=-1, keepdims=True)
    spread = jnp.mean(center * center, axis=-1, keepdims=True)
    inverse = lax.rsqrt(spread + NORM_EPS)
    return center * inverse, inverse


def norm_back(gy, gain, xh, inverse):
    e = gy * gain
    return inverse * (
        e - jnp.mean(e, axis=-1, keepdims=True) - xh * jnp.mean(e * xh, axis=-1, keepdims=True)
    )


def column_sum(values):
    return jnp.sum(values, axis=0, keepdims=True)


def image_values(ref, m):
    return jnp.concatenate([ref[IMGS * k + m] for k in range(4)], axis=0)


def set_image(ref, m, values):
    for k in range(4):
        ref[IMGS * k + m] = values[64 * k : 64 * k + 64]


def valid_slots(info, m):
    columns = []
    for k in range(4):
        slot = lax.broadcasted_iota(jnp.int32, (64, 1), 0) + info[FLIP + k] * 64
        inside = ((slot >> 4) < info[LIMIT + m]) & ((slot & 15) < info[LIMIT + m])
        columns.append(inside.astype(F32))
    return jnp.concatenate(columns, axis=0)


def blocks_of(info):
    return lambda b, i: info[b] * 8 + info[4 + i]


def joined(weights, block, b):
    return jnp.concatenate([weights[block(b, i)] for i in range(8)], axis=0)


def head_cut(ref, j):
    lane = (j % 9) * HD
    base = lane // 128 * 128
    tile = ref[j // 9, :, 0, :, base : base + 128].reshape(SLOTS, 128)
    return tile[:, lane - base : lane - base + HD]


def pack_first_body(io, ins, outs):
    io.need(0, 1)
    qkv, table = ins[0][...], ins[1][...]
    table = jnp.concatenate([table, jnp.zeros((50, table.shape[1]), F32)], axis=0)
    outs[0][:, 0:512] = qkv[:, 0:512].astype(BF16)
    outs[0][:, 512:640] = jnp.concatenate([qkv[:, 512:576], jnp.transpose(table)], axis=1).astype(BF16)


def pack_second_body(io, ins, outs):
    io.need(0, 1, 2)
    up, turned, out = (ref[...].astype(BF16) for ref in ins)
    for group in range(GROUPS):
        at, row = 128 * group, 96 * group
        pieces = (up[:, at : at + 128], up[:, at + 384 : at + 512], turned[:96, at : at + 128], turned[96:, at : at + 128])
        for n, piece in enumerate(pieces):
            outs[0][row : row + 96, 128 * n : 128 * n + 128] = piece
    outs[0][288:336, :] = pack_out(out)


def project_body(io, info, ins, outs, n1):
    x, weights = ins
    qkv, table = outs
    block = blocks_of(info)
    io.need(0)
    for m in range(IMGS):
        n1[m], _ = norm_parts(image_values(x, m).astype(F32))
    io.need(1)
    tail = jnp.concatenate([weights[block(0, i), :, 512:640] for i in range(8)], axis=0)
    vec = jnp.transpose(tail.astype(F32))[64:80]
    table[...] = vec
    bias = jnp.concatenate(
        [vec[2:3], jnp.zeros((1, D), F32), vec[3:4], jnp.zeros((1, 64), F32)], axis=1
    )
    normed = [(n1[m] * vec[0:1] + vec[1:2]).astype(BF16) for m in range(IMGS)]
    for b in range(4):
        w = joined(weights, block, b)
        for m in range(IMGS):
            part = dot(normed[m], w) + bias[:, 576 * b : 576 * b + W1]
            qkv[b, :, m] = part.astype(BF16).reshape(4, 64, W1)


def attend_kernel(info, qkv, mixed, total):
    column = (valid_slots(info, pl.program_id(0)) - 1.0) * -MASK_FILL
    for pair in range(H // 2):
        halves = []
        for h in (2 * pair, 2 * pair + 1):
            q = head_cut(qkv, h) * BF16(HD**-0.5)
            k = head_cut(qkv, H + h)
            v = head_cut(qkv, 2 * H + h)
            scores = dot_nt(k, q) + column
            highest = jnp.max(scores, axis=0, keepdims=True)
            shifted = jnp.exp(scores - highest)
            totals = column_sum(shifted)
            low = (shifted * (1.0 / totals)).astype(BF16)
            total[0, h : h + 1, :] = highest + jnp.log(totals)
            halves.append(dot_tn(v, low))
        both = jnp.transpose(jnp.concatenate(halves, axis=0))
        mixed[:, 0, :, 128 * pair : 128 * pair + 128] = both.astype(BF16).reshape(4, 64, 128)


def gelu_parts(v):
    cdf = 0.5 * (1.0 + lax.erf(v * (0.5**0.5)))
    pdf = jnp.exp(v * v * -0.5) * ((2.0 * math.pi) ** -0.5)
    return v * cdf, cdf + v * pdf


def spread_group(weights, up, down):
    for b in range(4):
        for i in range(8):
            piece = weights[b * 8 + i]
            up[96 * i : 96 * i + 96, 256 * b : 256 * b + 256] = piece[:, 0:256]
            for e in range(2):
                down[192 * b + 96 * e : 192 * b + 96 * e + 96, 128 * i : 128 * i + 128] = piece[
                    :, 256 + 128 * e : 384 + 128 * e
                ]


def feed_group(group, vec, n2, gb, up, down, act, gh, br2, gn2, bias_grad, grads, row, block):
    up_bias = jnp.concatenate(
        [
            vec[10 + i // 2 : 11 + i // 2, 384 * (i % 2) + 128 * group : 384 * (i % 2) + 128 * group + 128]
            for i in range(8)
        ],
        axis=1,
    )
    bias_sum = jnp.zeros((1, TILE), F32)
    for m in range(IMGS):
        rows = slice(m * SLOTS, m * SLOTS + SLOTS)
        active, slope = gelu_parts(dot(n2[rows], up[...]) + up_bias)
        act[rows] = active.astype(BF16)
        low = (dot(gb[rows], down[...]) * slope).astype(BF16)
        gh[rows] = low
        bias_sum += column_sum(low.astype(F32))
    bias_grad[:, TILE * group : TILE * group + TILE] = bias_sum
    for m in range(IMGS):
        rows = slice(m * SLOTS, m * SLOTS + SLOTS)
        new = dot_nt(act[rows], down[...])
        br2[rows] = new if group == 0 else br2[rows] + new
        new = dot_nt(gh[rows], up[...])
        gn2[rows] = new if group == 0 else gn2[rows] + new
    at = slice(row, row + 96)
    up_grad = dot_tn(n2[...], gh[...]).astype(BF16)
    for b in range(4):
        for i in range(8):
            grads[block(b, i), at, 0:256] = up_grad[96 * i : 96 * i + 96, 256 * b : 256 * b + 256]
    down_grad = dot_tn(gb[...], act[...]).astype(BF16)
    for b in range(4):
        for i in range(8):
            for e in range(2):
                grads[block(b, i), at, 256 + 128 * e : 384 + 128 * e] = down_grad[
                    192 * b + 96 * e : 192 * b + 96 * e + 96, 128 * i : 128 * i + 128
                ]


def feed_body(
    io, info, far, ins, outs, groups, tails, up, down, act, gh, br2, gn2, out, branch_ref, n2, gb, sems
):
    x, mixed, table, cot = ins
    layer, middle_grad, mixed_grad, vec_grad, bias_grad, grads, last_grads = outs
    block = blocks_of(info)
    copies = [pltpu.make_async_copy(far.at[:, pl.ds(288, 48)], tails, sems.at[3])] + [
        pltpu.make_async_copy(far.at[:, pl.ds(96 * s, 96)], groups.at[s], sems.at[s]) for s in range(GROUPS)
    ]
    for copy in copies:
        copy.start()
    copies[0].wait()
    for b in range(4):
        for i in range(8):
            wide = tails[b * 8 + i, 0:32, 0:384]
            thin = tails[b * 8 + i, :, 384:512]
            for g in range(3):
                out[96 * i + 32 * g : 96 * i + 32 * g + 32, 192 * b : 192 * b + 128] = wide[:, 128 * g : 128 * g + 128]
            for g in range(2):
                out[96 * i + 48 * g : 96 * i + 48 * g + 48, 192 * b + 128 : 192 * b + 192] = thin[:, 64 * g : 64 * g + 64]
    io.need(0, 1, 2, 3)
    vec = table[...]
    for m in range(IMGS):
        rows = slice(m * SLOTS, m * SLOTS + SLOTS)
        branch = dot(mixed[:, m].reshape(SLOTS, D), out[...]) + vec[4:5]
        branch_ref[rows] = branch
        xh, _ = norm_parts(image_values(x, m).astype(F32) + vec[5:6] * branch)
        n2[rows] = (xh * vec[6:7] + vec[7:8]).astype(BF16)
        back = image_values(cot, m).astype(F32) * valid_slots(info, m)
        gb[rows] = (back * vec[9:10]).astype(BF16)
    for group in range(GROUPS):
        copies[1 + group].wait()
        spread_group(groups.at[group], up, down)
        target, row, at = (grads, 96 * group, lambda b, i: b * 8 + i) if group < 2 else (last_grads, 0, block)
        feed_group(group, table, n2, gb, up, down, act, gh, br2, gn2, bias_grad, target, row, at)
        if group == 1:
            io.put(5)
    sums = [jnp.zeros((1, D), F32) for _ in range(10)]
    for m in range(IMGS):
        rows = slice(m * SLOTS, m * SLOTS + SLOTS)
        valid = valid_slots(info, m)
        back = image_values(cot, m).astype(F32) * valid
        branch = branch_ref[rows]
        middle = image_values(x, m).astype(F32) + vec[5:6] * branch
        xh, inverse = norm_parts(middle)
        branch_two = br2[rows] + vec[8:9]
        set_image(layer, m, ((middle + vec[9:10] * branch_two) * valid).astype(BF16))
        sums[9] += column_sum(back * branch_two)
        sums[8] += column_sum(gb[rows].astype(F32))
        gy = gn2[rows]
        sums[6] += column_sum(gy * xh)
        sums[7] += column_sum(gy)
        grad = norm_back(gy, vec[6:7], xh, inverse) + back
        middle_grad[rows] = grad
        sums[5] += column_sum(grad * branch)
        low = (grad * vec[5:6]).astype(BF16)
        sums[4] += column_sum(low.astype(F32))
        gh[rows, :D] = low
        mixed_grad[:, m] = dot_nt(low, out[...]).astype(BF16).reshape(4, 64, D)
        act[rows, :D] = mixed[:, m].reshape(SLOTS, D)
    for k in range(10):
        vec_grad[k : k + 1] = sums[k]
    vec_grad[10:16] = jnp.zeros((6, D), F32)
    io.put(0, 1, 2, 3, 4)
    out_grad = dot_tn(act[:, :D], gh[:, :D]).astype(BF16)
    for b in range(4):
        for i in range(8):
            piece = out_grad[96 * i : 96 * i + 96, 192 * b : 192 * b + 192]
            at = block(b, i)
            for g in range(3):
                last_grads[at, 96:128, 128 * g : 128 * g + 128] = piece[32 * g : 32 * g + 32, 0:128]
            last_grads[at, 128:144, 0:384] = jnp.zeros((16, 384), BF16)
            last_grads[at, 96:144, 384:512] = jnp.concatenate([piece[0:48, 128:192], piece[48:96, 128:192]], axis=1)


def attend_back_kernel(info, qkv, total, mixed_grad, gq):
    column = (valid_slots(info, pl.program_id(0)) - 1.0) * -MASK_FILL
    for b in range(4):
        gq[b, :, 0, :, 512:640] = jnp.zeros((4, 64, 128), BF16)
    for h in range(H):
        q = head_cut(qkv, h) * BF16(HD**-0.5)
        k = head_cut(qkv, H + h)
        v = head_cut(qkv, 2 * H + h)
        base = h // 2 * 128
        tile = mixed_grad[:, 0, :, base : base + 128].reshape(SLOTS, 128)
        grad_out = tile[:, h % 2 * HD : h % 2 * HD + HD]
        scores = dot_nt(k, q) + column
        again = jnp.exp(scores - total[0, h : h + 1, :])
        grad_weights = dot_nt(v, grad_out)
        center = column_sum(again * grad_weights)
        grad_scores = (again * (grad_weights - center)).astype(BF16)
        parts = (
            jnp.transpose(dot_tn(k, grad_scores)) * (HD**-0.5),
            dot(grad_scores, q),
            dot(again.astype(BF16), grad_out),
        )
        for j, part in zip((h, H + h, 2 * H + h), parts):
            lane = (j % 9) * HD
            gq[j // 9, :, 0, :, lane : lane + HD] = part.astype(BF16).reshape(4, 64, HD)


def project_back_body(io, info, ins, outs, n1):
    x, table, gq, weights, vec_in, bias, middle_grad = ins
    token_grad, grads = outs
    block = blocks_of(info)
    io.need(0, 1)
    vec = table[...]
    io.need(2, 3)
    gy = [jnp.zeros((SLOTS, D), F32) for _ in range(IMGS)]
    for b in range(4):
        w = joined(weights, block, b)
        for m in range(IMGS):
            gy[m] += dot_nt(gq[b, :, m].reshape(SLOTS, W1), w)
    io.need(4, 5, 6)
    gain_sum, shift_sum = jnp.zeros((1, D), F32), jnp.zeros((1, D), F32)
    for m in range(IMGS):
        rows = slice(m * SLOTS, m * SLOTS + SLOTS)
        xh, inverse = norm_parts(image_values(x, m).astype(F32))
        n1[rows] = (xh * vec[0:1] + vec[1:2]).astype(BF16)
        gain_sum += column_sum(gy[m] * xh)
        shift_sum += column_sum(gy[m])
        grad = norm_back(gy[m], vec[0:1], xh, inverse) + middle_grad[rows]
        set_image(token_grad, m, grad.astype(BF16))
    io.put(0)
    col = []
    for b in range(4):
        total = jnp.zeros((1, W1), F32)
        for m in range(IMGS):
            total += column_sum(gq[b, :, m].reshape(SLOTS, W1).astype(F32))
        col.append(total[:, :576])
    flat = jnp.concatenate(col, axis=1)
    up_rows = [
        jnp.concatenate(
            [bias[:, TILE * s + 128 * i : TILE * s + 128 * i + 128] for i in (2 * k, 2 * k + 1) for s in range(GROUPS)],
            axis=1,
        )
        for k in range(4)
    ]
    rows = [jnp.zeros((64, D), F32), gain_sum, shift_sum, flat[:, :D], flat[:, 2 * D :], vec_in[4:10]]
    tail = jnp.transpose(jnp.concatenate(rows + up_rows + [jnp.zeros((50, D), F32)], axis=0))
    for b in range(4):
        grad_rows = jnp.concatenate([gq[b, :, m].reshape(SLOTS, W1) for m in range(IMGS)], axis=0)
        grad = dot_tn(n1[...], grad_rows)
        last = (grad[:, 512:640] + tail).astype(BF16)
        grad = grad.astype(BF16)
        for i in range(8):
            at = block(b, i)
            grads[at, :, 0:512] = grad[96 * i : 96 * i + 96, 0:512]
            grads[at, :, 512:640] = last[96 * i : 96 * i + 96]


def total_of(refs):
    return sum(ref[...].astype(F32) for ref in refs)


def step_into(outs, refs, gradient, rate, decay):
    master, first, second = (ref[...] for ref in refs)
    for ref, value in zip(outs, adamw_update(master, gradient, first, second, rate, decay)):
        ref[...] = value


def feed_step_body(io, ins, outs):
    io.need(*range(14))
    up, turned, out = unpack_groups(ins[0][0].astype(F32), total_of(ins[1:5]))
    step_into(outs[0:3], ins[5:8], up, D ** (-0.5), MATRIX_DECAY)
    step_into(outs[3:6], ins[8:11], turned, FF ** (-0.5), MATRIX_DECAY)
    step_into(outs[6:9], ins[11:14], out, (D // 64) ** (-0.5), MATRIX_DECAY)


def project_step_body(io, ins, outs):
    io.need(*range(10))
    total = total_of(ins[0:4])
    step_into(outs[0:3], ins[4:7], total[:, :576], D ** (-0.5), MATRIX_DECAY)
    vector_grad = jnp.transpose(total[:, 512:640])[64:78]
    step_into(outs[3:6], ins[7:10], vector_grad, VECTOR_RATE, 0.0)
    outs[6][...] = vector_grad[8:9]


def place_body(io, info, ins, outs):
    io.need(0)
    for k in range(4):
        outs[0][pl.ds(info[FLIP + k] * IMGS, IMGS)] = ins[0][IMGS * k : IMGS * k + IMGS].astype(outs[0].dtype)


def swap_band(values, k):
    return lax.ppermute(values, "band", [(b, b ^ k) for b in range(lax.axis_size("band"))])


def swap_dp(values, k):
    return lax.ppermute(values, "dp", [(d, d ^ k) for d in range(lax.axis_size("dp"))])


def swap_corner(values):
    bands, rows = lax.axis_size("band"), lax.axis_size("dp")
    pairs = [(d * bands + b, (d ^ 1) * bands + (b ^ 2)) for d in range(rows) for b in range(bands)]
    return lax.ppermute(values, ("dp", "band"), pairs)


def swap_pieces(pieces):
    return [pieces[0]] + [swap_dp(pieces[k], 2 * k) for k in (1, 2, 3)]


def image_parts(values, mine):
    groups = values.reshape(4, IMGS, 64, D)
    return [lax.dynamic_index_in_dim(groups, mine ^ k, 0, keepdims=False) for k in range(4)]


def swap_images(parts):
    return [parts[0]] + [swap_band(parts[k], k) for k in (1, 2, 3)]


def pack_first(qkv, vectors):
    return jnp.concatenate([qkv, vectors, jnp.zeros((qkv.shape[0], W1 - 590), BF16)], axis=1)


def pack_group(up, turned, group):
    at = 128 * group
    pieces = (up[:, at : at + 128], up[:, at + 384 : at + 512], turned[:96, at : at + 128], turned[96:, at : at + 128])
    return jnp.concatenate(pieces, axis=1)


def pack_out(out):
    wide = jnp.concatenate([out[:32, :128], out[32:64, :128], out[64:, :128]], axis=1)
    thin = jnp.concatenate([out[:48, 128:], out[48:, 128:]], axis=1)
    return jnp.concatenate([jnp.concatenate([wide, jnp.zeros((16, 384), BF16)], axis=0), thin], axis=1)


def unpack_groups(head, rest):
    groups, last = [head[:96], head[96:], rest[:96]], rest[96:]
    up = jnp.concatenate([groups[s][:, 128 * e : 128 * e + 128] for e in range(2) for s in range(GROUPS)], axis=1)
    turned = jnp.concatenate(
        [
            jnp.concatenate([groups[s][:, 256 + 128 * e : 384 + 128 * e] for s in range(GROUPS)], axis=1)
            for e in range(2)
        ],
        axis=0,
    )
    wide = jnp.concatenate([last[:32, 128 * g : 128 * g + 128] for g in range(3)], axis=0)
    thin = jnp.concatenate([last[:, 384:448], last[:, 448:512]], axis=0)
    return up, turned, jnp.concatenate([wide, thin], axis=1)


def together(*values):
    return lax.optimization_barrier(values)


def gather_blocks_full(blocks):
    parts = [blocks, swap_band(blocks, 2)]
    return parts + [swap_band(part, 1) for part in parts]


def add(*terms):
    return sum(term.astype(F32) for term in terms).astype(BF16)


NEAR, ACROSS, BESIDE, CORNER = [slice(4 * k, 4 * k + 4) for k in range(4)]


def corner_halves(keep, other):
    return [add(keep[cut], other[cut]) for cut in (slice(12, 14), slice(14, 16))]


def side_parts(keep, other, from_across, from_beside):
    zeros = jnp.zeros_like(from_across)
    across = add(keep[ACROSS], other[ACROSS], jnp.concatenate([zeros, from_beside]))
    beside = add(keep[BESIDE], other[BESIDE], jnp.concatenate([from_across, zeros]))
    return across, beside


def three_parts(keep, other):
    return [add(keep[part], other[part]) for part in (ACROSS, BESIDE, CORNER)]


def swap_three(parts):
    return [swap_dp(parts[0], 1), swap_band(parts[1], 2), swap_corner(parts[2])]


def near_parts(keep, other, *more):
    return [add(keep[k], other[k], *(part[k] for part in more)) for k in range(4)]


def reduce_blocks_full(keep, send):
    other = swap_band(send, 1)
    got = swap_band(add(keep[8:], other[8:]), 2)
    return add(keep[:8], other[:8], got)


def image_call(body, info, operands, outs, flops):
    def spec(shape):
        place = next(k for k, size in enumerate(shape) if size == IMGS)
        block = tuple(1 if k == place else size for k, size in enumerate(shape))
        return pl.BlockSpec(block, lambda m: tuple(m if k == place else 0 for k in range(len(shape))))

    moved = sum(v.size * v.dtype.itemsize for v in (*operands, *outs))
    return pl.pallas_call(
        body,
        grid=(IMGS,),
        out_shape=outs,
        in_specs=[pl.BlockSpec(memory_space=pltpu.SMEM)] + [spec(v.shape) for v in operands],
        out_specs=tuple(spec(v.shape) for v in outs),
        compiler_params=pltpu.CompilerParams(vmem_limit_bytes=58 * MIB),
        cost_estimate=pl.CostEstimate(flops=flops, bytes_accessed=moved, transcendentals=0),
    )(info, *operands)


def on_device(
    tokens, cotangent, image_rows, qkv_weight, out_weight, up_weight, down_weight, vectors,
    qkv_first, out_first, up_first, down_first, vector_first,
    qkv_second, out_second, up_second, down_second, vector_second,
):
    dp_mine = lax.axis_index("dp")
    mine = lax.axis_index("band")
    direct = lax.axis_size("dp") == 8
    numbers = lambda n: jnp.arange(n, dtype=jnp.int32)
    flip = numbers(4) ^ mine
    if direct:
        turn = numbers(8) ^ dp_mine
        place = turn % 2 * 4 + turn // 2
    else:
        place = numbers(8)
    limits = lax.dynamic_slice_in_dim(image_rows, mine * IMGS, IMGS)
    info = jnp.concatenate([flip % 2 * 2 + flip // 2, place, flip, limits]).astype(jnp.int32)
    if direct:
        (pack1,) = staged_call(pack_first_body, [], [qkv_weight, vectors.T], [sds((96, W1), BF16)], [], 1_000_000)
        near1 = swap_pieces([pack1] * 4)
        x = image_parts(tokens, mine)
        x[2:4] = [swap_band(x[2], 2), swap_band(x[3], 3)]
        pack1, wide_up = together(pack1, up_weight)
        (pack2,) = staged_call(
            pack_second_body, [], [wide_up, down_weight.T, out_weight], [sds((336, 512), BF16)], [], 1_000_000
        )
        second = lax.all_gather(pack2, ("band", "dp"), axis=0)
        cot = image_parts(cotangent, mine)
        near1, cot, x = together(near1, cot, x)
        x[1] = swap_band(x[1], 1)
        near1 = jnp.stack(near1)
        across1, beside1, x = together(swap_dp(near1, 1), swap_band(near1, 2), x)
        corner1 = [swap_band(across1[:2], 2), swap_dp(beside1[2:], 1)]
        near1c, across1c, beside1c = [swap_band(part, 1) for part in (near1, across1, beside1)]
        corner1, near1c, across1c, beside1c = together(corner1, near1c, across1c, beside1c)
        corner1c, cot = together([swap_band(part, 1) for part in corner1], cot)
        first = [near1, across1, beside1, *corner1, near1c, across1c, beside1c, *corner1c]
        cot = swap_images(cot)
    else:
        low = [w.astype(BF16) for w in (qkv_weight, out_weight, up_weight, down_weight, vectors)]
        x = swap_images(image_parts(tokens, mine))
        cot = swap_images(image_parts(cotangent, mine))
        qkv_all, out_all, up_all, down_all, vec_all = [
            lax.all_gather(w, "dp", axis=0, tiled=True) for w in low
        ]
        cut = lambda v, n: [v[n * i : n * i + n] for i in range(8)]
        first = jnp.stack([pack_first(q, v) for q, v in zip(cut(qkv_all, 96), cut(vec_all, 96))])
        groups = [
            jnp.stack([pack_group(u, d.T, s) for u, d in zip(cut(up_all, 96), cut(down_all, 384))])
            for s in range(GROUPS)
        ]
        outs = jnp.stack([pack_out(o) for o in cut(out_all, 96)])
        first = gather_blocks_full(first)
        second = lax.all_gather(jnp.concatenate([*groups, outs], axis=1), "band", axis=0, tiled=True)

    rows_shape = (4, IMGS, 64, D)
    vmem = pltpu.VMEM
    piece = [sds((IMGS, 64, D), BF16)] * 4
    wide, wide32 = sds((R, D), BF16), sds((R, D), F32)
    table = sds((16, D), F32)
    qkv_shape = sds((4, 4, IMGS, 64, W1), BF16)
    halves = lambda rows, lanes: [sds((16, rows, lanes), BF16)] * 2
    qkv, vec = staged_call(
        project_body, [info], [x, first], [qkv_shape, table], [vmem((IMGS, SLOTS, D), F32)], 2_800_000_000
    )
    mixed, totals = image_call(
        attend_kernel, info, (qkv,), (sds(rows_shape, BF16), sds((IMGS, H, SLOTS), F32)), 3_000_000_000
    )
    *layer, middle_grad, mixed_grad, vec_grad, bias_grad, grads0, keep1, send1 = staged_call(
        feed_body, [info], [x, mixed, vec, cot],
        [piece, wide32, sds(rows_shape, BF16), table, sds((1, FF), F32), sds((32, 192, 512), BF16), halves(144, 512)],
        [vmem((GROUPS, 32, 96, 512), BF16), vmem((32, 48, 512), BF16)]
        + [vmem((R, TILE), BF16) for _ in range(4)]
        + [vmem((R, D), F32), vmem((R, D), F32), vmem((R, D), BF16), vmem((R, D), F32)]
        + [vmem((R, D), BF16), vmem((R, D), BF16), pltpu.SemaphoreType.DMA((4,))],
        25_000_000_000, [second],
    )
    home = lambda parts: [parts[0]] + [swap_band(parts[k], k) for k in (1, 2, 3)]
    if direct:
        total0 = lax.psum_scatter(grads0, ("band", "dp"), scatter_dimension=0, tiled=True)
        other1, mixed_grad = together(swap_band(send1, 1), mixed_grad)
        corner1, mixed_grad = together(corner_halves(keep1, other1), mixed_grad)
        got_corner1 = [swap_dp(corner1[0], 1), swap_band(corner1[1], 2)]
    (gq,) = image_call(attend_back_kernel, info, (qkv, totals, mixed_grad), (qkv_shape,), 6_000_000_000)
    if direct:
        gq, got_corner1 = together(gq, got_corner1)
        across1, beside1 = side_parts(keep1, other1, *got_corner1)
        gq, across1, beside1 = together(gq, across1, beside1)
        got_across1, got_beside1 = swap_dp(across1, 1), swap_band(beside1, 2)
        layer = home(layer)
    *token_grad, keep2, send2 = staged_call(
        project_back_body, [info], [x, vec, gq, first, vec_grad, bias_grad, middle_grad],
        [piece, halves(96, W1)], [vmem((R, D), BF16)], 5_600_000_000,
    )
    states = [
        (up_weight, up_first, up_second), (down_weight.T, down_first.T, down_second.T),
        (out_weight, out_first, out_second), (qkv_weight, qkv_first, qkv_second),
        (vectors.T, vector_first.T, vector_second.T),
    ]
    like = lambda state: [sds(v.shape, F32) for v in state]
    if direct:
        send2, got_across1, got_beside1, layer = together(send2, got_across1, got_beside1, layer)
        other2 = swap_band(send2, 1)
        near1 = near_parts(keep1, other1, got_across1, got_beside1)
        other2, near1 = together(other2, near1)
        corner2 = corner_halves(keep2, other2)
        got_corner2 = [swap_dp(corner2[0], 1), swap_band(corner2[1], 2)]
        got_corner2, near1, token_grad = together(got_corner2, near1, token_grad)
        across2, beside2 = side_parts(keep2, other2, *got_corner2)
        across2, beside2, near1, token_grad = together(across2, beside2, near1, token_grad)
        got_across2, got_beside2 = swap_dp(across2, 1), swap_band(beside2, 2)
        parts1 = swap_pieces(near1)
        got_across2, got_beside2, token_grad = together(got_across2, got_beside2, token_grad)
        near2 = near_parts(keep2, other2, got_across2, got_beside2)
        near2, parts1, token_grad = together(near2, parts1, token_grad)
        parts2 = swap_pieces(near2)
        token_grad = home(token_grad)
        news = staged_call(
            feed_step_body, [], [total0] + parts1 + [v for s in states[:3] for v in s],
            [v for s in states[:3] for v in like(s)], [], 20_000_000,
        )
        last = staged_call(
            project_step_body, [], parts2 + [v for s in states[3:] for v in s],
            [v for s in states[3:] for v in like(s)] + [sds((1, 96), F32)], [], 10_000_000,
        )
        news = [news[0:3], [v.T for v in news[3:6]], news[6:9], last[0:3], [v.T for v in last[3:6]]]
        down_bias_gradient = last[6].reshape(-1)
    else:
        grads0 = lax.psum_scatter(grads0, "band", scatter_dimension=0, tiled=True)
        grads = [grads0] + [reduce_blocks_full(*pair) for pair in ((keep1, send1), (keep2, send2))]
        parts = [unpack_groups(grads[0][i], grads[1][i]) for i in range(8)]
        parts = [(up, turned.T, out) for up, turned, out in parts]
        full = [jnp.concatenate(p) for p in zip(*parts)] + [grads[2].reshape(D, W1)[:, :576], grads[2].reshape(D, W1)[:, 576:590]]
        full = [lax.psum_scatter(g.astype(F32), "dp", scatter_dimension=0, tiled=True) for g in full]
        states[1] = (down_weight, down_first, down_second)
        states[4] = (vectors, vector_first, vector_second)
        rates = (D ** (-0.5), FF ** (-0.5), (D // 64) ** (-0.5), D ** (-0.5), VECTOR_RATE)
        decays = (MATRIX_DECAY,) * 4 + (0.0,)
        news = [
            adamw_update(master, grad, one, two, rate, decay)
            for (master, one, two), grad, rate, decay in zip(states, full, rates, decays)
        ]
        down_bias_gradient = full[4][:, 8]
        layer, token_grad = home(layer), home(token_grad)
    place_call = lambda parts, dtype: staged_call(place_body, [info], [parts], [sds(tokens.shape, dtype)], [], 1_000_000)[0]
    layer_out = place_call(layer, BF16)
    token_out = place_call(token_grad, F32)
    order = [news[3], news[2], news[0], news[1], news[4]]
    return (
        (layer_out, token_out)
        + tuple(n[0] for n in order)
        + tuple(n[1] for n in order)
        + tuple(n[2] for n in order)
        + (down_bias_gradient,)
    )


def solution(mesh):
    rows, matrix, table = P("dp", "band", None), P("dp", "band"), P("dp", None)
    state = (matrix, matrix, matrix, matrix, table)
    return jax.shard_map(
        on_device,
        mesh=mesh,
        in_specs=(rows, rows, P("dp")) + state + state + state,
        out_specs=(rows, rows) + state + state + state + (P("dp"),),
        check_vma=False,
    )
```

```python
import math
from functools import partial

import jax
import jax.numpy as jnp
from jax import lax
from jax.experimental import pallas as pl
from jax.experimental.pallas import tpu as pltpu
from jax.sharding import PartitionSpec as P

D = 768
H = 12
HD = 64
FF = 3072
GRID = 16
STEP = 7
SLOTS = 256
NORM_EPS = 1e-06
ADAM_EPS = 1e-08
BETA_ONE = 0.5
BETA_TWO = 0.6
MATRIX_DECAY = 0.05
VECTOR_RATE = 0.5
MASK_FILL = -1e30
R = 768
IMGS = 3
W1 = 640
GROUPS = 3
TILE = FF // GROUPS
FLIP, LIMIT, SECOND, FIRST = 12, 16, 19, 31
F32 = jnp.float32
BF16 = jnp.bfloat16
MIB = 1024 * 1024


def adamw_update(master, gradient, moment_one, moment_two, step_rate, weight_decay):
    first_new = BETA_ONE * moment_one + (1.0 - BETA_ONE) * gradient
    second_new = BETA_TWO * moment_two + (1.0 - BETA_TWO) * gradient * gradient
    first_hat = first_new / (1.0 - BETA_ONE**STEP)
    second_hat = second_new / (1.0 - BETA_TWO**STEP)
    master_new = master - step_rate * (
        first_hat / (jnp.sqrt(second_hat) + ADAM_EPS) + weight_decay * master
    )
    return (master_new, first_new, second_new)


def dot(a, b):
    return lax.dot_general(a, b, (((1,), (0,)), ((), ())), preferred_element_type=F32)


def dot_nt(a, b):
    return lax.dot_general(a, b, (((1,), (1,)), ((), ())), preferred_element_type=F32)


def dot_tn(a, b):
    return lax.dot_general(a, b, (((0,), (0,)), ((), ())), preferred_element_type=F32)


def sds(shape, dtype):
    return jax.ShapeDtypeStruct(shape, dtype)


def as_list(value):
    return list(value) if isinstance(value, list) else [value]


class Staging:
    def __init__(self, ins, in_sems, outs, out_sems):
        self.waits = [[pltpu.make_async_copy(s, t, in_sems.at[n]) for s, t, n in group] for group in ins]
        self.puts = [[pltpu.make_async_copy(s, t, out_sems.at[n]) for s, t, n in group] for group in outs]
        self.waited, self.started, self.begun = set(), set(), False

    def begin(self):
        if not self.begun:
            self.begun = True
            for group in self.waits:
                for copy in group:
                    copy.start()

    def need(self, *which):
        self.begin()
        for k in which:
            if k not in self.waited:
                self.waited.add(k)
                for copy in self.waits[k]:
                    copy.wait()

    def put(self, *which):
        for k in which:
            if k not in self.started:
                self.started.add(k)
                for copy in self.puts[k]:
                    copy.start()

    def finish(self):
        self.need(*range(len(self.waits)))
        self.put(*range(len(self.puts)))
        for group in self.puts:
            for copy in group:
                copy.wait()


def staged_call(body, smem, operands, outs, scratch, flops, far=(), far_outs=()):
    given = [[v if isinstance(v, tuple) else (v, None) for v in as_list(group)] for group in operands]
    operands = given
    picks = [pick for group in operands for _, pick in group]
    operands = [[v if pick is None else sds(v.shape[1:], v.dtype) for v, pick in group] for group in operands]
    outs = [as_list(v) for v in outs]
    flat_in = [v for group in given for v, _ in group]
    flat_out = [v for group in outs for v in group]

    def buffer(group):
        return pltpu.VMEM((sum(v.shape[0] for v in group), *group[0].shape[1:]), group[0].dtype)

    def kernel(*refs):
        refs = list(refs)
        take = lambda n: [refs.pop(0) for _ in range(n)]
        info, sources, raw, targets, raw_out = [
            take(len(part)) for part in (smem, flat_in, far, flat_out, far_outs)
        ]
        sources = [ref if pick is None else ref.at[pick] for ref, pick in zip(sources, picks)]
        in_refs, out_refs, extra = take(len(operands)), take(len(outs)), take(len(scratch))
        in_sems, out_sems = refs

        def pairs(groups, far, near, outward):
            result, n = [], 0
            for group, ref in zip(groups, near):
                row, entry = 0, []
                for v in group:
                    part = ref if len(group) == 1 else ref.at[pl.ds(row, v.shape[0])]
                    entry.append((part, far[n], n) if outward else (far[n], part, n))
                    row, n = row + v.shape[0], n + 1
                result.append(entry)
            return result

        staging = Staging(
            pairs(operands, sources, in_refs, False), in_sems, pairs(outs, targets, out_refs, True), out_sems
        )
        body(staging, *info, *raw, *raw_out, in_refs, out_refs, *extra)
        staging.finish()

    moved = sum(v.size * v.dtype.itemsize for v in (*flat_in, *far, *flat_out, *far_outs))
    return pl.pallas_call(
        kernel,
        out_shape=(*flat_out, *far_outs),
        in_specs=[pl.BlockSpec(memory_space=pltpu.SMEM) for _ in smem]
        + [pl.BlockSpec(memory_space=pl.ANY) for _ in (*flat_in, *far)],
        out_specs=tuple(pl.BlockSpec(memory_space=pl.ANY) for _ in (*flat_out, *far_outs)),
        scratch_shapes=[buffer(g) for g in operands]
        + [buffer(g) for g in outs]
        + list(scratch)
        + [pltpu.SemaphoreType.DMA((len(flat_in),)), pltpu.SemaphoreType.DMA((len(flat_out),))],
        compiler_params=pltpu.CompilerParams(vmem_limit_bytes=58 * MIB),
        cost_estimate=pl.CostEstimate(flops=flops, bytes_accessed=moved, transcendentals=0),
    )(*smem, *flat_in, *far)


def first_rows(rows):
    return rows // 32 * 16


def part_shapes(rows, lanes):
    low = first_rows(rows)
    pair = [sds((2, 4, low, lanes), BF16), sds((2, 4, rows - low, lanes), BF16)]
    return pair + pair + pair + pair


def part_copies(grads, refs, sems):
    rows = grads.shape[1]
    low = first_rows(rows)
    copies = []
    for core in range(2):
        for first in (1, 0):
            by_dp, by_band = refs[core * 4 + (1 - first) * 2], refs[core * 4 + (1 - first) * 2 + 1]
            for n in range(2):
                at = core * 16 + n * 8 + first * 4
                copies.append((grads.at[pl.ds(at, 4), pl.ds(0, low)], by_dp.at[n]))
                at = core * 16 + first * 8 + n * 4
                copies.append((grads.at[pl.ds(at, 4), pl.ds(low, rows - low)], by_band.at[n]))
    return [pltpu.make_async_copy(source, target, sems.at[n]) for n, (source, target) in enumerate(copies)]


def norm_parts(values):
    center = values - jnp.mean(values, axis=-1, keepdims=True)
    spread = jnp.mean(center * center, axis=-1, keepdims=True)
    inverse = lax.rsqrt(spread + NORM_EPS)
    return center * inverse, inverse


def norm_back(gy, gain, xh, inverse):
    e = gy * gain
    return inverse * (
        e - jnp.mean(e, axis=-1, keepdims=True) - xh * jnp.mean(e * xh, axis=-1, keepdims=True)
    )


def column_sum(values):
    return jnp.sum(values, axis=0, keepdims=True)


def image_values(ref, m):
    return jnp.concatenate([ref[IMGS * k + m] for k in range(4)], axis=0)


def set_image(ref, m, values):
    for k in range(4):
        ref[IMGS * k + m] = values[64 * k : 64 * k + 64]


def valid_slots(info, m):
    columns = []
    for k in range(4):
        slot = lax.broadcasted_iota(jnp.int32, (64, 1), 0) + info[FLIP + k] * 64
        inside = ((slot >> 4) < info[LIMIT + m]) & ((slot & 15) < info[LIMIT + m])
        columns.append(inside.astype(F32))
    return jnp.concatenate(columns, axis=0)


def blocks_of(info):
    return lambda b, i: info[b] * 8 + info[4 + i]


def blocks_first(info):
    return lambda b, i: info[b] * 8 + info[FIRST + i]


def blocks_second(info):
    return lambda b, i: info[SECOND + b] * 8 + info[SECOND + 4 + i]


def joined(weights, block, b):
    return jnp.concatenate([weights[block(b, i)] for i in range(8)], axis=0)


def head_cut(ref, j):
    lane = (j % 9) * HD
    base = lane // 128 * 128
    tile = ref[j // 9, :, 0, :, base : base + 128].reshape(SLOTS, 128)
    return tile[:, lane - base : lane - base + HD]


def pack_first_body(io, ins, outs):
    io.need(0, 1)
    qkv, table = ins[0][...], ins[1][...]
    table = jnp.concatenate([table, jnp.zeros((50, table.shape[1]), F32)], axis=0)
    outs[0][:, 0:512] = qkv[:, 0:512].astype(BF16)
    outs[0][:, 512:640] = jnp.concatenate([qkv[:, 512:576], jnp.transpose(table)], axis=1).astype(BF16)


def pack_second_body(io, ins, outs):
    io.need(0, 1, 2)
    up, turned, out = (ref[...].astype(BF16) for ref in ins)
    for group in range(GROUPS):
        at, row = 128 * group, 96 * group
        pieces = (up[:, at : at + 128], up[:, at + 384 : at + 512], turned[:96, at : at + 128], turned[96:, at : at + 128])
        for n, piece in enumerate(pieces):
            outs[0][row : row + 96, 128 * n : 128 * n + 128] = piece
    outs[0][288:336, :] = pack_out(out)


def project_body(io, info, ins, outs, n1):
    x, weights = ins
    qkv, table = outs
    block = blocks_first(info)
    io.need(0)
    for m in range(IMGS):
        n1[m], _ = norm_parts(image_values(x, m).astype(F32))
    io.need(1)
    tail = jnp.concatenate([weights[block(0, i), :, 512:640] for i in range(8)], axis=0)
    vec = jnp.transpose(tail.astype(F32))[64:80]
    table[...] = vec
    bias = jnp.concatenate(
        [vec[2:3], jnp.zeros((1, D), F32), vec[3:4], jnp.zeros((1, 64), F32)], axis=1
    )
    normed = [(n1[m] * vec[0:1] + vec[1:2]).astype(BF16) for m in range(IMGS)]
    for b in range(4):
        w = joined(weights, block, b)
        for m in range(IMGS):
            part = dot(normed[m], w) + bias[:, 576 * b : 576 * b + W1]
            qkv[b, :, m] = part.astype(BF16).reshape(4, 64, W1)


def attend_kernel(info, qkv, mixed, total):
    column = (valid_slots(info, pl.program_id(0)) - 1.0) * -MASK_FILL
    for pair in range(H // 2):
        halves = []
        for h in (2 * pair, 2 * pair + 1):
            q = head_cut(qkv, h) * BF16(HD**-0.5)
            k = head_cut(qkv, H + h)
            v = head_cut(qkv, 2 * H + h)
            scores = dot_nt(k, q) + column
            highest = jnp.max(scores, axis=0, keepdims=True)
            shifted = jnp.exp(scores - highest)
            totals = column_sum(shifted)
            low = (shifted * (1.0 / totals)).astype(BF16)
            total[0, h : h + 1, :] = highest + jnp.log(totals)
            halves.append(dot_tn(v, low))
        both = jnp.transpose(jnp.concatenate(halves, axis=0))
        mixed[:, 0, :, 128 * pair : 128 * pair + 128] = both.astype(BF16).reshape(4, 64, 128)


def gelu_parts(v):
    cdf = 0.5 * (1.0 + lax.erf(v * (0.5**0.5)))
    pdf = jnp.exp(v * v * -0.5) * ((2.0 * math.pi) ** -0.5)
    return v * cdf, cdf + v * pdf


def spread_group(weights, row, block, up, down):
    for b in range(4):
        for i in range(8):
            piece = weights[block(b, i), row : row + 96]
            up[96 * i : 96 * i + 96, 256 * b : 256 * b + 256] = piece[:, 0:256]
            for e in range(2):
                down[192 * b + 96 * e : 192 * b + 96 * e + 96, 128 * i : 128 * i + 128] = piece[
                    :, 256 + 128 * e : 384 + 128 * e
                ]


def feed_group(
    group, vec, n2, gb, up, down, act, gh, br2, gn2, bias_grad, lane, grads, row, block, before=None, after=None
):
    up_bias = jnp.concatenate(
        [
            vec[10 + i // 2 : 11 + i // 2, 384 * (i % 2) + 128 * group : 384 * (i % 2) + 128 * group + 128]
            for i in range(8)
        ],
        axis=1,
    )
    bias_sum = jnp.zeros((1, TILE), F32)
    for m in range(IMGS):
        rows = slice(m * SLOTS, m * SLOTS + SLOTS)
        active, slope = gelu_parts(dot(n2[rows], up[...]) + up_bias)
        act[rows] = active.astype(BF16)
        low = (dot(gb[rows], down[...]) * slope).astype(BF16)
        gh[rows] = low
        bias_sum += column_sum(low.astype(F32))
    bias_grad[:, lane : lane + TILE] = bias_sum
    if before:
        before()
    for m in range(IMGS):
        rows = slice(m * SLOTS, m * SLOTS + SLOTS)
        new = dot_nt(act[rows], down[...])
        br2[rows] = new if group == 0 else br2[rows] + new
        new = dot_nt(gh[rows], up[...])
        gn2[rows] = new if group == 0 else gn2[rows] + new
    if after:
        after()
    at = slice(row, row + 96)
    up_grad = dot_tn(n2[...], gh[...]).astype(BF16)
    for b in range(4):
        for i in range(8):
            grads[block(b, i), at, 0:256] = up_grad[96 * i : 96 * i + 96, 256 * b : 256 * b + 256]
    down_grad = dot_tn(gb[...], act[...]).astype(BF16)
    for b in range(4):
        for i in range(8):
            for e in range(2):
                grads[block(b, i), at, 256 + 128 * e : 384 + 128 * e] = down_grad[
                    192 * b + 96 * e : 192 * b + 96 * e + 96, 128 * i : 128 * i + 128
                ]


def store_parts(grads, targets, sems):
    puts = part_copies(grads, targets, sems)
    for put in puts:
        put.start()
    return puts


def load_rows(sources, row, rows, target, sems):
    copies, at = [], 0
    for n, ref in enumerate(sources):
        size = ref.shape[0]
        copies.append(pltpu.make_async_copy(ref.at[:, pl.ds(row, rows)], target.at[pl.ds(at, size)], sems.at[n]))
        at += size
    for copy in copies:
        copy.start()
    return copies


def feed_first_body(io, info, second, ins, outs, groups, tails, up, down, act, gh, sems):
    x, mixed, table, cot = ins
    n2, gb, branch_ref, out, br2, gn2, bias_grad, grads = outs
    second_block = blocks_second(info)
    small = load_rows([second], 288, 48, tails, sems.at[0])
    io.begin()
    large = load_rows([second], 0, 192, groups, sems.at[1])
    for copy in small:
        copy.wait()
    for b in range(4):
        for i in range(8):
            wide = tails[second_block(b, i), 0:32, 0:384]
            thin = tails[second_block(b, i), :, 384:512]
            for g in range(3):
                out[96 * i + 32 * g : 96 * i + 32 * g + 32, 192 * b : 192 * b + 128] = wide[:, 128 * g : 128 * g + 128]
            for g in range(2):
                out[96 * i + 48 * g : 96 * i + 48 * g + 48, 192 * b + 128 : 192 * b + 192] = thin[:, 64 * g : 64 * g + 64]
    io.need(0, 1, 2, 3)
    vec = table[...]
    for m in range(IMGS):
        rows = slice(m * SLOTS, m * SLOTS + SLOTS)
        branch = dot(mixed[:, m].reshape(SLOTS, D), out[...]) + vec[4:5]
        branch_ref[rows] = branch
        xh, _ = norm_parts(image_values(x, m).astype(F32) + vec[5:6] * branch)
        n2[rows] = (xh * vec[6:7] + vec[7:8]).astype(BF16)
        back = image_values(cot, m).astype(F32) * valid_slots(info, m)
        gb[rows] = (back * vec[9:10]).astype(BF16)
    io.put(0, 1, 2, 3)
    for copy in large:
        copy.wait()
    for group in range(2):
        spread_group(groups, 96 * group, second_block, up, down)
        feed_group(
            group, table, n2, gb, up, down, act, gh, br2, gn2, bias_grad, TILE * group, grads, 96 * group,
            lambda b, i: b * 8 + i, None, (lambda: io.put(4, 5)) if group else None,
        )


def feed_last_body(io, info, second, *refs):
    *targets, ins, outs, groups, up, down, act, gh, grads, sems, put_sems = refs
    n2, gb, table, br2, gn2, x, cot, mixed, branch_ref, out = ins
    layer, middle_grad, mixed_grad, vec_grad, bias_grad = outs
    block, second_block = blocks_of(info), blocks_second(info)
    large = load_rows([second], 192, 96, groups, sems)
    io.begin()
    for copy in large:
        copy.wait()
    spread_group(groups, 0, second_block, up, down)
    io.need(0, 1, 2)
    feed_group(
        2, table, n2, gb, up, down, act, gh, br2, gn2, bias_grad, 0, grads, 0, block, lambda: io.need(3, 4)
    )
    io.need(5, 6, 7, 8, 9)
    vec = table[...]
    sums = [jnp.zeros((1, D), F32) for _ in range(10)]
    for m in range(IMGS):
        rows = slice(m * SLOTS, m * SLOTS + SLOTS)
        valid = valid_slots(info, m)
        back = image_values(cot, m).astype(F32) * valid
        branch = branch_ref[rows]
        middle = image_values(x, m).astype(F32) + vec[5:6] * branch
        xh, inverse = norm_parts(middle)
        branch_two = br2[rows] + vec[8:9]
        set_image(layer, m, ((middle + vec[9:10] * branch_two) * valid).astype(BF16))
        sums[9] += column_sum(back * branch_two)
        sums[8] += column_sum(gb[rows].astype(F32))
        gy = gn2[rows]
        sums[6] += column_sum(gy * xh)
        sums[7] += column_sum(gy)
        grad = norm_back(gy, vec[6:7], xh, inverse) + back
        middle_grad[rows] = grad
        sums[5] += column_sum(grad * branch)
        low = (grad * vec[5:6]).astype(BF16)
        sums[4] += column_sum(low.astype(F32))
        gh[rows, :D] = low
        mixed_grad[:, m] = dot_nt(low, out[...]).astype(BF16).reshape(4, 64, D)
        act[rows, :D] = mixed[:, m].reshape(SLOTS, D)
    for k in range(10):
        vec_grad[k : k + 1] = sums[k]
    vec_grad[10:16] = jnp.zeros((6, D), F32)
    io.put(0, 1, 2, 3, 4)
    out_grad = dot_tn(act[:, :D], gh[:, :D]).astype(BF16)
    for b in range(4):
        for i in range(8):
            piece = out_grad[96 * i : 96 * i + 96, 192 * b : 192 * b + 192]
            at = block(b, i)
            for g in range(3):
                grads[at, 96:128, 128 * g : 128 * g + 128] = piece[32 * g : 32 * g + 32, 0:128]
            grads[at, 128:144, 0:384] = jnp.zeros((16, 384), BF16)
            grads[at, 96:144, 384:512] = jnp.concatenate([piece[0:48, 128:192], piece[48:96, 128:192]], axis=1)
    for put in store_parts(grads, targets, put_sems):
        put.wait()


def attend_back_kernel(info, qkv, total, mixed_grad, gq):
    column = (valid_slots(info, pl.program_id(0)) - 1.0) * -MASK_FILL
    for b in range(4):
        gq[b, :, 0, :, 512:640] = jnp.zeros((4, 64, 128), BF16)
    for h in range(H):
        q = head_cut(qkv, h) * BF16(HD**-0.5)
        k = head_cut(qkv, H + h)
        v = head_cut(qkv, 2 * H + h)
        base = h // 2 * 128
        tile = mixed_grad[:, 0, :, base : base + 128].reshape(SLOTS, 128)
        grad_out = tile[:, h % 2 * HD : h % 2 * HD + HD]
        scores = dot_nt(k, q) + column
        again = jnp.exp(scores - total[0, h : h + 1, :])
        grad_weights = dot_nt(v, grad_out)
        center = column_sum(again * grad_weights)
        grad_scores = (again * (grad_weights - center)).astype(BF16)
        parts = (
            jnp.transpose(dot_tn(k, grad_scores)) * (HD**-0.5),
            dot(grad_scores, q),
            dot(again.astype(BF16), grad_out),
        )
        for j, part in zip((h, H + h, 2 * H + h), parts):
            lane = (j % 9) * HD
            gq[j // 9, :, 0, :, lane : lane + HD] = part.astype(BF16).reshape(4, 64, HD)


def project_back_body(io, info, *refs):
    *targets, ins, outs, n1, grads, put_sems = refs
    x, table, gq, weights, vec_in, bias_head, bias_rest, middle_grad = ins
    (token_grad,) = outs
    block = blocks_of(info)
    io.need(0, 1)
    vec = table[...]
    for m in range(IMGS):
        xh, _ = norm_parts(image_values(x, m).astype(F32))
        n1[m * SLOTS : m * SLOTS + SLOTS] = (xh * vec[0:1] + vec[1:2]).astype(BF16)
    io.need(2, 3)
    gy = [jnp.zeros((SLOTS, D), F32) for _ in range(IMGS)]
    for b in range(4):
        w = joined(weights, blocks_first(info), b)
        for m in range(IMGS):
            gy[m] += dot_nt(gq[b, :, m].reshape(SLOTS, W1), w)
    io.need(4, 5, 6, 7)
    bias = jnp.concatenate([bias_head[...], bias_rest[...]], axis=1)
    gain_sum, shift_sum = jnp.zeros((1, D), F32), jnp.zeros((1, D), F32)
    for m in range(IMGS):
        rows = slice(m * SLOTS, m * SLOTS + SLOTS)
        xh, inverse = norm_parts(image_values(x, m).astype(F32))
        gain_sum += column_sum(gy[m] * xh)
        shift_sum += column_sum(gy[m])
        grad = norm_back(gy[m], vec[0:1], xh, inverse) + middle_grad[rows]
        set_image(token_grad, m, grad.astype(BF16))
    io.put(0)
    col = []
    for b in range(4):
        total = jnp.zeros((1, W1), F32)
        for m in range(IMGS):
            total += column_sum(gq[b, :, m].reshape(SLOTS, W1).astype(F32))
        col.append(total[:, :576])
    flat = jnp.concatenate(col, axis=1)
    up_rows = [
        jnp.concatenate(
            [bias[:, TILE * s + 128 * i : TILE * s + 128 * i + 128] for i in (2 * k, 2 * k + 1) for s in range(GROUPS)],
            axis=1,
        )
        for k in range(4)
    ]
    rows = [jnp.zeros((64, D), F32), gain_sum, shift_sum, flat[:, :D], flat[:, 2 * D :], vec_in[4:10]]
    tail = jnp.transpose(jnp.concatenate(rows + up_rows + [jnp.zeros((50, D), F32)], axis=0))
    for b in range(4):
        grad_rows = jnp.concatenate([gq[b, :, m].reshape(SLOTS, W1) for m in range(IMGS)], axis=0)
        grad = dot_tn(n1[...], grad_rows)
        last = (grad[:, 512:640] + tail).astype(BF16)
        grad = grad.astype(BF16)
        for i in range(8):
            at = block(b, i)
            grads[at, :, 0:512] = grad[96 * i : 96 * i + 96, 0:512]
            grads[at, :, 512:640] = last[96 * i : 96 * i + 96]
    puts = part_copies(grads, targets, put_sems)
    for put in puts:
        put.start()
    for put in puts:
        put.wait()


def near_body(io, ins, outs):
    low = ins[0].shape[1]
    for s in range(2):
        terms = ins[4 * s : 4 * s + 4]
        io.need(*range(4 * s, 4 * s + 4))
        rows = slice(low, None) if s else slice(0, low)
        for z in range(4):
            outs[0][z, rows] = sum(term[z].astype(F32) for term in terms).astype(BF16)


def total_of(ref):
    return sum(ref[z].astype(F32) for z in range(ref.shape[0]))


def step_into(outs, refs, gradient, rate, decay):
    master, first, second = (ref[...] for ref in refs)
    for ref, value in zip(outs, adamw_update(master, gradient, first, second, rate, decay)):
        ref[...] = value


def feed_step_body(io, ins, outs):
    io.need(*range(11))
    up, turned, out = unpack_groups(total_of(ins[0]), total_of(ins[1]))
    step_into(outs[0:3], ins[2:5], up, D ** (-0.5), MATRIX_DECAY)
    step_into(outs[3:6], ins[5:8], turned, FF ** (-0.5), MATRIX_DECAY)
    step_into(outs[6:9], ins[8:11], out, (D // 64) ** (-0.5), MATRIX_DECAY)


def project_step_body(io, ins, outs):
    io.need(*range(7))
    total = total_of(ins[0])
    step_into(outs[0:3], ins[1:4], total[:, :576], D ** (-0.5), MATRIX_DECAY)
    vector_grad = jnp.transpose(total[:, 512:640])[64:78]
    step_into(outs[3:6], ins[4:7], vector_grad, VECTOR_RATE, 0.0)
    outs[6][...] = vector_grad[8:9]


def place_body(io, info, ins, outs):
    io.need(0)
    for k in range(4):
        outs[0][pl.ds(info[FLIP + k] * IMGS, IMGS)] = ins[0][IMGS * k : IMGS * k + IMGS].astype(outs[0].dtype)


def swap_band(values, k):
    return lax.ppermute(values, "band", [(b, b ^ k) for b in range(lax.axis_size("band"))])


def swap_dp(values, k):
    return lax.ppermute(values, "dp", [(d, d ^ k) for d in range(lax.axis_size("dp"))])


def trade_columns(blocks):
    groups = [[2 * z + x for z in range(4)] for x in range(2)]
    return lax.all_to_all(blocks, "dp", split_axis=0, concat_axis=0, axis_index_groups=groups, tiled=True)


def gather_columns(shard):
    return trade_columns(jnp.broadcast_to(shard[None], (4, *shard.shape)))


def image_parts(values, mine):
    groups = values.reshape(4, IMGS, 64, D)
    return [lax.dynamic_index_in_dim(groups, mine ^ k, 0, keepdims=False) for k in range(4)]


def swap_images(parts):
    return [parts[0]] + [swap_band(parts[k], k) for k in (1, 2, 3)]


def pack_first(qkv, vectors):
    return jnp.concatenate([qkv, vectors, jnp.zeros((qkv.shape[0], W1 - 590), BF16)], axis=1)


def pack_group(up, turned, group):
    at = 128 * group
    pieces = (up[:, at : at + 128], up[:, at + 384 : at + 512], turned[:96, at : at + 128], turned[96:, at : at + 128])
    return jnp.concatenate(pieces, axis=1)


def pack_out(out):
    wide = jnp.concatenate([out[:32, :128], out[32:64, :128], out[64:, :128]], axis=1)
    thin = jnp.concatenate([out[:48, 128:], out[48:, 128:]], axis=1)
    return jnp.concatenate([jnp.concatenate([wide, jnp.zeros((16, 384), BF16)], axis=0), thin], axis=1)


def unpack_groups(head, rest):
    groups, last = [head[:96], head[96:], rest[:96]], rest[96:]
    up = jnp.concatenate([groups[s][:, 128 * e : 128 * e + 128] for e in range(2) for s in range(GROUPS)], axis=1)
    turned = jnp.concatenate(
        [
            jnp.concatenate([groups[s][:, 256 + 128 * e : 384 + 128 * e] for s in range(GROUPS)], axis=1)
            for e in range(2)
        ],
        axis=0,
    )
    wide = jnp.concatenate([last[:32, 128 * g : 128 * g + 128] for g in range(3)], axis=0)
    thin = jnp.concatenate([last[:, 384:448], last[:, 448:512]], axis=0)
    return up, turned, jnp.concatenate([wide, thin], axis=1)


def together(*values):
    return lax.optimization_barrier(values)


def gather_blocks_full(blocks):
    parts = [blocks, swap_band(blocks, 2)]
    return parts + [swap_band(part, 1) for part in parts]


def add(*terms):
    return sum(term.astype(F32) for term in terms).astype(BF16)


def start_swap(parts, *others):
    return together([swap_band(part, 1) for part in parts[4:6]], parts, *others)


def first_parts(parts, swapped):
    return [add(mine, other) for mine, other in zip(parts[0:2], swapped)]


def later_parts(parts, swapped, got):
    return [add(mine[1], other[1], new[1]) for mine, other, new in zip(parts[2:4], swapped, got)]


def near_sum(parts, swapped, got, got_last):
    terms = []
    for n in range(2):
        terms += [(parts[2 + n], 0), (swapped[n], 0), (got[n], 0), got_last[n]]
    low, high = parts[0].shape[2], parts[1].shape[2]
    return staged_call(near_body, [], terms, [sds((4, low + high, parts[0].shape[3]), BF16)], [], 1_000_000)[0]


def reduce_blocks_full(parts):
    swapped = [swap_band(part, 1) for part in parts[4:]]
    first = first_parts(parts, swapped[:2])
    kept = [add(mine, other) for mine, other in zip(parts[2:4], swapped[2:])]
    by_dp = jnp.concatenate([kept[0][:, None], first[0][:, None]], axis=1)
    by_band = jnp.concatenate([kept[1][None], first[1][None]], axis=0)
    full = jnp.concatenate([by_dp, by_band], axis=3)
    got = swap_band(full[1], 2)
    return add(full[0], got).reshape(8, *full.shape[3:])


def image_call(body, info, operands, outs, flops):
    def spec(shape):
        place = next(k for k, size in enumerate(shape) if size == IMGS)
        block = tuple(1 if k == place else size for k, size in enumerate(shape))
        return pl.BlockSpec(block, lambda m: tuple(m if k == place else 0 for k in range(len(shape))))

    moved = sum(v.size * v.dtype.itemsize for v in (*operands, *outs))
    return pl.pallas_call(
        body,
        grid=(IMGS,),
        out_shape=outs,
        in_specs=[pl.BlockSpec(memory_space=pltpu.SMEM)] + [spec(v.shape) for v in operands],
        out_specs=tuple(spec(v.shape) for v in outs),
        compiler_params=pltpu.CompilerParams(vmem_limit_bytes=58 * MIB),
        cost_estimate=pl.CostEstimate(flops=flops, bytes_accessed=moved, transcendentals=0),
    )(info, *operands)


def on_device(
    tokens, cotangent, image_rows, qkv_weight, out_weight, up_weight, down_weight, vectors,
    qkv_first, out_first, up_first, down_first, vector_first,
    qkv_second, out_second, up_second, down_second, vector_second,
):
    dp_mine = lax.axis_index("dp")
    mine = lax.axis_index("band")
    direct = lax.axis_size("dp") == 8
    numbers = lambda n: jnp.arange(n, dtype=jnp.int32)
    flip = numbers(4) ^ mine
    if direct:
        turn = numbers(8) ^ dp_mine
        place = turn % 2 * 4 + numbers(8) // 2
        first_place = turn % 2 * 4 + turn // 2
    else:
        place = first_place = numbers(8)
    limits = lax.dynamic_slice_in_dim(image_rows, mine * IMGS, IMGS)
    info = jnp.concatenate([flip % 2 * 2 + flip // 2, place, flip, limits, numbers(4), numbers(8), first_place]).astype(jnp.int32)
    if direct:
        (pack2,) = staged_call(
            pack_second_body, [], [up_weight, down_weight.T, out_weight], [sds((336, 512), BF16)], [], 1_000_000
        )
        pack2, qkv_first_use = together(pack2, qkv_weight)
        (pack1,) = staged_call(
            pack_first_body, [], [qkv_first_use, vectors.T], [sds((96, W1), BF16)], [], 1_000_000
        )
        near1 = [pack1] + [swap_dp(pack1, 2 * k) for k in (1, 2, 3)]
        x = image_parts(tokens, mine)
        x[2:4] = [swap_band(x[2], 2), swap_band(x[3], 3)]
        second = [lax.all_gather(pack2, ("band", "dp"), axis=0)]
        cot = image_parts(cotangent, mine)
        near1, cot, x = together(near1, cot, x)
        near1 = jnp.stack(near1)
        x[1] = swap_band(x[1], 1)
        across1, beside1, x = together(swap_dp(near1, 1), swap_band(near1, 2), x)
        corner1 = [swap_band(across1[:2], 2), swap_dp(beside1[2:], 1)]
        near1c, across1c, beside1c = [swap_band(part, 1) for part in (near1, across1, beside1)]
        corner1, near1c, across1c, beside1c = together(corner1, near1c, across1c, beside1c)
        corner1c, cot = together([swap_band(part, 1) for part in corner1], cot)
        first = [near1, across1, beside1, *corner1, near1c, across1c, beside1c, *corner1c]
        cot = swap_images(cot)
    else:
        low = [w.astype(BF16) for w in (qkv_weight, out_weight, up_weight, down_weight, vectors)]
        x = swap_images(image_parts(tokens, mine))
        cot = swap_images(image_parts(cotangent, mine))
        qkv_all, out_all, up_all, down_all, vec_all = [
            lax.all_gather(w, "dp", axis=0, tiled=True) for w in low
        ]
        cut = lambda v, n: [v[n * i : n * i + n] for i in range(8)]
        first = jnp.stack([pack_first(q, v) for q, v in zip(cut(qkv_all, 96), cut(vec_all, 96))])
        groups = [
            jnp.stack([pack_group(u, d.T, s) for u, d in zip(cut(up_all, 96), cut(down_all, 384))])
            for s in range(GROUPS)
        ]
        outs = jnp.stack([pack_out(o) for o in cut(out_all, 96)])
        first = gather_blocks_full(first)
        second = [lax.all_gather(jnp.concatenate([*groups, outs], axis=1), "band", axis=0, tiled=True)]

    rows_shape = (4, IMGS, 64, D)
    vmem = pltpu.VMEM
    piece = [sds((IMGS, 64, D), BF16)] * 4
    wide, wide32 = sds((R, D), BF16), sds((R, D), F32)
    table = sds((16, D), F32)
    qkv_shape = sds((4, 4, IMGS, 64, W1), BF16)
    qkv, vec = staged_call(
        project_body, [info], [x, first], [qkv_shape, table], [vmem((IMGS, SLOTS, D), F32)], 2_800_000_000
    )
    mixed, totals = image_call(
        attend_kernel, info, (qkv,), (sds(rows_shape, BF16), sds((IMGS, H, SLOTS), F32)), 3_000_000_000
    )
    group_scratch = [vmem((R, TILE), BF16) for _ in range(4)] + [vmem((32, 144, 512), BF16)]
    n2, gb, branch, out, br2, gn2, bias_head, grads1 = staged_call(
        feed_first_body, [info], [x, mixed, vec, cot],
        [wide, wide, wide32, wide, wide32, wide32, sds((1, 2 * TILE), F32), sds((32, 192, 512), BF16)],
        [vmem((32, 192, 512), BF16), vmem((32, 48, 512), BF16)]
        + group_scratch[:4] + [pltpu.SemaphoreType.DMA((2, 1))],
        17_000_000_000, second,
    )
    total1 = lax.psum_scatter(grads1, ("band", "dp") if direct else "band", scatter_dimension=0, tiled=True)
    fed = staged_call(
        feed_last_body, [info], [n2, gb, vec, br2, gn2, x, cot, mixed, branch, out],
        [piece, wide32, sds(rows_shape, BF16), table, sds((1, TILE), F32)],
        [vmem((32, 96, 512), BF16)]
        + group_scratch + [pltpu.SemaphoreType.DMA((1,)), pltpu.SemaphoreType.DMA((16,))],
        10_000_000_000, second, part_shapes(144, 512),
    )
    layer, grads2 = list(fed[:4]), list(fed[8:])
    middle_grad, mixed_grad, vec_grad, bias_rest = fed[4:8]
    home = lambda parts: [parts[0]] + [swap_band(parts[k], k) for k in (1, 2, 3)]
    if direct:
        others2, grads2, mixed_grad, layer = start_swap(grads2, mixed_grad, layer)
        sides2, mixed_grad = together(first_parts(grads2, others2), mixed_grad)
        got2 = [swap_dp(sides2[0], 1), swap_band(sides2[1], 2)]
        rest2 = [swap_band(part, 1) for part in grads2[6:]]
        layer[1:3] = [swap_band(layer[1], 1), swap_band(layer[2], 2)]
    (gq,) = image_call(attend_back_kernel, info, (qkv, totals, mixed_grad), (qkv_shape,), 6_000_000_000)
    if direct:
        gq, got2, rest2, layer = together(gq, got2, rest2, layer)
        last2, gq = together(later_parts(grads2, rest2, got2), gq)
        got_last2 = [swap_band(last2[0], 2), swap_dp(last2[1], 1)]
        layer[3] = swap_band(layer[3], 3)
    t0, t1, t2, t3, *grads3 = staged_call(
        project_back_body, [info], [x, vec, gq, first, vec_grad, bias_head, bias_rest, middle_grad],
        [piece], [vmem((R, D), BF16), vmem((32, 96, W1), BF16), pltpu.SemaphoreType.DMA((16,))], 5_600_000_000,
        [], part_shapes(96, W1),
    )
    token_grad = [t0, t1, t2, t3]
    place_call = lambda parts, dtype: staged_call(place_body, [info], [parts], [sds(tokens.shape, dtype)], [], 1_000_000)[0]
    states = [
        (up_weight, up_first, up_second), (down_weight.T, down_first.T, down_second.T),
        (out_weight, out_first, out_second), (qkv_weight, qkv_first, qkv_second),
        (vectors.T, vector_first.T, vector_second.T),
    ]
    like = lambda state: [sds(v.shape, F32) for v in state]
    if direct:
        got_last2, layer, grads3, token_grad = together(got_last2, layer, grads3, token_grad)
        others3, token_grad = together([swap_band(part, 1) for part in grads3[4:6]], token_grad)
        sides3 = first_parts(grads3, others3)
        got3 = [swap_dp(sides3[0], 1), swap_band(sides3[1], 2)]
        rest3 = [swap_band(part, 1) for part in grads3[6:]]
        near2 = near_sum(grads2, rest2, got2, got_last2)
        parts2 = trade_columns(near2)
        layer_out = place_call(layer, BF16)
        got3, rest3, near2, token_grad, layer_out = together(got3, rest3, near2, token_grad, layer_out)
        last3, token_grad = together(later_parts(grads3, rest3, got3), token_grad)
        got_last3 = [swap_band(last3[0], 2), swap_dp(last3[1], 1)]
        got_last3, token_grad = together(got_last3, token_grad)
        token_grad = home(token_grad)
        near3 = near_sum(grads3, rest3, got3, got_last3)
        near3, parts2 = together(near3, parts2)
        parts3 = trade_columns(near3)
        last = staged_call(
            project_step_body, [], [parts3] + [v for s in states[3:] for v in s],
            [v for s in states[3:] for v in like(s)] + [sds((1, 96), F32)], [], 10_000_000,
        )
        total1, last = together(total1, last)
        news = staged_call(
            feed_step_body, [], [total1, parts2] + [v for s in states[:3] for v in s],
            [v for s in states[:3] for v in like(s)], [], 20_000_000,
        )
        token_grad, news = together(token_grad, news)
        token_out = place_call(token_grad, F32)
        news = [news[0:3], [v.T for v in news[3:6]], news[6:9], last[0:3], [v.T for v in last[3:6]]]
        down_bias_gradient = last[6].reshape(-1)
    else:
        grads = [total1] + [reduce_blocks_full(part) for part in (grads2, grads3)]
        parts = [unpack_groups(grads[0][i], grads[1][i]) for i in range(8)]
        parts = [(up, turned.T, out) for up, turned, out in parts]
        full = [jnp.concatenate(p) for p in zip(*parts)] + [grads[2].reshape(D, W1)[:, :576], grads[2].reshape(D, W1)[:, 576:590]]
        full = [lax.psum_scatter(g.astype(F32), "dp", scatter_dimension=0, tiled=True) for g in full]
        states[1] = (down_weight, down_first, down_second)
        states[4] = (vectors, vector_first, vector_second)
        rates = (D ** (-0.5), FF ** (-0.5), (D // 64) ** (-0.5), D ** (-0.5), VECTOR_RATE)
        decays = (MATRIX_DECAY,) * 4 + (0.0,)
        news = [
            adamw_update(master, grad, one, two, rate, decay)
            for (master, one, two), grad, rate, decay in zip(states, full, rates, decays)
        ]
        down_bias_gradient = full[4][:, 8]
        layer_out, token_out = place_call(home(layer), BF16), place_call(home(token_grad), F32)
    order = [news[3], news[2], news[0], news[1], news[4]]
    return (
        (layer_out, token_out)
        + tuple(n[0] for n in order)
        + tuple(n[1] for n in order)
        + tuple(n[2] for n in order)
        + (down_bias_gradient,)
    )


def solution(mesh):
    rows, matrix, table = P("dp", "band", None), P("dp", "band"), P("dp", None)
    state = (matrix, matrix, matrix, matrix, table)
    return jax.shard_map(
        on_device,
        mesh=mesh,
        in_specs=(rows, rows, P("dp")) + state + state + state,
        out_specs=(rows, rows) + state + state + state + (P("dp"),),
        check_vma=False,
    )
```

```python
import math
from functools import partial

import jax
import jax.numpy as jnp
from jax import lax
from jax.experimental import pallas as pl
from jax.experimental.pallas import tpu as pltpu
from jax.sharding import PartitionSpec as P

D = 768
H = 12
HD = 64
FF = 3072
GRID = 16
STEP = 7
SLOTS = 256
NORM_EPS = 1e-06
ADAM_EPS = 1e-08
BETA_ONE = 0.5
BETA_TWO = 0.6
MATRIX_DECAY = 0.05
VECTOR_RATE = 0.5
MASK_FILL = -1e30
R = 768
IMGS = 3
W1 = 640
GROUPS = 3
TILE = FF // GROUPS
FLIP, LIMIT, SECOND, FIRST = 12, 16, 19, 31
F32 = jnp.float32
BF16 = jnp.bfloat16
MIB = 1024 * 1024


def adamw_update(master, gradient, moment_one, moment_two, step_rate, weight_decay):
    first_new = BETA_ONE * moment_one + (1.0 - BETA_ONE) * gradient
    second_new = BETA_TWO * moment_two + (1.0 - BETA_TWO) * gradient * gradient
    first_hat = first_new / (1.0 - BETA_ONE**STEP)
    second_hat = second_new / (1.0 - BETA_TWO**STEP)
    master_new = master - step_rate * (
        first_hat / (jnp.sqrt(second_hat) + ADAM_EPS) + weight_decay * master
    )
    return (master_new, first_new, second_new)


def dot(a, b):
    return lax.dot_general(a, b, (((1,), (0,)), ((), ())), preferred_element_type=F32)


def dot_nt(a, b):
    return lax.dot_general(a, b, (((1,), (1,)), ((), ())), preferred_element_type=F32)


def dot_tn(a, b):
    return lax.dot_general(a, b, (((0,), (0,)), ((), ())), preferred_element_type=F32)


def sds(shape, dtype):
    return jax.ShapeDtypeStruct(shape, dtype)


def as_list(value):
    return list(value) if isinstance(value, list) else [value]


class Staging:
    def __init__(self, ins, in_sems, outs, out_sems):
        self.waits = [[pltpu.make_async_copy(s, t, in_sems.at[n]) for s, t, n in group] for group in ins]
        self.puts = [[pltpu.make_async_copy(s, t, out_sems.at[n]) for s, t, n in group] for group in outs]
        self.waited, self.started, self.begun = set(), set(), False

    def begin(self):
        if not self.begun:
            self.begun = True
            for group in self.waits:
                for copy in group:
                    copy.start()

    def need(self, *which):
        self.begin()
        for k in which:
            if k not in self.waited:
                self.waited.add(k)
                for copy in self.waits[k]:
                    copy.wait()

    def put(self, *which):
        for k in which:
            if k not in self.started:
                self.started.add(k)
                for copy in self.puts[k]:
                    copy.start()

    def finish(self):
        self.need(*range(len(self.waits)))
        self.put(*range(len(self.puts)))
        for group in self.puts:
            for copy in group:
                copy.wait()


def staged_call(body, smem, operands, outs, scratch, flops, far=(), far_outs=()):
    given = [[v if isinstance(v, tuple) else (v, None) for v in as_list(group)] for group in operands]
    operands = given
    picks = [pick for group in operands for _, pick in group]
    operands = [[v if pick is None else sds(v.shape[1:], v.dtype) for v, pick in group] for group in operands]
    outs = [as_list(v) for v in outs]
    flat_in = [v for group in given for v, _ in group]
    flat_out = [v for group in outs for v in group]

    def buffer(group):
        return pltpu.VMEM((sum(v.shape[0] for v in group), *group[0].shape[1:]), group[0].dtype)

    def kernel(*refs):
        refs = list(refs)
        take = lambda n: [refs.pop(0) for _ in range(n)]
        info, sources, raw, targets, raw_out = [
            take(len(part)) for part in (smem, flat_in, far, flat_out, far_outs)
        ]
        sources = [ref if pick is None else ref.at[pick] for ref, pick in zip(sources, picks)]
        in_refs, out_refs, extra = take(len(operands)), take(len(outs)), take(len(scratch))
        in_sems, out_sems = refs

        def pairs(groups, far, near, outward):
            result, n = [], 0
            for group, ref in zip(groups, near):
                row, entry = 0, []
                for v in group:
                    part = ref if len(group) == 1 else ref.at[pl.ds(row, v.shape[0])]
                    entry.append((part, far[n], n) if outward else (far[n], part, n))
                    row, n = row + v.shape[0], n + 1
                result.append(entry)
            return result

        staging = Staging(
            pairs(operands, sources, in_refs, False), in_sems, pairs(outs, targets, out_refs, True), out_sems
        )
        body(staging, *info, *raw, *raw_out, in_refs, out_refs, *extra)
        staging.finish()

    moved = sum(v.size * v.dtype.itemsize for v in (*flat_in, *far, *flat_out, *far_outs))
    return pl.pallas_call(
        kernel,
        out_shape=(*flat_out, *far_outs),
        in_specs=[pl.BlockSpec(memory_space=pltpu.SMEM) for _ in smem]
        + [pl.BlockSpec(memory_space=pl.ANY) for _ in (*flat_in, *far)],
        out_specs=tuple(pl.BlockSpec(memory_space=pl.ANY) for _ in (*flat_out, *far_outs)),
        scratch_shapes=[buffer(g) for g in operands]
        + [buffer(g) for g in outs]
        + list(scratch)
        + [pltpu.SemaphoreType.DMA((len(flat_in),)), pltpu.SemaphoreType.DMA((len(flat_out),))],
        compiler_params=pltpu.CompilerParams(vmem_limit_bytes=58 * MIB),
        cost_estimate=pl.CostEstimate(flops=flops, bytes_accessed=moved, transcendentals=0),
    )(*smem, *flat_in, *far)


def first_rows(rows):
    return rows // 32 * 16


def part_shapes(rows, lanes):
    low = first_rows(rows)
    pair = [sds((2, 4, low, lanes), BF16), sds((2, 4, rows - low, lanes), BF16)]
    return pair + pair + pair + pair


def part_copies(grads, refs, sems):
    rows = grads.shape[1]
    low = first_rows(rows)
    copies = []
    for core in range(2):
        for first in (1, 0):
            by_dp, by_band = refs[core * 4 + (1 - first) * 2], refs[core * 4 + (1 - first) * 2 + 1]
            for n in range(2):
                at = core * 16 + n * 8 + first * 4
                copies.append((grads.at[pl.ds(at, 4), pl.ds(0, low)], by_dp.at[n]))
                at = core * 16 + first * 8 + n * 4
                copies.append((grads.at[pl.ds(at, 4), pl.ds(low, rows - low)], by_band.at[n]))
    return [pltpu.make_async_copy(source, target, sems.at[n]) for n, (source, target) in enumerate(copies)]


def norm_parts(values):
    center = values - jnp.mean(values, axis=-1, keepdims=True)
    spread = jnp.mean(center * center, axis=-1, keepdims=True)
    inverse = lax.rsqrt(spread + NORM_EPS)
    return center * inverse, inverse


def norm_back(gy, gain, xh, inverse):
    e = gy * gain
    return inverse * (
        e - jnp.mean(e, axis=-1, keepdims=True) - xh * jnp.mean(e * xh, axis=-1, keepdims=True)
    )


def column_sum(values):
    return jnp.sum(values, axis=0, keepdims=True)


def image_values(ref, m):
    return jnp.concatenate([ref[IMGS * k + m] for k in range(4)], axis=0)


def set_image(ref, m, values):
    for k in range(4):
        ref[IMGS * k + m] = values[64 * k : 64 * k + 64]


def valid_slots(info, m):
    columns = []
    for k in range(4):
        slot = lax.broadcasted_iota(jnp.int32, (64, 1), 0) + info[FLIP + k] * 64
        inside = ((slot >> 4) < info[LIMIT + m]) & ((slot & 15) < info[LIMIT + m])
        columns.append(inside.astype(F32))
    return jnp.concatenate(columns, axis=0)


def blocks_of(info):
    return lambda b, i: info[b] * 8 + info[4 + i]


def blocks_first(info):
    return lambda b, i: info[b] * 8 + info[FIRST + i]


def blocks_second(info):
    return lambda b, i: info[SECOND + b] * 8 + info[SECOND + 4 + i]


def joined(weights, block, b):
    return jnp.concatenate([weights[block(b, i)] for i in range(8)], axis=0)


def head_cut(ref, j):
    lane = (j % 9) * HD
    base = lane // 128 * 128
    tile = ref[j // 9, :, 0, :, base : base + 128].reshape(SLOTS, 128)
    return tile[:, lane - base : lane - base + HD]


def pack_first_body(io, ins, outs):
    io.need(0, 1)
    qkv, table = ins[0][...], ins[1][...]
    table = jnp.concatenate([table, jnp.zeros((50, table.shape[1]), F32)], axis=0)
    outs[0][:, 0:512] = qkv[:, 0:512].astype(BF16)
    outs[0][:, 512:640] = jnp.concatenate([qkv[:, 512:576], jnp.transpose(table)], axis=1).astype(BF16)


def pack_second_body(io, ins, outs):
    io.need(0, 1, 2)
    up, turned, out = (ref[...].astype(BF16) for ref in ins)
    for group in range(GROUPS):
        at, row = 128 * group, 96 * group
        pieces = (up[:, at : at + 128], up[:, at + 384 : at + 512], turned[:96, at : at + 128], turned[96:, at : at + 128])
        for n, piece in enumerate(pieces):
            outs[0][row : row + 96, 128 * n : 128 * n + 128] = piece
    outs[0][288:336, :] = pack_out(out)


def project_body(io, info, ins, outs, n1):
    x, weights = ins
    qkv, table = outs
    block = blocks_first(info)
    io.need(0)
    for m in range(IMGS):
        n1[m], _ = norm_parts(image_values(x, m).astype(F32))
    io.need(1)
    tail = jnp.concatenate([weights[block(0, i), :, 512:640] for i in range(8)], axis=0)
    vec = jnp.transpose(tail.astype(F32))[64:80]
    table[...] = vec
    bias = jnp.concatenate(
        [vec[2:3], jnp.zeros((1, D), F32), vec[3:4], jnp.zeros((1, 64), F32)], axis=1
    )
    normed = [(n1[m] * vec[0:1] + vec[1:2]).astype(BF16) for m in range(IMGS)]
    for b in range(4):
        w = joined(weights, block, b)
        for m in range(IMGS):
            part = dot(normed[m], w) + bias[:, 576 * b : 576 * b + W1]
            qkv[b, :, m] = part.astype(BF16).reshape(4, 64, W1)


def attend_kernel(info, qkv, mixed, total):
    column = (valid_slots(info, pl.program_id(0)) - 1.0) * -MASK_FILL
    for pair in range(H // 2):
        halves = []
        for h in (2 * pair, 2 * pair + 1):
            q = head_cut(qkv, h) * BF16(HD**-0.5)
            k = head_cut(qkv, H + h)
            v = head_cut(qkv, 2 * H + h)
            scores = dot_nt(k, q) + column
            highest = jnp.max(scores, axis=0, keepdims=True)
            shifted = jnp.exp(scores - highest)
            totals = column_sum(shifted)
            low = (shifted * (1.0 / totals)).astype(BF16)
            total[0, h : h + 1, :] = highest + jnp.log(totals)
            halves.append(dot_tn(v, low))
        both = jnp.transpose(jnp.concatenate(halves, axis=0))
        mixed[:, 0, :, 128 * pair : 128 * pair + 128] = both.astype(BF16).reshape(4, 64, 128)


def gelu_parts(v):
    cdf = 0.5 * (1.0 + lax.erf(v * (0.5**0.5)))
    pdf = jnp.exp(v * v * -0.5) * ((2.0 * math.pi) ** -0.5)
    return v * cdf, cdf + v * pdf


def spread_group(weights, row, block, up, down):
    for b in range(4):
        for i in range(8):
            piece = weights[block(b, i), row : row + 96]
            up[96 * i : 96 * i + 96, 256 * b : 256 * b + 256] = piece[:, 0:256]
            for e in range(2):
                down[192 * b + 96 * e : 192 * b + 96 * e + 96, 128 * i : 128 * i + 128] = piece[
                    :, 256 + 128 * e : 384 + 128 * e
                ]


def feed_group(
    group, vec, n2, gb, up, down, act, gh, br2, gn2, bias_grad, lane, grads, row, block, before=None, after=None
):
    up_bias = jnp.concatenate(
        [
            vec[10 + i // 2 : 11 + i // 2, 384 * (i % 2) + 128 * group : 384 * (i % 2) + 128 * group + 128]
            for i in range(8)
        ],
        axis=1,
    )
    bias_sum = jnp.zeros((1, TILE), F32)
    for m in range(IMGS):
        rows = slice(m * SLOTS, m * SLOTS + SLOTS)
        active, slope = gelu_parts(dot(n2[rows], up[...]) + up_bias)
        act[rows] = active.astype(BF16)
        low = (dot(gb[rows], down[...]) * slope).astype(BF16)
        gh[rows] = low
        bias_sum += column_sum(low.astype(F32))
    bias_grad[:, lane : lane + TILE] = bias_sum
    if before:
        before()
    for m in range(IMGS):
        rows = slice(m * SLOTS, m * SLOTS + SLOTS)
        new = dot_nt(act[rows], down[...])
        br2[rows] = new if group == 0 else br2[rows] + new
        new = dot_nt(gh[rows], up[...])
        gn2[rows] = new if group == 0 else gn2[rows] + new
    if after:
        after()
    at = slice(row, row + 96)
    up_grad = dot_tn(n2[...], gh[...]).astype(BF16)
    for b in range(4):
        for i in range(8):
            grads[block(b, i), at, 0:256] = up_grad[96 * i : 96 * i + 96, 256 * b : 256 * b + 256]
    down_grad = dot_tn(gb[...], act[...]).astype(BF16)
    for b in range(4):
        for i in range(8):
            for e in range(2):
                grads[block(b, i), at, 256 + 128 * e : 384 + 128 * e] = down_grad[
                    192 * b + 96 * e : 192 * b + 96 * e + 96, 128 * i : 128 * i + 128
                ]


def store_parts(grads, targets, sems):
    puts = part_copies(grads, targets, sems)
    for put in puts:
        put.start()
    return puts


def load_rows(sources, row, rows, target, sems):
    copies, at = [], 0
    for n, ref in enumerate(sources):
        size = ref.shape[0]
        copies.append(pltpu.make_async_copy(ref.at[:, pl.ds(row, rows)], target.at[pl.ds(at, size)], sems.at[n]))
        at += size
    for copy in copies:
        copy.start()
    return copies


def feed_first_body(io, info, second, ins, outs, groups, tails, up, down, act, gh, sems):
    x, mixed, table, cot = ins
    n2, gb, branch_ref, out, br2, gn2, bias_grad, grads = outs
    second_block = blocks_second(info)
    small = load_rows([second], 288, 48, tails, sems.at[0])
    io.begin()
    large = load_rows([second], 0, 192, groups, sems.at[1])
    for copy in small:
        copy.wait()
    for b in range(4):
        for i in range(8):
            wide = tails[second_block(b, i), 0:32, 0:384]
            thin = tails[second_block(b, i), :, 384:512]
            for g in range(3):
                out[96 * i + 32 * g : 96 * i + 32 * g + 32, 192 * b : 192 * b + 128] = wide[:, 128 * g : 128 * g + 128]
            for g in range(2):
                out[96 * i + 48 * g : 96 * i + 48 * g + 48, 192 * b + 128 : 192 * b + 192] = thin[:, 64 * g : 64 * g + 64]
    io.need(0, 1, 2, 3)
    vec = table[...]
    for m in range(IMGS):
        rows = slice(m * SLOTS, m * SLOTS + SLOTS)
        branch = dot(mixed[:, m].reshape(SLOTS, D), out[...]) + vec[4:5]
        branch_ref[rows] = branch
        xh, _ = norm_parts(image_values(x, m).astype(F32) + vec[5:6] * branch)
        n2[rows] = (xh * vec[6:7] + vec[7:8]).astype(BF16)
        back = image_values(cot, m).astype(F32) * valid_slots(info, m)
        gb[rows] = (back * vec[9:10]).astype(BF16)
    io.put(0, 1, 2, 3)
    for copy in large:
        copy.wait()
    for group in range(2):
        spread_group(groups, 96 * group, second_block, up, down)
        feed_group(
            group, table, n2, gb, up, down, act, gh, br2, gn2, bias_grad, TILE * group, grads, 96 * group,
            lambda b, i: b * 8 + i, None, (lambda: io.put(4, 5)) if group else None,
        )


def feed_last_body(io, info, second, *refs):
    *targets, ins, outs, groups, up, down, act, gh, grads, sems, put_sems = refs
    n2, gb, table, br2, gn2, x, cot, mixed, branch_ref, out = ins
    layer, middle_grad, mixed_grad, vec_grad, bias_grad = outs
    block, second_block = blocks_of(info), blocks_second(info)
    large = load_rows([second], 192, 96, groups, sems)
    io.begin()
    for copy in large:
        copy.wait()
    spread_group(groups, 0, second_block, up, down)
    io.need(0, 1, 2)
    feed_group(
        2, table, n2, gb, up, down, act, gh, br2, gn2, bias_grad, 0, grads, 0, block, lambda: io.need(3, 4)
    )
    io.need(5, 6, 7, 8, 9)
    vec = table[...]
    sums = [jnp.zeros((1, D), F32) for _ in range(10)]
    for m in range(IMGS):
        rows = slice(m * SLOTS, m * SLOTS + SLOTS)
        valid = valid_slots(info, m)
        back = image_values(cot, m).astype(F32) * valid
        branch = branch_ref[rows]
        middle = image_values(x, m).astype(F32) + vec[5:6] * branch
        xh, inverse = norm_parts(middle)
        branch_two = br2[rows] + vec[8:9]
        set_image(layer, m, ((middle + vec[9:10] * branch_two) * valid).astype(BF16))
        sums[9] += column_sum(back * branch_two)
        sums[8] += column_sum(gb[rows].astype(F32))
        gy = gn2[rows]
        sums[6] += column_sum(gy * xh)
        sums[7] += column_sum(gy)
        grad = norm_back(gy, vec[6:7], xh, inverse) + back
        middle_grad[rows] = grad
        sums[5] += column_sum(grad * branch)
        low = (grad * vec[5:6]).astype(BF16)
        sums[4] += column_sum(low.astype(F32))
        gh[rows, :D] = low
        mixed_grad[:, m] = dot_nt(low, out[...]).astype(BF16).reshape(4, 64, D)
        act[rows, :D] = mixed[:, m].reshape(SLOTS, D)
    for k in range(10):
        vec_grad[k : k + 1] = sums[k]
    vec_grad[10:16] = jnp.zeros((6, D), F32)
    io.put(0, 1, 2, 3, 4)
    out_grad = dot_tn(act[:, :D], gh[:, :D]).astype(BF16)
    for b in range(4):
        for i in range(8):
            piece = out_grad[96 * i : 96 * i + 96, 192 * b : 192 * b + 192]
            at = block(b, i)
            for g in range(3):
                grads[at, 96:128, 128 * g : 128 * g + 128] = piece[32 * g : 32 * g + 32, 0:128]
            grads[at, 128:144, 0:384] = jnp.zeros((16, 384), BF16)
            grads[at, 96:144, 384:512] = jnp.concatenate([piece[0:48, 128:192], piece[48:96, 128:192]], axis=1)
    for put in store_parts(grads, targets, put_sems):
        put.wait()


def attend_back_kernel(info, qkv, total, mixed_grad, gq):
    column = (valid_slots(info, pl.program_id(0)) - 1.0) * -MASK_FILL
    for b in range(4):
        gq[b, :, 0, :, 512:640] = jnp.zeros((4, 64, 128), BF16)
    for h in range(H):
        q = head_cut(qkv, h) * BF16(HD**-0.5)
        k = head_cut(qkv, H + h)
        v = head_cut(qkv, 2 * H + h)
        base = h // 2 * 128
        tile = mixed_grad[:, 0, :, base : base + 128].reshape(SLOTS, 128)
        grad_out = tile[:, h % 2 * HD : h % 2 * HD + HD]
        scores = dot_nt(k, q) + column
        again = jnp.exp(scores - total[0, h : h + 1, :])
        grad_weights = dot_nt(v, grad_out)
        center = column_sum(again * grad_weights)
        grad_scores = (again * (grad_weights - center)).astype(BF16)
        parts = (
            jnp.transpose(dot_tn(k, grad_scores)) * (HD**-0.5),
            dot(grad_scores, q),
            dot(again.astype(BF16), grad_out),
        )
        for j, part in zip((h, H + h, 2 * H + h), parts):
            lane = (j % 9) * HD
            gq[j // 9, :, 0, :, lane : lane + HD] = part.astype(BF16).reshape(4, 64, HD)


def project_back_body(io, info, *refs):
    *targets, ins, outs, n1, grads, put_sems = refs
    x, table, gq, weights, vec_in, bias_head, bias_rest, middle_grad = ins
    (token_grad,) = outs
    block = blocks_of(info)
    io.need(0, 1)
    vec = table[...]
    for m in range(IMGS):
        xh, _ = norm_parts(image_values(x, m).astype(F32))
        n1[m * SLOTS : m * SLOTS + SLOTS] = (xh * vec[0:1] + vec[1:2]).astype(BF16)
    io.need(2, 3)
    gy = [jnp.zeros((SLOTS, D), F32) for _ in range(IMGS)]
    for b in range(4):
        w = joined(weights, blocks_first(info), b)
        for m in range(IMGS):
            gy[m] += dot_nt(gq[b, :, m].reshape(SLOTS, W1), w)
    io.need(4, 5, 6, 7)
    bias = jnp.concatenate([bias_head[...], bias_rest[...]], axis=1)
    gain_sum, shift_sum = jnp.zeros((1, D), F32), jnp.zeros((1, D), F32)
    for m in range(IMGS):
        rows = slice(m * SLOTS, m * SLOTS + SLOTS)
        xh, inverse = norm_parts(image_values(x, m).astype(F32))
        gain_sum += column_sum(gy[m] * xh)
        shift_sum += column_sum(gy[m])
        grad = norm_back(gy[m], vec[0:1], xh, inverse) + middle_grad[rows]
        set_image(token_grad, m, grad.astype(BF16))
    io.put(0)
    col = []
    for b in range(4):
        total = jnp.zeros((1, W1), F32)
        for m in range(IMGS):
            total += column_sum(gq[b, :, m].reshape(SLOTS, W1).astype(F32))
        col.append(total[:, :576])
    flat = jnp.concatenate(col, axis=1)
    up_rows = [
        jnp.concatenate(
            [bias[:, TILE * s + 128 * i : TILE * s + 128 * i + 128] for i in (2 * k, 2 * k + 1) for s in range(GROUPS)],
            axis=1,
        )
        for k in range(4)
    ]
    rows = [jnp.zeros((64, D), F32), gain_sum, shift_sum, flat[:, :D], flat[:, 2 * D :], vec_in[4:10]]
    tail = jnp.transpose(jnp.concatenate(rows + up_rows + [jnp.zeros((50, D), F32)], axis=0))
    for b in range(4):
        grad_rows = jnp.concatenate([gq[b, :, m].reshape(SLOTS, W1) for m in range(IMGS)], axis=0)
        grad = dot_tn(n1[...], grad_rows)
        last = (grad[:, 512:640] + tail).astype(BF16)
        grad = grad.astype(BF16)
        for i in range(8):
            at = block(b, i)
            grads[at, :, 0:512] = grad[96 * i : 96 * i + 96, 0:512]
            grads[at, :, 512:640] = last[96 * i : 96 * i + 96]
    puts = part_copies(grads, targets, put_sems)
    for put in puts:
        put.start()
    for put in puts:
        put.wait()


def near_body(io, ins, outs):
    low = ins[0].shape[1]
    for s in range(2):
        terms = ins[4 * s : 4 * s + 4]
        io.need(*range(4 * s, 4 * s + 4))
        rows = slice(low, None) if s else slice(0, low)
        for z in range(4):
            outs[0][z, rows] = sum(term[z].astype(F32) for term in terms).astype(BF16)


def total_of(ref):
    return sum(ref[z].astype(F32) for z in range(ref.shape[0]))


def step_into(outs, refs, gradient, rate, decay):
    master, first, second = (ref[...] for ref in refs)
    for ref, value in zip(outs, adamw_update(master, gradient, first, second, rate, decay)):
        ref[...] = value


def final_body(io, info, ins, outs):
    total1, parts2, parts3, tokens = ins[0:4]
    io.need(3)
    for k in range(4):
        outs[0][pl.ds(info[FLIP + k] * IMGS, IMGS)] = tokens[IMGS * k : IMGS * k + IMGS].astype(F32)
    io.put(0)
    io.need(2, *range(13, 19))
    total = total_of(parts3)
    step_into(outs[1:4], ins[13:16], total[:, :576], D ** (-0.5), MATRIX_DECAY)
    vector_grad = jnp.transpose(total[:, 512:640])[64:78]
    step_into(outs[4:7], ins[16:19], vector_grad, VECTOR_RATE, 0.0)
    outs[7][...] = vector_grad[8:9]
    io.put(1, 2, 3, 4, 5, 6, 7)
    io.need(*range(19))
    up, turned, out = unpack_groups(total1[0].astype(F32), total_of(parts2))
    step_into(outs[8:11], ins[4:7], up, D ** (-0.5), MATRIX_DECAY)
    io.put(8, 9, 10)
    step_into(outs[11:14], ins[7:10], turned, FF ** (-0.5), MATRIX_DECAY)
    io.put(11, 12, 13)
    step_into(outs[14:17], ins[10:13], out, (D // 64) ** (-0.5), MATRIX_DECAY)


def place_body(io, info, ins, outs):
    io.need(0)
    for k in range(4):
        outs[0][pl.ds(info[FLIP + k] * IMGS, IMGS)] = ins[0][IMGS * k : IMGS * k + IMGS].astype(outs[0].dtype)


def swap_band(values, k):
    return lax.ppermute(values, "band", [(b, b ^ k) for b in range(lax.axis_size("band"))])


def swap_dp(values, k):
    return lax.ppermute(values, "dp", [(d, d ^ k) for d in range(lax.axis_size("dp"))])


def trade_columns(blocks):
    groups = [[2 * z + x for z in range(4)] for x in range(2)]
    return lax.all_to_all(blocks, "dp", split_axis=0, concat_axis=0, axis_index_groups=groups, tiled=True)


def gather_columns(shard):
    return trade_columns(jnp.broadcast_to(shard[None], (4, *shard.shape)))


def image_parts(values, mine):
    groups = values.reshape(4, IMGS, 64, D)
    return [lax.dynamic_index_in_dim(groups, mine ^ k, 0, keepdims=False) for k in range(4)]


def swap_images(parts):
    return [parts[0]] + [swap_band(parts[k], k) for k in (1, 2, 3)]


def pack_first(qkv, vectors):
    return jnp.concatenate([qkv, vectors, jnp.zeros((qkv.shape[0], W1 - 590), BF16)], axis=1)


def pack_group(up, turned, group):
    at = 128 * group
    pieces = (up[:, at : at + 128], up[:, at + 384 : at + 512], turned[:96, at : at + 128], turned[96:, at : at + 128])
    return jnp.concatenate(pieces, axis=1)


def pack_out(out):
    wide = jnp.concatenate([out[:32, :128], out[32:64, :128], out[64:, :128]], axis=1)
    thin = jnp.concatenate([out[:48, 128:], out[48:, 128:]], axis=1)
    return jnp.concatenate([jnp.concatenate([wide, jnp.zeros((16, 384), BF16)], axis=0), thin], axis=1)


def unpack_groups(head, rest):
    groups, last = [head[:96], head[96:], rest[:96]], rest[96:]
    up = jnp.concatenate([groups[s][:, 128 * e : 128 * e + 128] for e in range(2) for s in range(GROUPS)], axis=1)
    turned = jnp.concatenate(
        [
            jnp.concatenate([groups[s][:, 256 + 128 * e : 384 + 128 * e] for s in range(GROUPS)], axis=1)
            for e in range(2)
        ],
        axis=0,
    )
    wide = jnp.concatenate([last[:32, 128 * g : 128 * g + 128] for g in range(3)], axis=0)
    thin = jnp.concatenate([last[:, 384:448], last[:, 448:512]], axis=0)
    return up, turned, jnp.concatenate([wide, thin], axis=1)


def together(*values):
    return lax.optimization_barrier(values)


def gather_blocks_full(blocks):
    parts = [blocks, swap_band(blocks, 2)]
    return parts + [swap_band(part, 1) for part in parts]


def add(*terms):
    return sum(term.astype(F32) for term in terms).astype(BF16)


def start_swap(parts, *others):
    return together([swap_band(part, 1) for part in parts[4:6]], parts, *others)


def first_parts(parts, swapped):
    return [add(mine, other) for mine, other in zip(parts[0:2], swapped)]


def later_parts(parts, swapped, got):
    return [add(mine[1], other[1], new[1]) for mine, other, new in zip(parts[2:4], swapped, got)]


def near_sum(parts, swapped, got, got_last):
    terms = []
    for n in range(2):
        terms += [(parts[2 + n], 0), (swapped[n], 0), (got[n], 0), got_last[n]]
    low, high = parts[0].shape[2], parts[1].shape[2]
    return staged_call(near_body, [], terms, [sds((4, low + high, parts[0].shape[3]), BF16)], [], 1_000_000)[0]


def reduce_blocks_full(parts):
    swapped = [swap_band(part, 1) for part in parts[4:]]
    first = first_parts(parts, swapped[:2])
    kept = [add(mine, other) for mine, other in zip(parts[2:4], swapped[2:])]
    by_dp = jnp.concatenate([kept[0][:, None], first[0][:, None]], axis=1)
    by_band = jnp.concatenate([kept[1][None], first[1][None]], axis=0)
    full = jnp.concatenate([by_dp, by_band], axis=3)
    got = swap_band(full[1], 2)
    return add(full[0], got).reshape(8, *full.shape[3:])


def image_call(body, info, operands, outs, flops):
    def spec(shape):
        place = next(k for k, size in enumerate(shape) if size == IMGS)
        block = tuple(1 if k == place else size for k, size in enumerate(shape))
        return pl.BlockSpec(block, lambda m: tuple(m if k == place else 0 for k in range(len(shape))))

    moved = sum(v.size * v.dtype.itemsize for v in (*operands, *outs))
    return pl.pallas_call(
        body,
        grid=(IMGS,),
        out_shape=outs,
        in_specs=[pl.BlockSpec(memory_space=pltpu.SMEM)] + [spec(v.shape) for v in operands],
        out_specs=tuple(spec(v.shape) for v in outs),
        compiler_params=pltpu.CompilerParams(vmem_limit_bytes=58 * MIB),
        cost_estimate=pl.CostEstimate(flops=flops, bytes_accessed=moved, transcendentals=0),
    )(info, *operands)


def on_device(
    tokens, cotangent, image_rows, qkv_weight, out_weight, up_weight, down_weight, vectors,
    qkv_first, out_first, up_first, down_first, vector_first,
    qkv_second, out_second, up_second, down_second, vector_second,
):
    dp_mine = lax.axis_index("dp")
    mine = lax.axis_index("band")
    direct = lax.axis_size("dp") == 8
    numbers = lambda n: jnp.arange(n, dtype=jnp.int32)
    flip = numbers(4) ^ mine
    if direct:
        turn = numbers(8) ^ dp_mine
        place = turn % 2 * 4 + numbers(8) // 2
        first_place = turn % 2 * 4 + turn // 2
    else:
        place = first_place = numbers(8)
    limits = lax.dynamic_slice_in_dim(image_rows, mine * IMGS, IMGS)
    info = jnp.concatenate([flip % 2 * 2 + flip // 2, place, flip, limits, numbers(4), numbers(8), first_place]).astype(jnp.int32)
    if direct:
        (pack2,) = staged_call(
            pack_second_body, [], [up_weight, down_weight.T, out_weight], [sds((336, 512), BF16)], [], 1_000_000
        )
        pack2, qkv_first_use = together(pack2, qkv_weight)
        (pack1,) = staged_call(
            pack_first_body, [], [qkv_first_use, vectors.T], [sds((96, W1), BF16)], [], 1_000_000
        )
        near1 = [pack1] + [swap_dp(pack1, 2 * k) for k in (1, 2, 3)]
        x = image_parts(tokens, mine)
        x[2:4] = [swap_band(x[2], 2), swap_band(x[3], 3)]
        second = [lax.all_gather(pack2, ("band", "dp"), axis=0)]
        cot = image_parts(cotangent, mine)
        near1, cot, x = together(near1, cot, x)
        near1 = jnp.stack(near1)
        x[1] = swap_band(x[1], 1)
        across1, beside1, x = together(swap_dp(near1, 1), swap_band(near1, 2), x)
        corner1 = [swap_band(across1[:2], 2), swap_dp(beside1[2:], 1)]
        near1c, across1c, beside1c = [swap_band(part, 1) for part in (near1, across1, beside1)]
        corner1, near1c, across1c, beside1c = together(corner1, near1c, across1c, beside1c)
        corner1c, cot = together([swap_band(part, 1) for part in corner1], cot)
        first = [near1, across1, beside1, *corner1, near1c, across1c, beside1c, *corner1c]
        cot = swap_images(cot)
    else:
        low = [w.astype(BF16) for w in (qkv_weight, out_weight, up_weight, down_weight, vectors)]
        x = swap_images(image_parts(tokens, mine))
        cot = swap_images(image_parts(cotangent, mine))
        qkv_all, out_all, up_all, down_all, vec_all = [
            lax.all_gather(w, "dp", axis=0, tiled=True) for w in low
        ]
        cut = lambda v, n: [v[n * i : n * i + n] for i in range(8)]
        first = jnp.stack([pack_first(q, v) for q, v in zip(cut(qkv_all, 96), cut(vec_all, 96))])
        groups = [
            jnp.stack([pack_group(u, d.T, s) for u, d in zip(cut(up_all, 96), cut(down_all, 384))])
            for s in range(GROUPS)
        ]
        outs = jnp.stack([pack_out(o) for o in cut(out_all, 96)])
        first = gather_blocks_full(first)
        second = [lax.all_gather(jnp.concatenate([*groups, outs], axis=1), "band", axis=0, tiled=True)]

    rows_shape = (4, IMGS, 64, D)
    vmem = pltpu.VMEM
    piece = [sds((IMGS, 64, D), BF16)] * 4
    wide, wide32 = sds((R, D), BF16), sds((R, D), F32)
    table = sds((16, D), F32)
    qkv_shape = sds((4, 4, IMGS, 64, W1), BF16)
    qkv, vec = staged_call(
        project_body, [info], [x, first], [qkv_shape, table], [vmem((IMGS, SLOTS, D), F32)], 2_800_000_000
    )
    mixed, totals = image_call(
        attend_kernel, info, (qkv,), (sds(rows_shape, BF16), sds((IMGS, H, SLOTS), F32)), 3_000_000_000
    )
    group_scratch = [vmem((R, TILE), BF16) for _ in range(4)] + [vmem((32, 144, 512), BF16)]
    n2, gb, branch, out, br2, gn2, bias_head, grads1 = staged_call(
        feed_first_body, [info], [x, mixed, vec, cot],
        [wide, wide, wide32, wide, wide32, wide32, sds((1, 2 * TILE), F32), sds((32, 192, 512), BF16)],
        [vmem((32, 192, 512), BF16), vmem((32, 48, 512), BF16)]
        + group_scratch[:4] + [pltpu.SemaphoreType.DMA((2, 1))],
        17_000_000_000, second,
    )
    total1 = lax.psum_scatter(grads1, ("band", "dp") if direct else "band", scatter_dimension=0, tiled=True)
    fed = staged_call(
        feed_last_body, [info], [n2, gb, vec, br2, gn2, x, cot, mixed, branch, out],
        [piece, wide32, sds(rows_shape, BF16), table, sds((1, TILE), F32)],
        [vmem((32, 96, 512), BF16)]
        + group_scratch + [pltpu.SemaphoreType.DMA((1,)), pltpu.SemaphoreType.DMA((16,))],
        10_000_000_000, second, part_shapes(144, 512),
    )
    layer, grads2 = list(fed[:4]), list(fed[8:])
    middle_grad, mixed_grad, vec_grad, bias_rest = fed[4:8]
    home = lambda parts: [parts[0]] + [swap_band(parts[k], k) for k in (1, 2, 3)]
    if direct:
        others2, grads2, mixed_grad, layer = start_swap(grads2, mixed_grad, layer)
        sides2, mixed_grad = together(first_parts(grads2, others2), mixed_grad)
        got2 = [swap_dp(sides2[0], 1), swap_band(sides2[1], 2)]
        rest2 = [swap_band(part, 1) for part in grads2[6:]]
        layer[1:3] = [swap_band(layer[1], 1), swap_band(layer[2], 2)]
    (gq,) = image_call(attend_back_kernel, info, (qkv, totals, mixed_grad), (qkv_shape,), 6_000_000_000)
    if direct:
        gq, got2, rest2, layer = together(gq, got2, rest2, layer)
        last2, gq = together(later_parts(grads2, rest2, got2), gq)
        got_last2 = [swap_band(last2[0], 2), swap_dp(last2[1], 1)]
        layer[3] = swap_band(layer[3], 3)
    t0, t1, t2, t3, *grads3 = staged_call(
        project_back_body, [info], [x, vec, gq, first, vec_grad, bias_head, bias_rest, middle_grad],
        [piece], [vmem((R, D), BF16), vmem((32, 96, W1), BF16), pltpu.SemaphoreType.DMA((16,))], 5_600_000_000,
        [], part_shapes(96, W1),
    )
    token_grad = [t0, t1, t2, t3]
    place_call = lambda parts, dtype: staged_call(place_body, [info], [parts], [sds(tokens.shape, dtype)], [], 1_000_000)[0]
    states = [
        (up_weight, up_first, up_second), (down_weight.T, down_first.T, down_second.T),
        (out_weight, out_first, out_second), (qkv_weight, qkv_first, qkv_second),
        (vectors.T, vector_first.T, vector_second.T),
    ]
    like = lambda state: [sds(v.shape, F32) for v in state]
    if direct:
        got_last2, layer, grads3, token_grad = together(got_last2, layer, grads3, token_grad)
        others3, token_grad = together([swap_band(part, 1) for part in grads3[4:6]], token_grad)
        sides3 = first_parts(grads3, others3)
        got3 = [swap_dp(sides3[0], 1), swap_band(sides3[1], 2)]
        rest3 = [swap_band(part, 1) for part in grads3[6:]]
        near2 = near_sum(grads2, rest2, got2, got_last2)
        parts2 = trade_columns(near2)
        layer_out = place_call(layer, BF16)
        got3, rest3, near2, token_grad, layer_out = together(got3, rest3, near2, token_grad, layer_out)
        last3, token_grad = together(later_parts(grads3, rest3, got3), token_grad)
        got_last3 = [swap_band(last3[0], 2), swap_dp(last3[1], 1)]
        got_last3, token_grad = together(got_last3, token_grad)
        token_grad = home(token_grad)
        near3 = near_sum(grads3, rest3, got3, got_last3)
        near3, parts2 = together(near3, parts2)
        parts3 = trade_columns(near3)
        token_out, *news = staged_call(
            final_body, [info], [total1, parts2, parts3, token_grad] + [v for s in states for v in s],
            [sds(tokens.shape, F32)] + [v for s in states[3:] for v in like(s)] + [sds((1, 96), F32)]
            + [v for s in states[:3] for v in like(s)], [], 20_000_000,
        )
        down_bias_gradient = news[6].reshape(-1)
        news = [news[7:10], [v.T for v in news[10:13]], news[13:16], news[0:3], [v.T for v in news[3:6]]]
    else:
        grads = [total1] + [reduce_blocks_full(part) for part in (grads2, grads3)]
        parts = [unpack_groups(grads[0][i], grads[1][i]) for i in range(8)]
        parts = [(up, turned.T, out) for up, turned, out in parts]
        full = [jnp.concatenate(p) for p in zip(*parts)] + [grads[2].reshape(D, W1)[:, :576], grads[2].reshape(D, W1)[:, 576:590]]
        full = [lax.psum_scatter(g.astype(F32), "dp", scatter_dimension=0, tiled=True) for g in full]
        states[1] = (down_weight, down_first, down_second)
        states[4] = (vectors, vector_first, vector_second)
        rates = (D ** (-0.5), FF ** (-0.5), (D // 64) ** (-0.5), D ** (-0.5), VECTOR_RATE)
        decays = (MATRIX_DECAY,) * 4 + (0.0,)
        news = [
            adamw_update(master, grad, one, two, rate, decay)
            for (master, one, two), grad, rate, decay in zip(states, full, rates, decays)
        ]
        down_bias_gradient = full[4][:, 8]
        layer_out, token_out = place_call(home(layer), BF16), place_call(home(token_grad), F32)
    order = [news[3], news[2], news[0], news[1], news[4]]
    return (
        (layer_out, token_out)
        + tuple(n[0] for n in order)
        + tuple(n[1] for n in order)
        + tuple(n[2] for n in order)
        + (down_bias_gradient,)
    )


def solution(mesh):
    rows, matrix, table = P("dp", "band", None), P("dp", "band"), P("dp", None)
    state = (matrix, matrix, matrix, matrix, table)
    return jax.shard_map(
        on_device,
        mesh=mesh,
        in_specs=(rows, rows, P("dp")) + state + state + state,
        out_specs=(rows, rows) + state + state + state + (P("dp"),),
        check_vma=False,
    )
```

```python
import math
from functools import partial

import jax
import jax.numpy as jnp
from jax import lax
from jax.experimental import pallas as pl
from jax.experimental.pallas import tpu as pltpu
from jax.sharding import PartitionSpec as P

D = 768
H = 12
HD = 64
FF = 3072
GRID = 16
STEP = 7
SLOTS = 256
NORM_EPS = 1e-06
ADAM_EPS = 1e-08
BETA_ONE = 0.5
BETA_TWO = 0.6
MATRIX_DECAY = 0.05
VECTOR_RATE = 0.5
MASK_FILL = -1e30
R = 768
IMGS = 3
W1 = 640
GROUPS = 3
TILE = FF // GROUPS
FLIP, LIMIT, SECOND, FIRST = 12, 16, 19, 31
F32 = jnp.float32
BF16 = jnp.bfloat16
MIB = 1024 * 1024


def adamw_update(master, gradient, moment_one, moment_two, step_rate, weight_decay):
    first_new = BETA_ONE * moment_one + (1.0 - BETA_ONE) * gradient
    second_new = BETA_TWO * moment_two + (1.0 - BETA_TWO) * gradient * gradient
    first_hat = first_new / (1.0 - BETA_ONE**STEP)
    second_hat = second_new / (1.0 - BETA_TWO**STEP)
    master_new = master - step_rate * (
        first_hat / (jnp.sqrt(second_hat) + ADAM_EPS) + weight_decay * master
    )
    return (master_new, first_new, second_new)


def dot(a, b):
    return lax.dot_general(a, b, (((1,), (0,)), ((), ())), preferred_element_type=F32)


def dot_nt(a, b):
    return lax.dot_general(a, b, (((1,), (1,)), ((), ())), preferred_element_type=F32)


def dot_tn(a, b):
    return lax.dot_general(a, b, (((0,), (0,)), ((), ())), preferred_element_type=F32)


def sds(shape, dtype):
    return jax.ShapeDtypeStruct(shape, dtype)


def as_list(value):
    return list(value) if isinstance(value, list) else [value]


class Staging:
    def __init__(self, ins, in_sems, outs, out_sems):
        self.waits = [[pltpu.make_async_copy(s, t, in_sems.at[n]) for s, t, n in group] for group in ins]
        self.puts = [[pltpu.make_async_copy(s, t, out_sems.at[n]) for s, t, n in group] for group in outs]
        self.waited, self.started, self.begun = set(), set(), False

    def begin(self):
        if not self.begun:
            self.begun = True
            for group in self.waits:
                for copy in group:
                    copy.start()

    def need(self, *which):
        self.begin()
        for k in which:
            if k not in self.waited:
                self.waited.add(k)
                for copy in self.waits[k]:
                    copy.wait()

    def put(self, *which):
        for k in which:
            if k not in self.started:
                self.started.add(k)
                for copy in self.puts[k]:
                    copy.start()

    def finish(self):
        self.need(*range(len(self.waits)))
        self.put(*range(len(self.puts)))
        for group in self.puts:
            for copy in group:
                copy.wait()


def staged_call(body, smem, operands, outs, scratch, flops, far=(), far_outs=()):
    given = [[v if isinstance(v, tuple) else (v, None) for v in as_list(group)] for group in operands]
    operands = given
    picks = [pick for group in operands for _, pick in group]
    operands = [[v if pick is None else sds(v.shape[1:], v.dtype) for v, pick in group] for group in operands]
    outs = [as_list(v) for v in outs]
    flat_in = [v for group in given for v, _ in group]
    flat_out = [v for group in outs for v in group]

    def buffer(group):
        return pltpu.VMEM((sum(v.shape[0] for v in group), *group[0].shape[1:]), group[0].dtype)

    def kernel(*refs):
        refs = list(refs)
        take = lambda n: [refs.pop(0) for _ in range(n)]
        info, sources, raw, targets, raw_out = [
            take(len(part)) for part in (smem, flat_in, far, flat_out, far_outs)
        ]
        sources = [ref if pick is None else ref.at[pick] for ref, pick in zip(sources, picks)]
        in_refs, out_refs, extra = take(len(operands)), take(len(outs)), take(len(scratch))
        in_sems, out_sems = refs

        def pairs(groups, far, near, outward):
            result, n = [], 0
            for group, ref in zip(groups, near):
                row, entry = 0, []
                for v in group:
                    part = ref if len(group) == 1 else ref.at[pl.ds(row, v.shape[0])]
                    entry.append((part, far[n], n) if outward else (far[n], part, n))
                    row, n = row + v.shape[0], n + 1
                result.append(entry)
            return result

        staging = Staging(
            pairs(operands, sources, in_refs, False), in_sems, pairs(outs, targets, out_refs, True), out_sems
        )
        body(staging, *info, *raw, *raw_out, in_refs, out_refs, *extra)
        staging.finish()

    moved = sum(v.size * v.dtype.itemsize for v in (*flat_in, *far, *flat_out, *far_outs))
    return pl.pallas_call(
        kernel,
        out_shape=(*flat_out, *far_outs),
        in_specs=[pl.BlockSpec(memory_space=pltpu.SMEM) for _ in smem]
        + [pl.BlockSpec(memory_space=pl.ANY) for _ in (*flat_in, *far)],
        out_specs=tuple(pl.BlockSpec(memory_space=pl.ANY) for _ in (*flat_out, *far_outs)),
        scratch_shapes=[buffer(g) for g in operands]
        + [buffer(g) for g in outs]
        + list(scratch)
        + [pltpu.SemaphoreType.DMA((len(flat_in),)), pltpu.SemaphoreType.DMA((len(flat_out),))],
        compiler_params=pltpu.CompilerParams(vmem_limit_bytes=58 * MIB),
        cost_estimate=pl.CostEstimate(flops=flops, bytes_accessed=moved, transcendentals=0),
    )(*smem, *flat_in, *far)


def first_rows(rows):
    return rows // 32 * 16


def part_shapes(rows, lanes):
    low = first_rows(rows)
    pair = [sds((2, 4, low, lanes), BF16), sds((2, 4, rows - low, lanes), BF16)]
    return pair + pair + pair + pair


def part_copies(grads, refs, sems):
    rows = grads.shape[1]
    low = first_rows(rows)
    copies = []
    for core in range(2):
        for first in (1, 0):
            by_dp, by_band = refs[core * 4 + (1 - first) * 2], refs[core * 4 + (1 - first) * 2 + 1]
            for n in range(2):
                at = core * 16 + n * 8 + first * 4
                copies.append((grads.at[pl.ds(at, 4), pl.ds(0, low)], by_dp.at[n]))
                at = core * 16 + first * 8 + n * 4
                copies.append((grads.at[pl.ds(at, 4), pl.ds(low, rows - low)], by_band.at[n]))
    return [pltpu.make_async_copy(source, target, sems.at[n]) for n, (source, target) in enumerate(copies)]


def norm_parts(values):
    center = values - jnp.mean(values, axis=-1, keepdims=True)
    spread = jnp.mean(center * center, axis=-1, keepdims=True)
    inverse = lax.rsqrt(spread + NORM_EPS)
    return center * inverse, inverse


def norm_back(gy, gain, xh, inverse):
    e = gy * gain
    return inverse * (
        e - jnp.mean(e, axis=-1, keepdims=True) - xh * jnp.mean(e * xh, axis=-1, keepdims=True)
    )


def column_sum(values):
    return jnp.sum(values, axis=0, keepdims=True)


def image_values(ref, m):
    return jnp.concatenate([ref[IMGS * k + m] for k in range(4)], axis=0)


def set_image(ref, m, values):
    for k in range(4):
        ref[IMGS * k + m] = values[64 * k : 64 * k + 64]


def valid_slots(info, m):
    columns = []
    for k in range(4):
        slot = lax.broadcasted_iota(jnp.int32, (64, 1), 0) + info[FLIP + k] * 64
        inside = ((slot >> 4) < info[LIMIT + m]) & ((slot & 15) < info[LIMIT + m])
        columns.append(inside.astype(F32))
    return jnp.concatenate(columns, axis=0)


def blocks_of(info):
    return lambda b, i: info[b] * 8 + info[4 + i]


def blocks_first(info):
    return lambda b, i: info[b] * 8 + info[FIRST + i]


def blocks_second(info):
    return lambda b, i: info[SECOND + b] * 8 + info[SECOND + 4 + i]


def joined(weights, block, b):
    return jnp.concatenate([weights[block(b, i)] for i in range(8)], axis=0)


def head_cut(ref, j):
    lane = (j % 9) * HD
    base = lane // 128 * 128
    tile = ref[j // 9, :, 0, :, base : base + 128].reshape(SLOTS, 128)
    return tile[:, lane - base : lane - base + HD]


def pack_first_body(io, ins, outs):
    io.need(0, 1)
    qkv, table = ins[0][...], ins[1][...]
    table = jnp.concatenate([table, jnp.zeros((50, table.shape[1]), F32)], axis=0)
    outs[0][:, 0:512] = qkv[:, 0:512].astype(BF16)
    outs[0][:, 512:640] = jnp.concatenate([qkv[:, 512:576], jnp.transpose(table)], axis=1).astype(BF16)


def pack_second_body(io, ins, outs):
    io.need(0, 1, 2)
    up, turned, out = (ref[...].astype(BF16) for ref in ins)
    for group in range(GROUPS):
        at, row = 128 * group, 96 * group
        pieces = (up[:, at : at + 128], up[:, at + 384 : at + 512], turned[:96, at : at + 128], turned[96:, at : at + 128])
        for n, piece in enumerate(pieces):
            outs[0][row : row + 96, 128 * n : 128 * n + 128] = piece
    outs[0][288:336, :] = pack_out(out)


def project_body(io, info, ins, outs, n1):
    x, weights = ins
    qkv, table = outs
    block = blocks_first(info)
    io.need(0)
    for m in range(IMGS):
        n1[m], _ = norm_parts(image_values(x, m).astype(F32))
    io.need(1)
    tail = jnp.concatenate([weights[block(0, i), :, 512:640] for i in range(8)], axis=0)
    vec = jnp.transpose(tail.astype(F32))[64:80]
    table[...] = vec
    bias = jnp.concatenate(
        [vec[2:3], jnp.zeros((1, D), F32), vec[3:4], jnp.zeros((1, 64), F32)], axis=1
    )
    normed = [(n1[m] * vec[0:1] + vec[1:2]).astype(BF16) for m in range(IMGS)]
    for b in range(4):
        w = joined(weights, block, b)
        for m in range(IMGS):
            part = dot(normed[m], w) + bias[:, 576 * b : 576 * b + W1]
            qkv[b, :, m] = part.astype(BF16).reshape(4, 64, W1)


def attend_kernel(info, qkv, mixed, total):
    column = (valid_slots(info, pl.program_id(0)) - 1.0) * -MASK_FILL
    for pair in range(H // 2):
        halves = []
        for h in (2 * pair, 2 * pair + 1):
            q = head_cut(qkv, h) * BF16(HD**-0.5)
            k = head_cut(qkv, H + h)
            v = head_cut(qkv, 2 * H + h)
            scores = dot_nt(k, q) + column
            highest = jnp.max(scores, axis=0, keepdims=True)
            shifted = jnp.exp(scores - highest)
            totals = column_sum(shifted)
            low = (shifted * (1.0 / totals)).astype(BF16)
            total[0, h : h + 1, :] = highest + jnp.log(totals)
            halves.append(dot_tn(v, low))
        both = jnp.transpose(jnp.concatenate(halves, axis=0))
        mixed[:, 0, :, 128 * pair : 128 * pair + 128] = both.astype(BF16).reshape(4, 64, 128)


def gelu_parts(v):
    cdf = 0.5 * (1.0 + lax.erf(v * (0.5**0.5)))
    pdf = jnp.exp(v * v * -0.5) * ((2.0 * math.pi) ** -0.5)
    return v * cdf, cdf + v * pdf


def spread_group(weights, row, block, up, down):
    for b in range(4):
        for i in range(8):
            piece = weights[block(b, i), row : row + 96]
            up[96 * i : 96 * i + 96, 256 * b : 256 * b + 256] = piece[:, 0:256]
            for e in range(2):
                down[192 * b + 96 * e : 192 * b + 96 * e + 96, 128 * i : 128 * i + 128] = piece[
                    :, 256 + 128 * e : 384 + 128 * e
                ]


def feed_group(
    group, vec, n2, gb, up, down, act, gh, br2, gn2, bias_grad, lane, grads, row, block, before=None, after=None
):
    up_bias = jnp.concatenate(
        [
            vec[10 + i // 2 : 11 + i // 2, 384 * (i % 2) + 128 * group : 384 * (i % 2) + 128 * group + 128]
            for i in range(8)
        ],
        axis=1,
    )
    bias_sum = jnp.zeros((1, TILE), F32)
    for m in range(IMGS):
        rows = slice(m * SLOTS, m * SLOTS + SLOTS)
        active, slope = gelu_parts(dot(n2[rows], up[...]) + up_bias)
        act[rows] = active.astype(BF16)
        low = (dot(gb[rows], down[...]) * slope).astype(BF16)
        gh[rows] = low
        bias_sum += column_sum(low.astype(F32))
    bias_grad[:, lane : lane + TILE] = bias_sum
    if before:
        before()

    def add_sums(total, wide, weight):
        for m in range(IMGS):
            rows = slice(m * SLOTS, m * SLOTS + SLOTS)
            new = dot_nt(wide[rows], weight[...])
            total[rows] = new if group == 0 else total[rows] + new

    if not after:
        add_sums(br2, act, down)
        add_sums(gn2, gh, up)
    at = slice(row, row + 96)
    up_grad = dot_tn(n2[...], gh[...]).astype(BF16)
    for b in range(4):
        for i in range(8):
            grads[block(b, i), at, 0:256] = up_grad[96 * i : 96 * i + 96, 256 * b : 256 * b + 256]
    down_grad = dot_tn(gb[...], act[...]).astype(BF16)
    for b in range(4):
        for i in range(8):
            for e in range(2):
                grads[block(b, i), at, 256 + 128 * e : 384 + 128 * e] = down_grad[
                    192 * b + 96 * e : 192 * b + 96 * e + 96, 128 * i : 128 * i + 128
                ]
    if after:
        after[0]()
        add_sums(br2, act, down)
        after[1]()
        add_sums(gn2, gh, up)


def store_parts(grads, targets, sems):
    puts = part_copies(grads, targets, sems)
    for put in puts:
        put.start()
    return puts


def load_rows(sources, row, rows, target, sems):
    copies, at = [], 0
    for n, ref in enumerate(sources):
        size = ref.shape[0]
        copies.append(pltpu.make_async_copy(ref.at[:, pl.ds(row, rows)], target.at[pl.ds(at, size)], sems.at[n]))
        at += size
    for copy in copies:
        copy.start()
    return copies


def feed_first_body(io, info, second, ins, outs, groups, tails, up, down, act, gh, sems):
    x, mixed, table, cot = ins
    n2, gb, branch_ref, out, br2, gn2, bias_grad, grads = outs
    second_block = blocks_second(info)
    small = load_rows([second], 288, 48, tails, sems.at[0])
    io.begin()
    large = load_rows([second], 0, 192, groups, sems.at[1])
    for copy in small:
        copy.wait()
    for b in range(4):
        for i in range(8):
            wide = tails[second_block(b, i), 0:32, 0:384]
            thin = tails[second_block(b, i), :, 384:512]
            for g in range(3):
                out[96 * i + 32 * g : 96 * i + 32 * g + 32, 192 * b : 192 * b + 128] = wide[:, 128 * g : 128 * g + 128]
            for g in range(2):
                out[96 * i + 48 * g : 96 * i + 48 * g + 48, 192 * b + 128 : 192 * b + 192] = thin[:, 64 * g : 64 * g + 64]
    io.need(0, 1, 2, 3)
    vec = table[...]
    for m in range(IMGS):
        rows = slice(m * SLOTS, m * SLOTS + SLOTS)
        branch = dot(mixed[:, m].reshape(SLOTS, D), out[...]) + vec[4:5]
        branch_ref[rows] = branch
        xh, _ = norm_parts(image_values(x, m).astype(F32) + vec[5:6] * branch)
        n2[rows] = (xh * vec[6:7] + vec[7:8]).astype(BF16)
        back = image_values(cot, m).astype(F32) * valid_slots(info, m)
        gb[rows] = (back * vec[9:10]).astype(BF16)
    io.put(0, 1, 2, 3)
    for copy in large:
        copy.wait()
    for group in range(2):
        spread_group(groups, 96 * group, second_block, up, down)
        feed_group(
            group, table, n2, gb, up, down, act, gh, br2, gn2, bias_grad, TILE * group, grads, 96 * group,
            lambda b, i: b * 8 + i, None, (lambda: io.put(6, 7), lambda: io.put(4)) if group else None,
        )


def feed_last_body(io, info, second, *refs):
    *targets, ins, outs, groups, up, down, act, gh, grads, sems, put_sems = refs
    n2, gb, table, br2, gn2, x, cot, mixed, branch_ref, out = ins
    layer, middle_grad, mixed_grad, vec_grad, bias_grad = outs
    block, second_block = blocks_of(info), blocks_second(info)
    large = load_rows([second], 192, 96, groups, sems)
    io.begin()
    for copy in large:
        copy.wait()
    spread_group(groups, 0, second_block, up, down)
    io.need(0, 1, 2)
    feed_group(
        2, table, n2, gb, up, down, act, gh, br2, gn2, bias_grad, 0, grads, 0, block, lambda: io.need(3, 4)
    )
    io.need(5, 6, 7, 8, 9)
    vec = table[...]
    sums = [jnp.zeros((1, D), F32) for _ in range(10)]
    for m in range(IMGS):
        rows = slice(m * SLOTS, m * SLOTS + SLOTS)
        valid = valid_slots(info, m)
        back = image_values(cot, m).astype(F32) * valid
        branch = branch_ref[rows]
        middle = image_values(x, m).astype(F32) + vec[5:6] * branch
        xh, inverse = norm_parts(middle)
        branch_two = br2[rows] + vec[8:9]
        set_image(layer, m, ((middle + vec[9:10] * branch_two) * valid).astype(BF16))
        sums[9] += column_sum(back * branch_two)
        sums[8] += column_sum(gb[rows].astype(F32))
        gy = gn2[rows]
        sums[6] += column_sum(gy * xh)
        sums[7] += column_sum(gy)
        grad = norm_back(gy, vec[6:7], xh, inverse) + back
        middle_grad[rows] = grad
        sums[5] += column_sum(grad * branch)
        low = (grad * vec[5:6]).astype(BF16)
        sums[4] += column_sum(low.astype(F32))
        gh[rows, :D] = low
        mixed_grad[:, m] = dot_nt(low, out[...]).astype(BF16).reshape(4, 64, D)
        act[rows, :D] = mixed[:, m].reshape(SLOTS, D)
    for k in range(10):
        vec_grad[k : k + 1] = sums[k]
    vec_grad[10:16] = jnp.zeros((6, D), F32)
    io.put(0, 1, 2, 3, 4)
    out_grad = dot_tn(act[:, :D], gh[:, :D]).astype(BF16)
    for b in range(4):
        for i in range(8):
            piece = out_grad[96 * i : 96 * i + 96, 192 * b : 192 * b + 192]
            at = block(b, i)
            for g in range(3):
                grads[at, 96:128, 128 * g : 128 * g + 128] = piece[32 * g : 32 * g + 32, 0:128]
            grads[at, 128:144, 0:384] = jnp.zeros((16, 384), BF16)
            grads[at, 96:144, 384:512] = jnp.concatenate([piece[0:48, 128:192], piece[48:96, 128:192]], axis=1)
    for put in store_parts(grads, targets, put_sems):
        put.wait()


def attend_back_kernel(info, qkv, total, mixed_grad, gq):
    column = (valid_slots(info, pl.program_id(0)) - 1.0) * -MASK_FILL
    for b in range(4):
        gq[b, :, 0, :, 512:640] = jnp.zeros((4, 64, 128), BF16)
    for h in range(H):
        q = head_cut(qkv, h) * BF16(HD**-0.5)
        k = head_cut(qkv, H + h)
        v = head_cut(qkv, 2 * H + h)
        base = h // 2 * 128
        tile = mixed_grad[:, 0, :, base : base + 128].reshape(SLOTS, 128)
        grad_out = tile[:, h % 2 * HD : h % 2 * HD + HD]
        scores = dot_nt(k, q) + column
        again = jnp.exp(scores - total[0, h : h + 1, :])
        grad_weights = dot_nt(v, grad_out)
        center = column_sum(again * grad_weights)
        grad_scores = (again * (grad_weights - center)).astype(BF16)
        parts = (
            jnp.transpose(dot_tn(k, grad_scores)) * (HD**-0.5),
            dot(grad_scores, q),
            dot(again.astype(BF16), grad_out),
        )
        for j, part in zip((h, H + h, 2 * H + h), parts):
            lane = (j % 9) * HD
            gq[j // 9, :, 0, :, lane : lane + HD] = part.astype(BF16).reshape(4, 64, HD)


def project_back_body(io, info, *refs):
    *targets, ins, outs, n1, grads, put_sems = refs
    x, table, gq, weights, vec_in, bias_head, bias_rest, middle_grad = ins
    (token_grad,) = outs
    block = blocks_of(info)
    io.need(0, 1)
    vec = table[...]
    for m in range(IMGS):
        xh, _ = norm_parts(image_values(x, m).astype(F32))
        n1[m * SLOTS : m * SLOTS + SLOTS] = (xh * vec[0:1] + vec[1:2]).astype(BF16)
    io.need(2, 3)
    gy = [jnp.zeros((SLOTS, D), F32) for _ in range(IMGS)]
    for b in range(4):
        w = joined(weights, blocks_first(info), b)
        for m in range(IMGS):
            gy[m] += dot_nt(gq[b, :, m].reshape(SLOTS, W1), w)
    io.need(4, 5, 6, 7)
    bias = jnp.concatenate([bias_head[...], bias_rest[...]], axis=1)
    gain_sum, shift_sum = jnp.zeros((1, D), F32), jnp.zeros((1, D), F32)
    for m in range(IMGS):
        rows = slice(m * SLOTS, m * SLOTS + SLOTS)
        xh, inverse = norm_parts(image_values(x, m).astype(F32))
        gain_sum += column_sum(gy[m] * xh)
        shift_sum += column_sum(gy[m])
        grad = norm_back(gy[m], vec[0:1], xh, inverse) + middle_grad[rows]
        set_image(token_grad, m, grad.astype(BF16))
    io.put(0)
    col = []
    for b in range(4):
        total = jnp.zeros((1, W1), F32)
        for m in range(IMGS):
            total += column_sum(gq[b, :, m].reshape(SLOTS, W1).astype(F32))
        col.append(total[:, :576])
    flat = jnp.concatenate(col, axis=1)
    up_rows = [
        jnp.concatenate(
            [bias[:, TILE * s + 128 * i : TILE * s + 128 * i + 128] for i in (2 * k, 2 * k + 1) for s in range(GROUPS)],
            axis=1,
        )
        for k in range(4)
    ]
    rows = [jnp.zeros((64, D), F32), gain_sum, shift_sum, flat[:, :D], flat[:, 2 * D :], vec_in[4:10]]
    tail = jnp.transpose(jnp.concatenate(rows + up_rows + [jnp.zeros((50, D), F32)], axis=0))
    for b in range(4):
        grad_rows = jnp.concatenate([gq[b, :, m].reshape(SLOTS, W1) for m in range(IMGS)], axis=0)
        grad = dot_tn(n1[...], grad_rows)
        last = (grad[:, 512:640] + tail).astype(BF16)
        grad = grad.astype(BF16)
        for i in range(8):
            at = block(b, i)
            grads[at, :, 0:512] = grad[96 * i : 96 * i + 96, 0:512]
            grads[at, :, 512:640] = last[96 * i : 96 * i + 96]
    puts = part_copies(grads, targets, put_sems)
    for put in puts:
        put.start()
    for put in puts:
        put.wait()


def near_body(io, ins, outs):
    low = ins[0].shape[1]
    for s in range(2):
        terms = ins[4 * s : 4 * s + 4]
        io.need(*range(4 * s, 4 * s + 4))
        rows = slice(low, None) if s else slice(0, low)
        for z in range(4):
            outs[0][z, rows] = sum(term[z].astype(F32) for term in terms).astype(BF16)


def total_of(ref):
    return sum(ref[z].astype(F32) for z in range(ref.shape[0]))


def step_into(outs, refs, gradient, rate, decay):
    master, first, second = (ref[...] for ref in refs)
    for ref, value in zip(outs, adamw_update(master, gradient, first, second, rate, decay)):
        ref[...] = value


def final_body(io, info, ins, outs):
    total1, parts2, parts3, tokens = ins[0:4]
    io.need(3)
    for k in range(4):
        outs[0][pl.ds(info[FLIP + k] * IMGS, IMGS)] = tokens[IMGS * k : IMGS * k + IMGS].astype(F32)
    io.put(0)
    io.need(2, *range(13, 19))
    total = total_of(parts3)
    step_into(outs[1:4], ins[13:16], total[:, :576], D ** (-0.5), MATRIX_DECAY)
    vector_grad = jnp.transpose(total[:, 512:640])[64:78]
    step_into(outs[4:7], ins[16:19], vector_grad, VECTOR_RATE, 0.0)
    outs[7][...] = vector_grad[8:9]
    io.put(1, 2, 3, 4, 5, 6, 7)
    io.need(*range(19))
    up, turned, out = unpack_groups(total1[0].astype(F32), total_of(parts2))
    step_into(outs[8:11], ins[4:7], up, D ** (-0.5), MATRIX_DECAY)
    io.put(8, 9, 10)
    step_into(outs[11:14], ins[7:10], turned, FF ** (-0.5), MATRIX_DECAY)
    io.put(11, 12, 13)
    step_into(outs[14:17], ins[10:13], out, (D // 64) ** (-0.5), MATRIX_DECAY)


def place_body(io, info, ins, outs):
    io.need(0)
    for k in range(4):
        outs[0][pl.ds(info[FLIP + k] * IMGS, IMGS)] = ins[0][IMGS * k : IMGS * k + IMGS].astype(outs[0].dtype)


def swap_band(values, k):
    return lax.ppermute(values, "band", [(b, b ^ k) for b in range(lax.axis_size("band"))])


def swap_dp(values, k):
    return lax.ppermute(values, "dp", [(d, d ^ k) for d in range(lax.axis_size("dp"))])


def trade_columns(blocks):
    groups = [[2 * z + x for z in range(4)] for x in range(2)]
    return lax.all_to_all(blocks, "dp", split_axis=0, concat_axis=0, axis_index_groups=groups, tiled=True)


def gather_columns(shard):
    return trade_columns(jnp.broadcast_to(shard[None], (4, *shard.shape)))


def image_parts(values, mine):
    groups = values.reshape(4, IMGS, 64, D)
    return [lax.dynamic_index_in_dim(groups, mine ^ k, 0, keepdims=False) for k in range(4)]


def swap_images(parts):
    return [parts[0]] + [swap_band(parts[k], k) for k in (1, 2, 3)]


def pack_first(qkv, vectors):
    return jnp.concatenate([qkv, vectors, jnp.zeros((qkv.shape[0], W1 - 590), BF16)], axis=1)


def pack_group(up, turned, group):
    at = 128 * group
    pieces = (up[:, at : at + 128], up[:, at + 384 : at + 512], turned[:96, at : at + 128], turned[96:, at : at + 128])
    return jnp.concatenate(pieces, axis=1)


def pack_out(out):
    wide = jnp.concatenate([out[:32, :128], out[32:64, :128], out[64:, :128]], axis=1)
    thin = jnp.concatenate([out[:48, 128:], out[48:, 128:]], axis=1)
    return jnp.concatenate([jnp.concatenate([wide, jnp.zeros((16, 384), BF16)], axis=0), thin], axis=1)


def unpack_groups(head, rest):
    groups, last = [head[:96], head[96:], rest[:96]], rest[96:]
    up = jnp.concatenate([groups[s][:, 128 * e : 128 * e + 128] for e in range(2) for s in range(GROUPS)], axis=1)
    turned = jnp.concatenate(
        [
            jnp.concatenate([groups[s][:, 256 + 128 * e : 384 + 128 * e] for s in range(GROUPS)], axis=1)
            for e in range(2)
        ],
        axis=0,
    )
    wide = jnp.concatenate([last[:32, 128 * g : 128 * g + 128] for g in range(3)], axis=0)
    thin = jnp.concatenate([last[:, 384:448], last[:, 448:512]], axis=0)
    return up, turned, jnp.concatenate([wide, thin], axis=1)


def together(*values):
    return lax.optimization_barrier(values)


def gather_blocks_full(blocks):
    parts = [blocks, swap_band(blocks, 2)]
    return parts + [swap_band(part, 1) for part in parts]


def add(*terms):
    return sum(term.astype(F32) for term in terms).astype(BF16)


def start_swap(parts, *others):
    return together([swap_band(part, 1) for part in parts[4:6]], parts, *others)


def first_parts(parts, swapped):
    return [add(mine, other) for mine, other in zip(parts[0:2], swapped)]


def later_parts(parts, swapped, got):
    return [add(mine[1], other[1], new[1]) for mine, other, new in zip(parts[2:4], swapped, got)]


def near_sum(parts, swapped, got, got_last):
    terms = []
    for n in range(2):
        terms += [(parts[2 + n], 0), (swapped[n], 0), (got[n], 0), got_last[n]]
    low, high = parts[0].shape[2], parts[1].shape[2]
    return staged_call(near_body, [], terms, [sds((4, low + high, parts[0].shape[3]), BF16)], [], 1_000_000)[0]


def reduce_blocks_full(parts):
    swapped = [swap_band(part, 1) for part in parts[4:]]
    first = first_parts(parts, swapped[:2])
    kept = [add(mine, other) for mine, other in zip(parts[2:4], swapped[2:])]
    by_dp = jnp.concatenate([kept[0][:, None], first[0][:, None]], axis=1)
    by_band = jnp.concatenate([kept[1][None], first[1][None]], axis=0)
    full = jnp.concatenate([by_dp, by_band], axis=3)
    got = swap_band(full[1], 2)
    return add(full[0], got).reshape(8, *full.shape[3:])


def image_call(body, info, operands, outs, flops):
    def spec(shape):
        place = next(k for k, size in enumerate(shape) if size == IMGS)
        block = tuple(1 if k == place else size for k, size in enumerate(shape))
        return pl.BlockSpec(block, lambda m: tuple(m if k == place else 0 for k in range(len(shape))))

    moved = sum(v.size * v.dtype.itemsize for v in (*operands, *outs))
    return pl.pallas_call(
        body,
        grid=(IMGS,),
        out_shape=outs,
        in_specs=[pl.BlockSpec(memory_space=pltpu.SMEM)] + [spec(v.shape) for v in operands],
        out_specs=tuple(spec(v.shape) for v in outs),
        compiler_params=pltpu.CompilerParams(vmem_limit_bytes=58 * MIB),
        cost_estimate=pl.CostEstimate(flops=flops, bytes_accessed=moved, transcendentals=0),
    )(info, *operands)


def on_device(
    tokens, cotangent, image_rows, qkv_weight, out_weight, up_weight, down_weight, vectors,
    qkv_first, out_first, up_first, down_first, vector_first,
    qkv_second, out_second, up_second, down_second, vector_second,
):
    dp_mine = lax.axis_index("dp")
    mine = lax.axis_index("band")
    direct = lax.axis_size("dp") == 8
    numbers = lambda n: jnp.arange(n, dtype=jnp.int32)
    flip = numbers(4) ^ mine
    if direct:
        turn = numbers(8) ^ dp_mine
        place = turn % 2 * 4 + numbers(8) // 2
        first_place = turn % 2 * 4 + turn // 2
    else:
        place = first_place = numbers(8)
    limits = lax.dynamic_slice_in_dim(image_rows, mine * IMGS, IMGS)
    info = jnp.concatenate([flip % 2 * 2 + flip // 2, place, flip, limits, numbers(4), numbers(8), first_place]).astype(jnp.int32)
    if direct:
        (pack2,) = staged_call(
            pack_second_body, [], [up_weight, down_weight.T, out_weight], [sds((336, 512), BF16)], [], 1_000_000
        )
        pack2, qkv_first_use = together(pack2, qkv_weight)
        (pack1,) = staged_call(
            pack_first_body, [], [qkv_first_use, vectors.T], [sds((96, W1), BF16)], [], 1_000_000
        )
        near1 = [pack1] + [swap_dp(pack1, 2 * k) for k in (1, 2, 3)]
        x = image_parts(tokens, mine)
        x[2:4] = [swap_band(x[2], 2), swap_band(x[3], 3)]
        second = [lax.all_gather(pack2, ("band", "dp"), axis=0)]
        cot = image_parts(cotangent, mine)
        near1, cot, x = together(near1, cot, x)
        near1 = jnp.stack(near1)
        x[1] = swap_band(x[1], 1)
        across1, beside1, x = together(swap_dp(near1, 1), swap_band(near1, 2), x)
        corner1 = [swap_band(across1[:2], 2), swap_dp(beside1[2:], 1)]
        near1c, across1c, beside1c = [swap_band(part, 1) for part in (near1, across1, beside1)]
        corner1, near1c, across1c, beside1c = together(corner1, near1c, across1c, beside1c)
        corner1c, cot = together([swap_band(part, 1) for part in corner1], cot)
        first = [near1, across1, beside1, *corner1, near1c, across1c, beside1c, *corner1c]
        cot = swap_images(cot)
    else:
        low = [w.astype(BF16) for w in (qkv_weight, out_weight, up_weight, down_weight, vectors)]
        x = swap_images(image_parts(tokens, mine))
        cot = swap_images(image_parts(cotangent, mine))
        qkv_all, out_all, up_all, down_all, vec_all = [
            lax.all_gather(w, "dp", axis=0, tiled=True) for w in low
        ]
        cut = lambda v, n: [v[n * i : n * i + n] for i in range(8)]
        first = jnp.stack([pack_first(q, v) for q, v in zip(cut(qkv_all, 96), cut(vec_all, 96))])
        groups = [
            jnp.stack([pack_group(u, d.T, s) for u, d in zip(cut(up_all, 96), cut(down_all, 384))])
            for s in range(GROUPS)
        ]
        outs = jnp.stack([pack_out(o) for o in cut(out_all, 96)])
        first = gather_blocks_full(first)
        second = [lax.all_gather(jnp.concatenate([*groups, outs], axis=1), "band", axis=0, tiled=True)]

    rows_shape = (4, IMGS, 64, D)
    vmem = pltpu.VMEM
    piece = [sds((IMGS, 64, D), BF16)] * 4
    wide, wide32 = sds((R, D), BF16), sds((R, D), F32)
    table = sds((16, D), F32)
    qkv_shape = sds((4, 4, IMGS, 64, W1), BF16)
    qkv, vec = staged_call(
        project_body, [info], [x, first], [qkv_shape, table], [vmem((IMGS, SLOTS, D), F32)], 2_800_000_000
    )
    mixed, totals = image_call(
        attend_kernel, info, (qkv,), (sds(rows_shape, BF16), sds((IMGS, H, SLOTS), F32)), 3_000_000_000
    )
    group_scratch = [vmem((R, TILE), BF16) for _ in range(4)] + [vmem((32, 144, 512), BF16)]
    n2, gb, branch, out, br2, gn2, bias_head, grads1 = staged_call(
        feed_first_body, [info], [x, mixed, vec, cot],
        [wide, wide, wide32, wide, wide32, wide32, sds((1, 2 * TILE), F32), sds((32, 192, 512), BF16)],
        [vmem((32, 192, 512), BF16), vmem((32, 48, 512), BF16)]
        + group_scratch[:4] + [pltpu.SemaphoreType.DMA((2, 1))],
        17_000_000_000, second,
    )
    total1 = lax.psum_scatter(grads1, ("band", "dp") if direct else "band", scatter_dimension=0, tiled=True)
    fed = staged_call(
        feed_last_body, [info], [n2, gb, vec, br2, gn2, x, cot, mixed, branch, out],
        [piece, wide32, sds(rows_shape, BF16), table, sds((1, TILE), F32)],
        [vmem((32, 96, 512), BF16)]
        + group_scratch + [pltpu.SemaphoreType.DMA((1,)), pltpu.SemaphoreType.DMA((16,))],
        10_000_000_000, second, part_shapes(144, 512),
    )
    layer, grads2 = list(fed[:4]), list(fed[8:])
    middle_grad, mixed_grad, vec_grad, bias_rest = fed[4:8]
    home = lambda parts: [parts[0]] + [swap_band(parts[k], k) for k in (1, 2, 3)]
    if direct:
        others2, grads2, mixed_grad, layer = start_swap(grads2, mixed_grad, layer)
        sides2, mixed_grad = together(first_parts(grads2, others2), mixed_grad)
        got2 = [swap_dp(sides2[0], 1), swap_band(sides2[1], 2)]
        rest2 = [swap_band(part, 1) for part in grads2[6:]]
        layer[1:3] = [swap_band(layer[1], 1), swap_band(layer[2], 2)]
    (gq,) = image_call(attend_back_kernel, info, (qkv, totals, mixed_grad), (qkv_shape,), 6_000_000_000)
    if direct:
        gq, got2, rest2, layer = together(gq, got2, rest2, layer)
        last2, gq = together(later_parts(grads2, rest2, got2), gq)
        got_last2 = [swap_band(last2[0], 2), swap_dp(last2[1], 1)]
        layer[3] = swap_band(layer[3], 3)
    t0, t1, t2, t3, *grads3 = staged_call(
        project_back_body, [info], [x, vec, gq, first, vec_grad, bias_head, bias_rest, middle_grad],
        [piece], [vmem((R, D), BF16), vmem((32, 96, W1), BF16), pltpu.SemaphoreType.DMA((16,))], 5_600_000_000,
        [], part_shapes(96, W1),
    )
    token_grad = [t0, t1, t2, t3]
    place_call = lambda parts, dtype: staged_call(place_body, [info], [parts], [sds(tokens.shape, dtype)], [], 1_000_000)[0]
    states = [
        (up_weight, up_first, up_second), (down_weight.T, down_first.T, down_second.T),
        (out_weight, out_first, out_second), (qkv_weight, qkv_first, qkv_second),
        (vectors.T, vector_first.T, vector_second.T),
    ]
    like = lambda state: [sds(v.shape, F32) for v in state]
    if direct:
        got_last2, layer, grads3, token_grad = together(got_last2, layer, grads3, token_grad)
        others3, token_grad = together([swap_band(part, 1) for part in grads3[4:6]], token_grad)
        sides3 = first_parts(grads3, others3)
        got3 = [swap_dp(sides3[0], 1), swap_band(sides3[1], 2)]
        rest3 = [swap_band(part, 1) for part in grads3[6:]]
        near2 = near_sum(grads2, rest2, got2, got_last2)
        parts2 = trade_columns(near2)
        layer_out = place_call(layer, BF16)
        got3, rest3, near2, token_grad, layer_out = together(got3, rest3, near2, token_grad, layer_out)
        last3, token_grad = together(later_parts(grads3, rest3, got3), token_grad)
        got_last3 = [swap_band(last3[0], 2), swap_dp(last3[1], 1)]
        got_last3, token_grad = together(got_last3, token_grad)
        token_grad = home(token_grad)
        near3 = near_sum(grads3, rest3, got3, got_last3)
        near3, parts2 = together(near3, parts2)
        parts3 = trade_columns(near3)
        token_out, *news = staged_call(
            final_body, [info], [total1, parts2, parts3, token_grad] + [v for s in states for v in s],
            [sds(tokens.shape, F32)] + [v for s in states[3:] for v in like(s)] + [sds((1, 96), F32)]
            + [v for s in states[:3] for v in like(s)], [], 20_000_000,
        )
        down_bias_gradient = news[6].reshape(-1)
        news = [news[7:10], [v.T for v in news[10:13]], news[13:16], news[0:3], [v.T for v in news[3:6]]]
    else:
        grads = [total1] + [reduce_blocks_full(part) for part in (grads2, grads3)]
        parts = [unpack_groups(grads[0][i], grads[1][i]) for i in range(8)]
        parts = [(up, turned.T, out) for up, turned, out in parts]
        full = [jnp.concatenate(p) for p in zip(*parts)] + [grads[2].reshape(D, W1)[:, :576], grads[2].reshape(D, W1)[:, 576:590]]
        full = [lax.psum_scatter(g.astype(F32), "dp", scatter_dimension=0, tiled=True) for g in full]
        states[1] = (down_weight, down_first, down_second)
        states[4] = (vectors, vector_first, vector_second)
        rates = (D ** (-0.5), FF ** (-0.5), (D // 64) ** (-0.5), D ** (-0.5), VECTOR_RATE)
        decays = (MATRIX_DECAY,) * 4 + (0.0,)
        news = [
            adamw_update(master, grad, one, two, rate, decay)
            for (master, one, two), grad, rate, decay in zip(states, full, rates, decays)
        ]
        down_bias_gradient = full[4][:, 8]
        layer_out, token_out = place_call(home(layer), BF16), place_call(home(token_grad), F32)
    order = [news[3], news[2], news[0], news[1], news[4]]
    return (
        (layer_out, token_out)
        + tuple(n[0] for n in order)
        + tuple(n[1] for n in order)
        + tuple(n[2] for n in order)
        + (down_bias_gradient,)
    )


def solution(mesh):
    rows, matrix, table = P("dp", "band", None), P("dp", "band"), P("dp", None)
    state = (matrix, matrix, matrix, matrix, table)
    return jax.shard_map(
        on_device,
        mesh=mesh,
        in_specs=(rows, rows, P("dp")) + state + state + state,
        out_specs=(rows, rows) + state + state + state + (P("dp"),),
        check_vma=False,
    )
```
